32 devices in a mesh: bucket: 4 (over z), seq: 8 (over y, x, core).
Axes of the slice: x: 2, y: 2, z: 4, core: 2. Of those that a mesh axis runs over, the one named last changes fastest.
Arguments:
- tokens: bfloat16 [4, 2112, 2048], P('bucket', 'seq'), may hold values from -6 to 6
- lengths: int32 [4, 4], P('bucket'), may hold values from 1 to 2108, as said below
- norm_gain: bfloat16 [2048], P(('bucket', 'seq')), may hold values from 0.099609375 to 1.8984375
- in_proj: bfloat16 [2048, 5120], P(('bucket', 'seq')), may hold values from -0.125 to 0.125
- conv_weight: bfloat16 [2560, 4], P(('bucket', 'seq')), may hold values from -3 to 3
- conv_bias: bfloat16 [2560], P(('bucket', 'seq')), may hold values from -3 to 3
- gate_weight: bfloat16 [2560, 320], P(('bucket', 'seq')), may hold values from -0.5 to 0.5
- gate_bias: bfloat16 [2560, 2], P(('bucket', 'seq')), may hold values from -4 to 4
- decay: bfloat16 [2560], P(('bucket', 'seq')), as said below
- out_proj: bfloat16 [2560, 2048], P(('bucket', 'seq')), may hold values from -0.3125 to 0.3125
- mlp_gain: bfloat16 [2048], P(('bucket', 'seq')), may hold values from 0.099609375 to 1.8984375
- gate_up: bfloat16 [2048, 12288], P(('bucket', 'seq')), may hold values from -0.125 to 0.125
- down_proj: bfloat16 [6144, 2048], P(('bucket', 'seq')), may hold values from -0.15625 to 0.15625
- cotangent: bfloat16 [4, 2112, 2048], P('bucket', 'seq'), may hold values from -6 to 6
Outputs:
- mixed: bfloat16 [4, 2112, 2048], P('bucket', 'seq')
- token_grad: float32 [4, 2112, 2048], P('bucket', 'seq')
- norm_gain_grad: float32 [2048], P(('bucket', 'seq'))
- in_proj_grad: float32 [2048, 5120], P(('bucket', 'seq'))
- conv_weight_grad: float32 [2560, 4], P(('bucket', 'seq'))
- conv_bias_grad: float32 [2560], P(('bucket', 'seq'))
- gate_weight_grad: float32 [2560, 320], P(('bucket', 'seq'))
- gate_bias_grad: float32 [2560, 2], P(('bucket', 'seq'))
- decay_grad: float32 [2560], P(('bucket', 'seq'))
- out_proj_grad: float32 [2560, 2048], P(('bucket', 'seq'))
- mlp_gain_grad: float32 [2048], P(('bucket', 'seq'))
- gate_up_grad: float32 [2048, 12288], P(('bucket', 'seq'))
- down_proj_grad: float32 [6144, 2048], P(('bucket', 'seq'))
The draws below stay inside these ranges and needn't reach their ends.
Inputs may be any that keep to these rules, and one draw needn't show every extreme that they name: Each bucket's 4 lengths are packed in order and sum to less than 2112; the rest of the bucket is padding. In every bucket one sequence, never the bucket's last, starts within the first 264 tokens and ends within the last 264 tokens. softplus(decay) lies between 0.09 / 2112 and 0.041.
All inputs are finite; a program needn't handle non-finite values.
Results may differ from the reference program's by a relative error of at most 0.0088.
Values may be sent and summed in bfloat16 or wider, within the bound.
No kernel may reach another device: no remote copies, remote signals or barrier semaphores. Data moves between devices by JAX's collectives and lax.ppermute only.
A program may use at most 512 MiB of HBM per device.

```python
import jax
import jax.numpy as jnp
from jax import lax

D = 2048
W = 2560
NB = 16
BW = 160
FF = 6144
CONV = 4
SLOTS = 4
TOK_DEV = 264
BUCKETS = 4
BUCKET = 2112


def draw_lengths(key, part):
    key = jax.random.fold_in(key, 11)
    key_long, key_short, key_pad, key_pick, key_edge = jax.random.split(key, 5)
    long_slot = jax.random.randint(key_long, (BUCKETS, 1), 0, SLOTS - 1)
    shorts = jax.random.randint(key_short, (BUCKETS, SLOTS), 1, TOK_DEV // 8 + 1)
    padding = jax.random.randint(key_pad, (BUCKETS, 1), 1, TOK_DEV // 4 + 1)
    picked = jax.random.randint(key_pick, (), 0, BUCKETS)
    edge = jax.random.randint(key_edge, (BUCKETS, 1), 1, 3)
    slot_ids = jnp.arange(SLOTS, dtype=jnp.int32)[None, :]
    bucket_ids = jnp.arange(BUCKETS, dtype=jnp.int32)[:, None]
    is_long = slot_ids == long_slot
    before = jnp.sum(jnp.where(slot_ids < long_slot, shorts, 0), axis=1, keepdims=True)
    after = jnp.sum(jnp.where(slot_ids > long_slot, shorts, 0), axis=1, keepdims=True)
    tail = jnp.where(bucket_ids == picked, edge, TOK_DEV - padding - after)
    long_length = BUCKET - TOK_DEV + tail - before
    return jnp.where(is_long, long_length, shorts).astype(jnp.int32)


def draw_decay(key, part):
    key = jax.random.fold_in(key, 13)
    key_pick, key_rate = jax.random.split(key, 2)
    slow_share = 0.5
    slow = jax.random.bernoulli(key_pick, slow_share, (W,))
    spread = jax.random.uniform(key_rate, (W,), jnp.float32)
    slow_rate = 0.1 / BUCKET * 5.0 ** spread
    fast_rate = 0.5 / BUCKET * (0.04 * BUCKET / 0.5) ** spread
    rate = jnp.where(slow, slow_rate, fast_rate)
    return jnp.log(jnp.expm1(rate)).astype(jnp.bfloat16)


def block_scale(own_key, extent, cuts, least, high):
    def one(dim, parts):
        draws = jax.random.uniform(jax.random.fold_in(jax.random.fold_in(own_key, 6), dim), (parts,), jnp.float32, least / len(cuts), high / len(cuts))
        return jnp.repeat(jnp.exp(draws), extent[dim] // parts).reshape((-1,) + (1,) * (len(extent) - dim - 1))

    level = one(*cuts[0])
    for cut in cuts[1:]:
        level = level * one(*cut)
    return level


def scatter_about(own_key, dims, deviation, most, cuts=(), kind=jnp.bfloat16):
    loudness = block_scale(own_key, dims, cuts, -0.22, 0.18) if cuts else 1.0
    values = jax.random.normal(own_key, dims, jnp.float32) * deviation * loudness
    return jnp.minimum(jnp.maximum(values, -most), most).astype(kind)


def setup_inputs(seed: int = 0) -> dict:
    key_list = jax.random.split(jax.random.key(seed), 15)
    return {
        "tokens": scatter_about(key_list[0], (BUCKETS, BUCKET, D), 1.0, 6.0, ((0, 4), (1, 8))),
        "lengths": draw_lengths(jax.random.fold_in(key_list[14], 71), 0),
        "norm_gain": jnp.clip(1.0 + 0.18 * jax.random.normal(key_list[2], (D,), jnp.float32), 0.099609375, 1.8984375).astype(jnp.bfloat16),
        "in_proj": scatter_about(key_list[3], (D, 2 * W), D ** -0.5, 0.125, ((0, 32),)),
        "conv_weight": scatter_about(key_list[4], (W, CONV), CONV ** -0.5, 3.0, ((0, 32),)),
        "conv_bias": scatter_about(key_list[5], (W,), 0.5, 3.0, ((0, 32),)),
        "gate_weight": scatter_about(key_list[6], (W, 2 * BW), BW ** -0.5, 0.5, ((0, 32),)),
        "gate_bias": scatter_about(key_list[7], (W, 2), 1.0, 4.0, ((0, 32),)),
        "decay": draw_decay(jax.random.fold_in(key_list[14], 71), 0),
        "out_proj": scatter_about(key_list[9], (W, D), (W // 8) ** -0.5, 0.3125, ((0, 32),)),
        "mlp_gain": jnp.clip(1.0 + 0.18 * jax.random.normal(key_list[10], (D,), jnp.float32), 0.099609375, 1.8984375).astype(jnp.bfloat16),
        "gate_up": scatter_about(key_list[11], (D, 2 * FF), D ** -0.5, 0.125, ((0, 32),)),
        "down_proj": scatter_about(key_list[12], (FF, D), (FF // 4) ** -0.5, 0.15625, ((0, 32),)),
        "cotangent": scatter_about(key_list[13], (BUCKETS, BUCKET, D), 1.0, 6.0, ((0, 4), (1, 8))),
    }


norm_eps = 1e-06
gate_scale = 8.0

@jax.custom_vjp
def low(v):
    return lax.optimization_barrier(v.astype(jnp.bfloat16)).astype(jnp.float32)

@jax.custom_vjp
def low_back(v):
    return v

def low_keep(v):
    return (low(v), None)

def low_pass(kept, grad):
    return (grad,)

def back_keep(v):
    return (v, None)

def back_low(kept, grad):
    return (low(grad),)
low.defvjp(low_keep, low_pass)
low_back.defvjp(back_keep, back_low)

def matmul(left, right):
    return jnp.dot(left, right, precision=lax.Precision.HIGHEST, preferred_element_type=jnp.float32)

def rms_scale(values, gain):
    return values * lax.rsqrt(lax.optimization_barrier(jnp.mean(values * values, axis=1, keepdims=True)) + norm_eps) * gain

def link(earlier, later):
    return (earlier[0] * later[0], later[0] * earlier[1] + later[1])

def segment_layout(lengths_row, positions):
    ends = jnp.cumsum(lengths_row).astype(jnp.int32)
    segment_ids = lax.optimization_barrier(jnp.sum((positions[:, None] >= ends[None, :]).astype(jnp.int32), axis=1))
    segment_ids = jnp.where(positions < 0, -1, segment_ids).astype(jnp.int32)
    keep = (positions < ends[-1]).astype(jnp.float32)
    return (segment_ids, keep)

def lru_terms(conv_out, gate_a, gate_i, decay, starts):
    rate = jax.nn.softplus(decay)
    log_step = -gate_scale * jax.nn.sigmoid(gate_a) * rate
    decay_step = jnp.where(starts, 0.0, jnp.exp(log_step))
    scaling = jnp.where(starts, 1.0, jnp.sqrt(-jnp.expm1(2.0 * log_step)))
    return (decay_step, conv_out * jax.nn.sigmoid(gate_i) * scaling)

def bucket_layer(inputs, lengths_row, weights):
    norm_gain, in_proj, conv_weight, conv_bias, gate_weight, gate_bias, decay, out_proj, mlp_gain, gate_up, down_proj = weights
    total = inputs.shape[0]
    width = conv_bias.shape[0]
    block_width = width // NB
    ff_width = down_proj.shape[0]
    positions = jnp.arange(total, dtype=jnp.int32)
    segment_ids, keep = segment_layout(lengths_row, positions)
    back_ids = segment_layout(lengths_row, positions - 1)[0]
    starts = (segment_ids != back_ids)[:, None]
    normed = low(rms_scale(inputs, norm_gain))
    projected = low_back(matmul(normed, in_proj))
    mixer_in = low(projected[:, :width])
    branch = projected[:, width:]
    convolved = conv_bias + mixer_in * conv_weight[:, 0]
    for offset in range(1, conv_weight.shape[1]):
        moved = jnp.concatenate([jnp.zeros((offset, width), jnp.float32), mixer_in[:total - offset]], axis=0)
        moved_ids = segment_layout(lengths_row, positions - offset)[0]
        same = (moved_ids == segment_ids)[:, None]
        convolved = convolved + jnp.where(same, moved, 0.0) * conv_weight[:, offset]
    conv_out = low(low_back(convolved))
    gates = jnp.einsum('tnc,ncd->tnd', conv_out.reshape(total, NB, block_width), gate_weight.reshape(NB, block_width, 2 * block_width), precision=lax.Precision.HIGHEST)
    gate_a = low_back(gates[:, :, :block_width].reshape(total, width) + gate_bias[:, 0])
    gate_i = low_back(gates[:, :, block_width:].reshape(total, width) + gate_bias[:, 1])
    decay_step, normalized = lru_terms(conv_out, gate_a, gate_i, decay, starts)
    hidden = lax.associative_scan(link, (decay_step, normalized), axis=0)[1]
    gated = low(hidden * jax.nn.gelu(branch))
    residual = inputs + low_back(matmul(gated, out_proj))
    normed_two = low(rms_scale(residual, mlp_gain))
    expanded = low_back(matmul(normed_two, gate_up))
    feed = low(jax.nn.gelu(expanded[:, :ff_width]) * expanded[:, ff_width:])
    return keep[:, None] * (residual + low_back(matmul(feed, down_proj)))

def reference(tokens, lengths, norm_gain, in_proj, conv_weight, conv_bias, gate_weight, gate_bias, decay, out_proj, mlp_gain, gate_up, down_proj, cotangent):
    weights = tuple((param.astype(jnp.float32) for param in (norm_gain, in_proj, conv_weight, conv_bias, gate_weight, gate_bias, decay, out_proj, mlp_gain, gate_up, down_proj)))
    inputs = tokens.astype(jnp.float32)

    def forward(values, params):

        def single(pair):
            return bucket_layer(pair[0], pair[1], params)
        return lax.map(jax.checkpoint(single), (values, lengths))
    mixed, pullback = jax.vjp(forward, inputs, weights)
    token_grad, grads = pullback(cotangent.astype(jnp.float32))
    return (mixed.astype(jnp.bfloat16), token_grad, grads[0], grads[1], grads[2], grads[3], grads[4], grads[5], grads[6], grads[7], grads[8], grads[9], grads[10])
```

```python
from functools import partial

import jax
import jax.numpy as jnp
from jax import lax
from jax.experimental import pallas as pl
from jax.experimental.pallas import tpu as pltpu
from jax.sharding import PartitionSpec as P

NB = 16


norm_eps = 1e-06
gate_scale = 8.0


def from_behind(block, axis, distance):
    devices = range(lax.axis_size(axis))
    route = [(i - distance, i) for i in devices if i - distance in devices]
    return lax.ppermute(block, axis, route)


def entering(part, axis, combine, identity, reverse):
    count = lax.axis_size(axis)
    place = lax.axis_index(axis)
    ahead = count - 1 - place if reverse else place
    gathered = jax.tree.map(lambda a: lax.all_gather(a, axis), part)
    state = jax.tree.map(lambda a, e: jnp.zeros_like(a) + jnp.asarray(e, a.dtype), part, identity)

    def one(lap, state):
        source = count - 1 - lap if reverse else lap
        return combine(
            state, jax.tree.map(lambda a: lax.dynamic_index_in_dim(a, source, 0, False), gathered)
        )

    return lax.fori_loop(0, ahead, one, state)


def rms_scale(values, gain):
    return values * lax.rsqrt(jnp.mean(values * values, axis=1, keepdims=True) + norm_eps) * gain


def link(earlier, later):
    return (earlier[0] * later[0], later[0] * earlier[1] + later[1])


def segment_layout(lengths_row, positions):
    ends = jnp.cumsum(lengths_row)
    segment_ids = jnp.sum((positions[:, None] >= ends[None, :]).astype(jnp.int32), axis=1)
    segment_ids = jnp.where(positions < 0, -1, segment_ids)
    keep = (positions < ends[-1]).astype(jnp.float32)
    return (segment_ids, keep)


def lru_terms(conv_out, gate_a, gate_i, decay, starts):
    rate = jax.nn.softplus(decay)
    log_step = -gate_scale * jax.nn.sigmoid(gate_a) * rate
    decay_step = jnp.where(starts, 0.0, jnp.exp(log_step))
    scaling = jnp.where(starts, 1.0, jnp.sqrt(-jnp.expm1(2.0 * log_step)))
    return (decay_step, conv_out * jax.nn.sigmoid(gate_i) * scaling)


def gated_gelu(values, split):
    return jax.nn.gelu(values[:, :split]) * values[:, split:]


def contract_last(left, right):
    return lax.dot_general(
        left, right, (((1,), (1,)), ((), ())), preferred_element_type=jnp.float32
    )


def contract_first(left, right):
    return lax.dot_general(
        left, right, (((0,), (0,)), ((), ())), preferred_element_type=jnp.float32
    )


def row_product(left, right):
    return contract_first(left, right)


def on_device(
    tokens,
    lengths,
    norm_gain,
    in_proj,
    conv_weight,
    conv_bias,
    gate_weight,
    gate_bias,
    decay,
    out_proj,
    mlp_gain,
    gate_up,
    down_proj,
    cotangent,
):
    inputs = tokens[0].astype(jnp.float32)
    tok_rows = inputs.shape[0]
    width = in_proj.shape[1] // 2
    ff_width = gate_up.shape[1] // 2
    block_width = width // NB
    kernel = conv_weight.shape[1]
    rim_rows = kernel - 1
    (
        gain_one_all,
        proj_all,
        conv_all,
        conv_bias_all,
        gate_all,
        gate_bias_all,
        decay_all,
        out_all,
        gain_two_all,
    ) = (
        lax.all_gather(norm_gain, ("bucket", "seq"), axis=0, tiled=True),
        lax.all_gather(in_proj, ("bucket", "seq"), axis=0, tiled=True),
        lax.all_gather(conv_weight, ("bucket", "seq"), axis=0, tiled=True),
        lax.all_gather(conv_bias, ("bucket", "seq"), axis=0, tiled=True),
        lax.all_gather(gate_weight, ("bucket", "seq"), axis=0, tiled=True),
        lax.all_gather(gate_bias, ("bucket", "seq"), axis=0, tiled=True),
        lax.all_gather(decay, ("bucket", "seq"), axis=0, tiled=True),
        lax.all_gather(out_proj, ("bucket", "seq"), axis=0, tiled=True),
        lax.all_gather(mlp_gain, ("bucket", "seq"), axis=0, tiled=True),
    )
    seq_index = lax.axis_index("seq")
    positions = seq_index * tok_rows + jnp.arange(tok_rows, dtype=jnp.int32)
    lengths_row = lengths[0]
    segment_ids, keep = segment_layout(lengths_row, positions)
    back_ids = segment_layout(lengths_row, positions - 1)[0]
    starts = (segment_ids != back_ids)[:, None]
    normed, norm_pull = jax.vjp(rms_scale, inputs, gain_one_all.astype(jnp.float32))
    normed_low = normed.astype(jnp.bfloat16)
    projected = jnp.dot(normed_low, proj_all, preferred_element_type=jnp.float32)
    mixer_in = projected[:, :width].astype(jnp.bfloat16)
    branch = projected[:, width:]
    rim = from_behind(mixer_in[tok_rows - rim_rows :], "seq", 1)
    extended = jnp.concatenate([rim, mixer_in], axis=0)
    conv_float = conv_all.astype(jnp.float32)
    lagged_terms = []
    convolved = jnp.zeros((tok_rows, width), jnp.float32) + conv_bias_all.astype(jnp.float32)
    for offset in range(kernel):
        earlier_ids = segment_layout(lengths_row, positions - offset)[0]
        lagged = jnp.where(
            (earlier_ids == segment_ids)[:, None],
            extended[rim_rows - offset : rim_rows - offset + tok_rows].astype(jnp.float32),
            0.0,
        )
        lagged_terms.append(lagged)
        convolved = convolved + lagged * conv_float[:, offset]
    conv_out = convolved.astype(jnp.bfloat16)
    gates = jnp.einsum(
        "tnc,ncd->tnd",
        conv_out.reshape(tok_rows, NB, block_width),
        gate_all.reshape(NB, block_width, 2 * block_width),
        preferred_element_type=jnp.float32,
    )
    gate_bias_float = gate_bias_all.astype(jnp.float32)
    gate_a = gates[:, :, :block_width].reshape(tok_rows, width) + gate_bias_float[:, 0]
    gate_i = gates[:, :, block_width:].reshape(tok_rows, width) + gate_bias_float[:, 1]
    (decay_step, normalized), lru_pull = jax.vjp(
        partial(lru_terms, starts=starts),
        conv_out.astype(jnp.float32),
        gate_a,
        gate_i,
        decay_all.astype(jnp.float32),
    )
    prefix_decay, prefix_state = lax.associative_scan(link, (decay_step, normalized), axis=0)
    carried = entering(
        (prefix_decay[-1], prefix_state[-1]),
        "seq",
        link,
        (jnp.ones((width,), jnp.float32), jnp.zeros((width,), jnp.float32)),
        False,
    )
    state_in = carried[1]
    hidden = prefix_state + prefix_decay * state_in
    branch_act, branch_pull = jax.vjp(jax.nn.gelu, branch)
    gated = (hidden * branch_act).astype(jnp.bfloat16)
    residual = inputs + jnp.dot(gated, out_all, preferred_element_type=jnp.float32)
    normed_two, norm_two_pull = jax.vjp(rms_scale, residual, gain_two_all.astype(jnp.float32))
    normed_two_low = normed_two.astype(jnp.bfloat16)
    gate_up_all, down_all = (
        lax.all_gather(gate_up, ("bucket", "seq"), axis=0, tiled=True),
        lax.all_gather(down_proj, ("bucket", "seq"), axis=0, tiled=True),
    )
    expanded = jnp.dot(normed_two_low, gate_up_all, preferred_element_type=jnp.float32)
    feed, feed_pull = jax.vjp(partial(gated_gelu, split=ff_width), expanded)
    feed_low = feed.astype(jnp.bfloat16)
    output_rows = residual + jnp.dot(feed_low, down_all, preferred_element_type=jnp.float32)
    mixed = (keep[:, None] * output_rows).astype(jnp.bfloat16)
    upstream = keep[:, None] * cotangent[0].astype(jnp.float32)
    upstream_low = upstream.astype(jnp.bfloat16)
    down_grad = lax.psum_scatter(
        row_product(feed_low, upstream_low), ("bucket", "seq"), scatter_dimension=0, tiled=True
    )
    feed_grad = contract_last(upstream_low, down_all)
    expanded_grad = feed_pull(feed_grad)[0].astype(jnp.bfloat16)
    gate_up_grad = lax.psum_scatter(
        row_product(normed_two_low, expanded_grad),
        ("bucket", "seq"),
        scatter_dimension=0,
        tiled=True,
    )
    normed_two_grad = contract_last(expanded_grad, gate_up_all)
    residual_part, gain_two_grad = norm_two_pull(normed_two_grad)
    residual_grad = upstream + residual_part
    residual_low = residual_grad.astype(jnp.bfloat16)
    out_grad = contract_first(gated, residual_low)
    gated_grad = contract_last(residual_low, out_all)
    hidden_grad = gated_grad * branch_act
    branch_grad = branch_pull(gated_grad * hidden)[0]
    next_decay = jnp.concatenate([decay_step[1:], jnp.ones((1, width), jnp.float32)], axis=0)
    suffix_decay, suffix_state = lax.associative_scan(
        link, (next_decay, hidden_grad), reverse=True, axis=0
    )
    returned = entering(
        (prefix_decay[-1], decay_step[0] * suffix_state[0]),
        "seq",
        link,
        (jnp.ones((width,), jnp.float32), jnp.zeros((width,), jnp.float32)),
        True,
    )
    incoming = returned[1]
    state_grad = suffix_state + suffix_decay * incoming
    state_before = jnp.concatenate([state_in[None, :], hidden[:-1]], axis=0)
    conv_grad_lru, gate_a_grad, gate_i_grad, decay_grad = lru_pull(
        (state_grad * state_before, state_grad)
    )
    gates_low = jnp.concatenate(
        [
            gate_a_grad.reshape(tok_rows, NB, block_width),
            gate_i_grad.reshape(tok_rows, NB, block_width),
        ],
        axis=2,
    ).astype(jnp.bfloat16)
    gate_grad = jnp.einsum(
        "tnc,tnd->ncd",
        conv_out.reshape(tok_rows, NB, block_width),
        gates_low,
        preferred_element_type=jnp.float32,
    ).reshape(width, 2 * block_width)
    bias_sums = jnp.sum(gates_low.astype(jnp.float32), axis=0)
    gate_bias_grad = jnp.stack(
        [bias_sums[:, :block_width].reshape(width), bias_sums[:, block_width:].reshape(width)],
        axis=1,
    )
    conv_grad_gates = jnp.einsum(
        "tnd,ncd->tnc",
        gates_low,
        gate_all.reshape(NB, block_width, 2 * block_width),
        preferred_element_type=jnp.float32,
    ).reshape(tok_rows, width)
    conv_low = (conv_grad_lru + conv_grad_gates).astype(jnp.bfloat16)
    head = from_behind(conv_low[:rim_rows], "seq", -1)
    trailing = jnp.concatenate([conv_low, head], axis=0)
    conv_low_float = conv_low.astype(jnp.float32)
    mixer_grad = jnp.zeros((tok_rows, width), jnp.float32)
    tap_grads = []
    for offset in range(kernel):
        later_ids = segment_layout(lengths_row, positions + offset)[0]
        ahead = jnp.where(
            (later_ids == segment_ids)[:, None],
            trailing[offset : offset + tok_rows].astype(jnp.float32),
            0.0,
        )
        mixer_grad = mixer_grad + ahead * conv_float[:, offset]
        tap_grads.append(jnp.sum(conv_low_float * lagged_terms[offset], axis=0))
    conv_weight_grad = jnp.stack(tap_grads, axis=1)
    conv_bias_grad = jnp.sum(conv_low_float, axis=0)
    proj_grad_low = jnp.concatenate([mixer_grad, branch_grad], axis=1).astype(jnp.bfloat16)
    in_proj_grad = contract_first(normed_low, proj_grad_low)
    normed_grad = contract_last(proj_grad_low, proj_all)
    input_part, gain_one_grad = norm_pull(normed_grad)
    token_grad = residual_grad + input_part
    summed = (
        lax.psum_scatter(gain_one_grad, ("bucket", "seq"), scatter_dimension=0, tiled=True),
        lax.psum_scatter(in_proj_grad, ("bucket", "seq"), scatter_dimension=0, tiled=True),
        lax.psum_scatter(conv_weight_grad, ("bucket", "seq"), scatter_dimension=0, tiled=True),
        lax.psum_scatter(conv_bias_grad, ("bucket", "seq"), scatter_dimension=0, tiled=True),
        lax.psum_scatter(gate_grad, ("bucket", "seq"), scatter_dimension=0, tiled=True),
        lax.psum_scatter(gate_bias_grad, ("bucket", "seq"), scatter_dimension=0, tiled=True),
        lax.psum_scatter(decay_grad, ("bucket", "seq"), scatter_dimension=0, tiled=True),
        lax.psum_scatter(out_grad, ("bucket", "seq"), scatter_dimension=0, tiled=True),
        lax.psum_scatter(gain_two_grad, ("bucket", "seq"), scatter_dimension=0, tiled=True),
    )
    return (
        mixed[None],
        token_grad[None],
        summed[0],
        summed[1],
        summed[2],
        summed[3],
        summed[4],
        summed[5],
        summed[6],
        summed[7],
        summed[8],
        gate_up_grad,
        down_grad,
    )


def swap_with(block, mask):
    route = [(i, i ^ mask) for i in range(lax.axis_size("seq"))]
    return lax.ppermute(block, "seq", route)


def plane_bits():
    return [1 << bit for bit in range(1, lax.axis_size("seq").bit_length() - 1)]


def gather_plane(block):
    half = block.shape[1] // 2
    sides = []
    for part, masks in (
        (block[None, :, :half], plane_bits()),
        (block[None, :, half:], plane_bits()[::-1]),
    ):
        order = [0]
        for mask in masks:
            part = jnp.concatenate([part, swap_with(part, mask)], axis=0)
            order = order + [i ^ mask for i in order]
        ranked = sorted(range(len(order)), key=order.__getitem__)
        if ranked != list(range(len(order))):
            part = jnp.concatenate([part[i : i + 1] for i in ranked], axis=0)
        sides.append(part)
    near = jnp.concatenate(sides, axis=2)
    return jnp.concatenate([near, swap_with(near, 1)], axis=0)


def reduce_plane(partial_rows):
    count, _, depth = partial_rows.shape
    near = partial_rows[: count // 2].astype(jnp.float32) + swap_with(
        partial_rows[count // 2 :].astype(jnp.bfloat16), 1
    ).astype(jnp.float32)
    upper, lower = near[:, :, : depth // 2], near[:, :, depth // 2 :]
    for mask in plane_bits()[::-1]:
        middle = upper.shape[0] // 2
        upper = upper[:middle] + swap_with(upper[middle:].astype(jnp.bfloat16), mask).astype(
            jnp.float32
        )
    for mask in plane_bits():
        lower = lower[0::2] + swap_with(lower[1::2].astype(jnp.bfloat16), mask).astype(jnp.float32)
    return jnp.concatenate([upper[0], lower[0]], axis=1)


def place_of(chunk, me, count):
    relative = jnp.bitwise_xor(chunk, me)
    return jnp.bitwise_and(relative, 1) * (count // 2) + jnp.right_shift(relative, 1)


def series_expm1(values):
    total = 1.0 + values * (1.0 / 7.0)
    for term in (6, 5, 4, 3, 2):
        total = 1.0 + values * (1.0 / term) * total
    return values * total


def segment_reach(info_ref, first, slots, shape, total):
    positions = first + lax.broadcasted_iota(jnp.int32, shape, 0)
    begin = jnp.zeros(shape, jnp.int32)
    finish = jnp.full(shape, total, jnp.int32)
    for slot in range(slots):
        end = info_ref[1 + slot]
        passed = positions >= end
        begin = jnp.where(passed, jnp.maximum(begin, end), begin)
        finish = jnp.where(passed, finish, jnp.minimum(finish, end))
    return positions - begin, finish - positions


def widen(mask, lanes):
    return jnp.concatenate([mask] * (lanes // mask.shape[1]), axis=1)


def gelu_parts(values):
    inner = 0.7978845608028654 * (values + 0.044715 * values * values * values)
    bent = jnp.tanh(inner)
    half = 0.5 * (1.0 + bent)
    slope = half + 0.5 * values * (1.0 - bent * bent) * 0.7978845608028654 * (
        1.0 + 3.0 * 0.044715 * values * values
    )
    return values * half, slope


ROWS = 8
TAP, BIAS, BIAS_A, BIAS_I, RATE = 0, 4, 5, 6, 7


def mixer_forward(
    taps,
    slots,
    info_ref,
    normed_ref,
    proj_ref,
    gate_ref,
    channel_ref,
    gated_ref,
    lagging_ref,
    conv_ref,
    branch_ref,
    gate_r_ref,
    gate_i_ref,
    hidden_ref,
    lag_edge_ref,
    hidden_edge_ref,
    projected,
    convolved,
    gates,
    carry,
    edge,
):
    chunk = pl.program_id(0)
    rows, lanes = convolved.shape
    tiles = rows // ROWS
    total = rows * pl.num_programs(0)

    @pl.when(chunk == 0)
    def _():
        carry[...] = jnp.zeros_like(carry)
        edge[...] = jnp.zeros_like(edge)

    product = jnp.dot(normed_ref[0], proj_ref[...], preferred_element_type=jnp.float32)
    low = product[:, :lanes].astype(jnp.bfloat16)
    lagging_ref[0] = low
    projected[:, :lanes] = low.astype(jnp.float32)
    branch_ref[0] = product[:, lanes:]
    place = lax.broadcasted_iota(jnp.int32, (ROWS, lanes), 0)

    def convolve(tile, before):
        at = pl.ds(pl.multiple_of(tile * ROWS, ROWS), ROWS)
        here = projected[at, :lanes]
        since, _ = segment_reach(info_ref, chunk * rows + tile * ROWS, slots, (ROWS, 128), total)
        value = channel_ref[BIAS : BIAS + 1, :] + here * channel_ref[TAP : TAP + 1, :]
        for lag in range(1, taps):
            moved = jnp.where(
                place < lag, pltpu.roll(before, lag, 0), pltpu.roll(here, lag, 0)
            )
            value = value + jnp.where(widen(since >= lag, lanes), moved, 0.0) * (
                channel_ref[TAP + lag : TAP + lag + 1, :]
            )
        convolved[at, :] = value
        return here

    last = lax.fori_loop(0, tiles, convolve, edge[...])
    edge[...] = last
    lag_edge_ref[0] = last
    conv_low = convolved[...].astype(jnp.bfloat16)
    conv_ref[0] = conv_low
    convolved[...] = conv_low.astype(jnp.float32)
    gates[...] = jnp.dot(conv_low, gate_ref[...], preferred_element_type=jnp.float32)

    def recur(tile, state):
        at = pl.ds(pl.multiple_of(tile * ROWS, ROWS), ROWS)
        since, _ = segment_reach(info_ref, chunk * rows + tile * ROWS, slots, (ROWS, 128), total)
        starts = widen(since == 0, lanes)
        gate_r = jax.nn.sigmoid(gates[at, :lanes] + channel_ref[BIAS_A : BIAS_A + 1, :])
        gate_i = jax.nn.sigmoid(gates[at, lanes:] + channel_ref[BIAS_I : BIAS_I + 1, :])
        gate_r_ref[0, at, :] = gate_r
        gate_i_ref[0, at, :] = gate_i
        less = series_expm1(-gate_scale * gate_r * channel_ref[RATE : RATE + 1, :])
        decay = jnp.where(starts, 0.0, 1.0 + less)
        scaling = jnp.where(starts, 1.0, jnp.sqrt(-less * (2.0 + less)))
        value = convolved[at, :] * gate_i * scaling
        for step in (1, 2, 4):
            inside = place >= step
            value = value + jnp.where(inside, decay * pltpu.roll(value, step, 0), 0.0)
            decay = jnp.where(inside, decay * pltpu.roll(decay, step, 0), decay)
        hidden = value + decay * state
        hidden_ref[0, at, :] = hidden
        projected[at, :lanes] = hidden * gelu_parts(branch_ref[0, at, :])[0]
        hidden_edge_ref[0] = hidden
        return jnp.broadcast_to(hidden[ROWS - 1 :], hidden.shape)

    carry[...] = lax.fori_loop(0, tiles, recur, carry[...])
    gated_ref[0] = projected[:, :lanes].astype(jnp.bfloat16)


def mixer_backward(
    taps,
    slots,
    info_ref,
    down_ref,
    out_ref,
    gate_ref,
    channel_ref,
    branch_ref,
    hidden_ref,
    gate_r_ref,
    gate_i_ref,
    conv_ref,
    lagging_ref,
    lag_edge_ref,
    hidden_edge_ref,
    projected_ref,
    gate_grad_ref,
    channel_grad_ref,
    coming,
    conv_part,
    lagged,
    gates,
    projected,
    conv_grad,
    grad_carry,
    decay_carry,
    sums,
):
    lap = pl.program_id(0)
    laps = pl.num_programs(0)
    chunk = laps - 1 - lap
    rows, lanes = conv_part.shape
    tiles = rows // ROWS
    total = rows * laps

    @pl.when(lap == 0)
    def _():
        grad_carry[...] = jnp.zeros_like(grad_carry)
        decay_carry[...] = jnp.zeros_like(decay_carry)
        conv_grad[...] = jnp.zeros_like(conv_grad)
        sums[...] = jnp.zeros_like(sums)
        gate_grad_ref[...] = jnp.zeros_like(gate_grad_ref)

    coming[...] = lax.dot_general(
        down_ref[0], out_ref[...], (((1,), (1,)), ((), ())), preferred_element_type=jnp.float32
    )
    lagged[...] = lagging_ref[0].astype(jnp.float32)
    conv_part[...] = conv_ref[0].astype(jnp.float32)
    place = lax.broadcasted_iota(jnp.int32, (ROWS, lanes), 0)
    first_chunk = chunk == 0

    def recur(step_index, carried):
        later_grad, later_decay, sum_a, sum_i, sum_rate = carried
        tile = tiles - 1 - step_index
        at = pl.ds(pl.multiple_of(tile * ROWS, ROWS), ROWS)
        ahead = pl.ds(pl.multiple_of(jnp.maximum(tile - 1, 0) * ROWS, ROWS), ROWS)
        since, _ = segment_reach(info_ref, chunk * rows + tile * ROWS, slots, (ROWS, 128), total)
        starts = widen(since == 0, lanes)
        gate_r = gate_r_ref[0, at, :]
        gate_i = gate_i_ref[0, at, :]
        hidden = hidden_ref[0, at, :]
        conv = conv_part[at, :]
        rate = channel_ref[RATE : RATE + 1, :]
        log_step = -gate_scale * gate_r * rate
        less = series_expm1(log_step)
        plain = 1.0 + less
        root = jnp.sqrt(-less * (2.0 + less))
        decay = jnp.where(starts, 0.0, plain)
        scaling = jnp.where(starts, 1.0, root)
        activated, slope = gelu_parts(branch_ref[0, at, :])
        down = coming[at, :]
        value = down * activated
        projected[at, lanes:] = down * hidden * slope
        weight = jnp.where(place == ROWS - 1, later_decay, pltpu.roll(decay, ROWS - 1, 0))
        for step in (1, 2, 4):
            inside = place < ROWS - step
            value = value + jnp.where(inside, weight * pltpu.roll(value, ROWS - step, 0), 0.0)
            weight = jnp.where(inside, weight * pltpu.roll(weight, ROWS - step, 0), weight)
        grad = value + weight * later_grad
        earlier = jnp.where(
            tile == 0,
            jnp.where(first_chunk, 0.0, hidden_edge_ref[0]),
            hidden_ref[0, ahead, :],
        )
        before = jnp.where(place == 0, pltpu.roll(earlier, 1, 0), pltpu.roll(hidden, 1, 0))
        scaled = grad * scaling
        conv_part[at, :] = scaled * gate_i
        grad_i = scaled * conv * gate_i * (1.0 - gate_i)
        grad_log = jnp.where(
            starts,
            0.0,
            grad * plain * (before - conv * gate_i * plain / root),
        )
        grad_rate = grad_log * gate_r
        grad_a = -gate_scale * rate * grad_rate * (1.0 - gate_r)
        grad_a = grad_a.astype(jnp.bfloat16).astype(jnp.float32)
        grad_i = grad_i.astype(jnp.bfloat16).astype(jnp.float32)
        gates[at, :lanes] = grad_a
        gates[at, lanes:] = grad_i
        return (
            jnp.broadcast_to(grad[:1], grad.shape),
            jnp.broadcast_to(decay[:1], decay.shape),
            sum_a + grad_a,
            sum_i + grad_i,
            sum_rate - gate_scale * grad_rate,
        )

    empty = jnp.zeros((ROWS, lanes), jnp.float32)
    grad_last, decay_last, sum_a, sum_i, sum_rate = lax.fori_loop(
        0, tiles, recur, (grad_carry[...], decay_carry[...], empty, empty, empty)
    )
    grad_carry[...] = grad_last
    decay_carry[...] = decay_last
    gates_low = gates[...].astype(jnp.bfloat16)
    gate_grad_ref[...] += lax.dot_general(
        conv_ref[0], gates_low, (((0,), (0,)), ((), ())), preferred_element_type=jnp.float32
    )
    from_gates = lax.dot_general(
        gates_low, gate_ref[...], (((1,), (1,)), ((), ())), preferred_element_type=jnp.float32
    )
    conv_grad[rows:, :] = conv_grad[:ROWS, :]
    conv_grad[:rows, :] = (conv_part[...] + from_gates).astype(jnp.bfloat16).astype(jnp.float32)

    def unconvolve(tile, carried):
        earlier, sum_bias, sum_taps = carried
        at = pl.ds(pl.multiple_of(tile * ROWS, ROWS), ROWS)
        beyond = pl.ds(pl.multiple_of((tile + 1) * ROWS, ROWS), ROWS)
        since, until = segment_reach(
            info_ref, chunk * rows + tile * ROWS, slots, (ROWS, 128), total
        )
        here = lagged[at, :]
        grad = conv_grad[at, :]
        later = conv_grad[beyond, :]
        value = grad * channel_ref[TAP : TAP + 1, :]
        new_taps = [sum_taps[0] + grad * here]
        for lag in range(1, taps):
            ahead = jnp.where(
                place < ROWS - lag, pltpu.roll(grad, ROWS - lag, 0), pltpu.roll(later, ROWS - lag, 0)
            )
            value = value + jnp.where(widen(until > lag, lanes), ahead, 0.0) * (
                channel_ref[TAP + lag : TAP + lag + 1, :]
            )
            moved = jnp.where(
                place < lag, pltpu.roll(earlier, lag, 0), pltpu.roll(here, lag, 0)
            )
            new_taps.append(
                sum_taps[lag] + grad * jnp.where(widen(since >= lag, lanes), moved, 0.0)
            )
        projected[at, :lanes] = value
        return here, sum_bias + grad, tuple(new_taps)

    _, sum_bias, sum_taps = lax.fori_loop(
        0, tiles, unconvolve, (lag_edge_ref[0], empty, (empty,) * taps)
    )
    projected_ref[0] = projected[...].astype(jnp.bfloat16)
    for place_in, part in enumerate((*sum_taps, sum_bias, sum_a, sum_i, sum_rate)):
        sums[place_in] += part

    @pl.when(lap == laps - 1)
    def _():
        channel_grad_ref[...] = jnp.sum(sums[...], axis=1)


VMEM_LIMIT = 48 * 1024 * 1024


def run_forward(info, normed, proj, gate, channels, taps, slots):
    count, rows, depth = normed.shape
    lanes = gate.shape[0]

    def at_place(chunk, info_ref):
        return (place_of(chunk, info_ref[0], count), 0, 0)

    def at_chunk(chunk, info_ref):
        return (chunk, 0, 0)

    def whole(chunk, info_ref):
        return (0, 0)

    def block(kind):
        return jax.ShapeDtypeStruct((count, rows, lanes), kind)

    narrow = pl.BlockSpec((1, rows, lanes), at_place)
    return pl.pallas_call(
        partial(mixer_forward, taps, slots),
        grid_spec=pltpu.PrefetchScalarGridSpec(
            num_scalar_prefetch=1,
            grid=(count,),
            in_specs=[
                pl.BlockSpec((1, rows, depth), at_place),
                pl.BlockSpec(proj.shape, whole),
                pl.BlockSpec(gate.shape, whole),
                pl.BlockSpec(channels.shape, whole),
            ],
            out_specs=[narrow] * 7 + [pl.BlockSpec((1, ROWS, lanes), at_chunk)] * 2,
            scratch_shapes=[
                pltpu.VMEM((rows, lanes), jnp.float32),
                pltpu.VMEM((rows, lanes), jnp.float32),
                pltpu.VMEM((rows, 2 * lanes), jnp.float32),
                pltpu.VMEM((ROWS, lanes), jnp.float32),
                pltpu.VMEM((ROWS, lanes), jnp.float32),
            ],
        ),
        out_shape=[
            block(jnp.bfloat16),
            block(jnp.bfloat16),
            block(jnp.bfloat16),
            block(jnp.float32),
            block(jnp.float32),
            block(jnp.float32),
            block(jnp.float32),
        ]
        + [jax.ShapeDtypeStruct((count, ROWS, lanes), jnp.float32)] * 2,
        compiler_params=pltpu.CompilerParams(
            dimension_semantics=("arbitrary",), vmem_limit_bytes=VMEM_LIMIT
        ),
        cost_estimate=pl.CostEstimate(
            flops=2 * count * rows * lanes * (2 * depth + 2 * lanes),
            bytes_accessed=2 * normed.size + 25 * count * rows * lanes,
            transcendentals=5 * count * rows * lanes,
        ),
        name="mixer_forward",
    )(info, normed, proj, gate, channels)


def run_backward(info, down, out, gate, channels, saved, taps, slots):
    _, lagging, conv, branch, gate_r, gate_i, hidden, lag_edge, hidden_edge = saved
    count, rows, depth = down.shape
    lanes = gate.shape[0]

    def at_place(lap, info_ref):
        return (place_of(count - 1 - lap, info_ref[0], count), 0, 0)

    def before(lap, info_ref):
        return (jnp.maximum(count - 2 - lap, 0), 0, 0)

    def whole(lap, info_ref):
        return (0, 0)

    narrow = pl.BlockSpec((1, rows, lanes), at_place)
    rim = pl.BlockSpec((1, ROWS, lanes), before)
    sums = taps + 4
    return pl.pallas_call(
        partial(mixer_backward, taps, slots),
        grid_spec=pltpu.PrefetchScalarGridSpec(
            num_scalar_prefetch=1,
            grid=(count,),
            in_specs=[
                pl.BlockSpec((1, rows, depth), at_place),
                pl.BlockSpec(out.shape, whole),
                pl.BlockSpec(gate.shape, whole),
                pl.BlockSpec(channels.shape, whole),
                narrow,
                narrow,
                narrow,
                narrow,
                narrow,
                narrow,
                rim,
                rim,
            ],
            out_specs=[
                pl.BlockSpec((1, rows, 2 * lanes), at_place),
                pl.BlockSpec((lanes, 2 * lanes), whole),
                pl.BlockSpec((sums, lanes), whole),
            ],
            scratch_shapes=[
                pltpu.VMEM((rows, lanes), jnp.float32),
                pltpu.VMEM((rows, lanes), jnp.float32),
                pltpu.VMEM((rows, lanes), jnp.float32),
                pltpu.VMEM((rows, 2 * lanes), jnp.float32),
                pltpu.VMEM((rows, 2 * lanes), jnp.float32),
                pltpu.VMEM((rows + ROWS, lanes), jnp.float32),
                pltpu.VMEM((ROWS, lanes), jnp.float32),
                pltpu.VMEM((ROWS, lanes), jnp.float32),
                pltpu.VMEM((sums, ROWS, lanes), jnp.float32),
            ],
        ),
        out_shape=[
            jax.ShapeDtypeStruct((count, rows, 2 * lanes), jnp.bfloat16),
            jax.ShapeDtypeStruct((lanes, 2 * lanes), jnp.float32),
            jax.ShapeDtypeStruct((sums, lanes), jnp.float32),
        ],
        compiler_params=pltpu.CompilerParams(
            dimension_semantics=("arbitrary",), vmem_limit_bytes=VMEM_LIMIT
        ),
        cost_estimate=pl.CostEstimate(
            flops=2 * count * rows * lanes * (depth + 4 * lanes),
            bytes_accessed=2 * down.size + 24 * count * rows * lanes,
            transcendentals=3 * count * rows * lanes,
        ),
        name="mixer_backward",
    )(info, down, out, gate, channels, branch, hidden, gate_r, gate_i, conv, lagging, lag_edge, hidden_edge)


def hand_out(rows, groups):
    dealt = lax.all_to_all(groups, "seq", split_axis=0, concat_axis=0, tiled=True)
    return lax.all_gather(dealt.reshape(-1, groups.shape[2]), "bucket", axis=0, tiled=True)


def hand_back(grad):
    count = lax.axis_size("seq")
    summed = lax.psum_scatter(
        grad.astype(jnp.bfloat16), "bucket", scatter_dimension=0, tiled=True
    )
    blocks = summed.reshape(count, -1, grad.shape[1])
    return lax.all_to_all(blocks, "seq", split_axis=0, concat_axis=0, tiled=True).astype(
        jnp.float32
    )


def pad_lanes(values, lanes):
    return jnp.pad(values, [(0, 0)] * (values.ndim - 1) + [(0, lanes - values.shape[-1])])


def by_channels(
    tokens,
    lengths,
    norm_gain,
    in_proj,
    conv_weight,
    conv_bias,
    gate_weight,
    gate_bias,
    decay,
    out_proj,
    mlp_gain,
    gate_up,
    down_proj,
    cotangent,
):
    planes = lax.axis_size("bucket")
    count = lax.axis_size("seq")
    me = lax.axis_index("seq")
    odd = jnp.bitwise_and(me, 1)
    inputs = tokens[0].astype(jnp.float32)
    rows, depth = inputs.shape
    own_rows = in_proj.shape[0]
    width = in_proj.shape[1] // 2
    block_width = width // NB
    held = planes // 2
    channels = held * block_width
    lanes = -(-channels // 128) * 128
    chunk_rows = conv_weight.shape[0]
    hidden_width = gate_up.shape[1] // 2 // count
    hidden_rows = down_proj.shape[0]
    taps = conv_weight.shape[1]
    slots = lengths.shape[1]

    by_row = jnp.concatenate(
        [out_proj, gate_weight, conv_weight, conv_bias[:, None], gate_bias, decay[:, None]], axis=1
    )
    by_row_width = by_row.shape[1]
    by_row = lax.all_gather(
        pad_lanes(by_row, -(-by_row_width // 128) * 128), "bucket", axis=0, tiled=False
    )
    gains = jnp.stack([norm_gain, mlp_gain])[None]
    gains = lax.all_gather(gains, "seq", axis=0, tiled=True)
    gains = lax.all_gather(gains[None], "bucket", axis=0, tiled=True).astype(jnp.float32)
    gain_one, gain_two = gains[:, :, 0].reshape(1, depth), gains[:, :, 1].reshape(1, depth)
    proj_groups = (
        in_proj.reshape(own_rows, 2, 2, held, count // 2, block_width)
        .transpose(4, 2, 0, 1, 3, 5)
        .reshape(count, own_rows, 2 * channels)
    )
    proj = hand_out(own_rows, proj_groups)
    proj = pad_lanes(proj.reshape(depth, 2, channels), lanes).reshape(depth, 2 * lanes)
    wide_groups = (
        gate_up.reshape(own_rows, 2, planes, count, hidden_rows)
        .transpose(3, 0, 1, 2, 4)
        .reshape(count, own_rows, 2 * hidden_width)
    )
    wide = hand_out(own_rows, wide_groups)
    narrow = lax.all_gather(down_proj, "bucket", axis=0, tiled=True)

    kept = lax.dynamic_slice_in_dim(by_row, odd * held, held, 0)
    given = lax.dynamic_slice_in_dim(by_row, (1 - odd) * held, held, 0)
    taken = swap_with(given, 1)
    pair = jnp.where(
        odd == 0, jnp.stack([kept, taken], axis=1), jnp.stack([taken, kept], axis=1)
    )
    by_channel = pair.reshape(channels, -1)
    out = jnp.pad(by_channel[:, :depth], [(0, lanes - channels), (0, 0)])
    gate_columns = 2 * block_width
    gate_rows = by_channel[:, depth : depth + gate_columns]
    gate_blocks = []
    for index in range(held):
        part = gate_rows[index * block_width : (index + 1) * block_width]
        at = index * block_width
        gate_blocks.append(
            jnp.concatenate(
                [
                    jnp.pad(side, [(0, 0), (at, lanes - at - block_width)])
                    for side in (part[:, :block_width], part[:, block_width:])
                ],
                axis=1,
            )
        )
    gate = jnp.pad(jnp.concatenate(gate_blocks, axis=0), [(0, lanes - channels), (0, 0)])
    small = by_channel[:, depth + gate_columns : by_row_width].astype(jnp.float32).T
    decay_channel = small[taps + 3]
    rate = jnp.pad(jax.nn.softplus(decay_channel), (0, lanes - channels), constant_values=0.01)
    channel = jnp.concatenate([pad_lanes(small[: taps + 3], lanes), rate[None]], axis=0)
    ends = jnp.cumsum(lengths[0]).astype(jnp.int32)
    info = jnp.concatenate([me[None].astype(jnp.int32), ends])

    positions = me * rows + jnp.arange(rows, dtype=jnp.int32)
    keep = (positions < ends[-1]).astype(jnp.float32)[:, None]
    upstream = keep * cotangent[0].astype(jnp.float32)
    scale_one = lax.rsqrt(jnp.mean(inputs * inputs, axis=1, keepdims=True) + norm_eps)
    normed = gather_plane((inputs * scale_one * gain_one).astype(jnp.bfloat16))
    upstream_all = gather_plane(upstream.astype(jnp.bfloat16)).reshape(-1, depth)
    saved = run_forward(info, normed, proj, gate, channel, taps, slots)
    gated = saved[0].reshape(-1, lanes)
    mixed_part = jnp.dot(gated, out, preferred_element_type=jnp.float32).astype(jnp.bfloat16)
    residual = inputs + reduce_plane(mixed_part.reshape(count, rows, depth))
    scale_two = lax.rsqrt(jnp.mean(residual * residual, axis=1, keepdims=True) + norm_eps)
    normed_two = gather_plane((residual * scale_two * gain_two).astype(jnp.bfloat16))
    normed_two = normed_two.reshape(-1, depth)
    expanded = jnp.dot(normed_two, wide, preferred_element_type=jnp.float32)
    feed, feed_pull = jax.vjp(partial(gated_gelu, split=hidden_width), expanded)
    feed_low = feed.astype(jnp.bfloat16)
    output_part = jnp.dot(feed_low, narrow, preferred_element_type=jnp.float32)
    output_part = output_part.astype(jnp.bfloat16).reshape(count, rows, depth)
    mixed = (keep * (residual + reduce_plane(output_part))).astype(jnp.bfloat16)

    feed_grad = contract_last(upstream_all, narrow)
    expanded_grad = feed_pull(feed_grad)[0].astype(jnp.bfloat16)
    normed_two_part = contract_last(expanded_grad, wide).astype(jnp.bfloat16)
    normed_two_grad = reduce_plane(normed_two_part.reshape(count, rows, depth))

    def norm_back(values, scale, gain, grad):
        scaled = grad * gain
        lean = jnp.mean(scaled * values, axis=1, keepdims=True)
        return scale * scaled - scale * scale * scale * lean * values

    residual_grad = upstream + norm_back(residual, scale_two, gain_two, normed_two_grad)
    residual_low = gather_plane(residual_grad.astype(jnp.bfloat16))
    proj_grad, gate_grad, channel_grad = run_backward(
        info, residual_low, out, gate, channel, saved, taps, slots
    )
    proj_grad = proj_grad.reshape(-1, 2 * lanes)
    normed_part = contract_last(proj_grad, proj).astype(jnp.bfloat16)
    normed_grad = reduce_plane(normed_part.reshape(count, rows, depth))
    token_grad = residual_grad + norm_back(inputs, scale_one, gain_one, normed_grad)

    down_grad = lax.psum_scatter(
        contract_first(feed_low, upstream_all).astype(jnp.bfloat16),
        "bucket",
        scatter_dimension=0,
        tiled=True,
    ).astype(jnp.float32)
    wide_grad = hand_back(contract_first(normed_two, expanded_grad))
    gate_up_grad = (
        wide_grad.reshape(count, own_rows, 2, planes, hidden_rows)
        .transpose(1, 2, 3, 0, 4)
        .reshape(own_rows, -1)
    )
    out_grad = contract_first(gated, residual_low.reshape(-1, depth))[:channels]
    gate_parts = []
    for index in range(held):
        at = index * block_width
        span = gate_grad[at : at + block_width]
        gate_parts.append(
            jnp.concatenate(
                [span[:, at : at + block_width], span[:, lanes + at : lanes + at + block_width]],
                axis=1,
            )
        )
    channel_grad = channel_grad[:, :channels]
    small_grad = jnp.concatenate(
        [
            channel_grad[: taps + 3],
            (channel_grad[taps + 3] * jax.nn.sigmoid(decay_channel))[None],
        ],
        axis=0,
    )
    by_row_grad = jnp.concatenate(
        [out_grad, jnp.concatenate(gate_parts, axis=0), small_grad.T], axis=1
    ).astype(jnp.bfloat16)
    by_row_grad = pad_lanes(by_row_grad, by_row.shape[2]).reshape(held, 2, chunk_rows, -1)
    kept = lax.dynamic_index_in_dim(by_row_grad, odd, 1, False)
    taken = swap_with(lax.dynamic_index_in_dim(by_row_grad, 1 - odd, 1, False), 1)
    by_row_grad = jnp.where(
        odd == 0, jnp.concatenate([kept, taken]), jnp.concatenate([taken, kept])
    )
    by_row_grad = lax.psum_scatter(
        by_row_grad.reshape(planes * chunk_rows, -1), "bucket", scatter_dimension=0, tiled=True
    ).astype(jnp.float32)
    out_proj_grad = by_row_grad[:, :depth]
    gate_weight_grad = by_row_grad[:, depth : depth + gate_columns]
    small_grad = by_row_grad[:, depth + gate_columns : by_row_width]
    narrow_grad = jnp.pad(
        contract_first(normed.reshape(-1, depth), proj_grad).reshape(depth, 2, lanes)[
            :, :, :channels
        ].reshape(depth, 2 * channels),
        [(0, 0), (0, 0)],
    )
    in_proj_grad = (
        hand_back(narrow_grad)
        .reshape(count // 2, 2, own_rows, 2, held, block_width)
        .transpose(2, 3, 1, 4, 0, 5)
        .reshape(own_rows, -1)
    )
    norm_gain_grad = jnp.sum(in_proj_grad * in_proj.astype(jnp.float32), axis=1) / norm_gain.astype(
        jnp.float32
    )
    mlp_gain_grad = jnp.sum(gate_up_grad * gate_up.astype(jnp.float32), axis=1) / mlp_gain.astype(
        jnp.float32
    )
    return (
        mixed[None],
        token_grad[None],
        norm_gain_grad,
        in_proj_grad,
        small_grad[:, :taps],
        small_grad[:, taps],
        gate_weight_grad,
        small_grad[:, taps + 1 : taps + 3],
        small_grad[:, taps + 3],
        out_proj_grad,
        mlp_gain_grad,
        gate_up_grad,
        down_grad,
    )


def solution(mesh):
    planes, count = mesh.shape["bucket"], mesh.shape["seq"]
    whole_blocks = planes % 2 == 0 and planes * count == 2 * NB
    return jax.shard_map(
        by_channels if whole_blocks else on_device,
        mesh=mesh,
        in_specs=(
            P("bucket", "seq", None),
            P("bucket", None),
            P(("bucket", "seq")),
            P(("bucket", "seq"), None),
            P(("bucket", "seq"), None),
            P(("bucket", "seq")),
            P(("bucket", "seq"), None),
            P(("bucket", "seq"), None),
            P(("bucket", "seq")),
            P(("bucket", "seq"), None),
            P(("bucket", "seq")),
            P(("bucket", "seq"), None),
            P(("bucket", "seq"), None),
            P("bucket", "seq", None),
        ),
        out_specs=(
            P("bucket", "seq", None),
            P("bucket", "seq", None),
            P(("bucket", "seq")),
            P(("bucket", "seq"), None),
            P(("bucket", "seq"), None),
            P(("bucket", "seq")),
            P(("bucket", "seq"), None),
            P(("bucket", "seq"), None),
            P(("bucket", "seq")),
            P(("bucket", "seq"), None),
            P(("bucket", "seq")),
            P(("bucket", "seq"), None),
            P(("bucket", "seq"), None),
        ),
        check_vma=False,
    )
```

```python
from functools import partial

import jax
import jax.numpy as jnp
from jax import lax
from jax.experimental import pallas as pl
from jax.experimental.pallas import tpu as pltpu
from jax.sharding import PartitionSpec as P

NB = 16


norm_eps = 1e-06
gate_scale = 8.0


def from_behind(block, axis, distance):
    devices = range(lax.axis_size(axis))
    route = [(i - distance, i) for i in devices if i - distance in devices]
    return lax.ppermute(block, axis, route)


def entering(part, axis, combine, identity, reverse):
    count = lax.axis_size(axis)
    place = lax.axis_index(axis)
    ahead = count - 1 - place if reverse else place
    gathered = jax.tree.map(lambda a: lax.all_gather(a, axis), part)
    state = jax.tree.map(lambda a, e: jnp.zeros_like(a) + jnp.asarray(e, a.dtype), part, identity)

    def one(lap, state):
        source = count - 1 - lap if reverse else lap
        return combine(
            state, jax.tree.map(lambda a: lax.dynamic_index_in_dim(a, source, 0, False), gathered)
        )

    return lax.fori_loop(0, ahead, one, state)


def rms_scale(values, gain):
    return values * lax.rsqrt(jnp.mean(values * values, axis=1, keepdims=True) + norm_eps) * gain


def link(earlier, later):
    return (earlier[0] * later[0], later[0] * earlier[1] + later[1])


def segment_layout(lengths_row, positions):
    ends = jnp.cumsum(lengths_row)
    segment_ids = jnp.sum((positions[:, None] >= ends[None, :]).astype(jnp.int32), axis=1)
    segment_ids = jnp.where(positions < 0, -1, segment_ids)
    keep = (positions < ends[-1]).astype(jnp.float32)
    return (segment_ids, keep)


def lru_terms(conv_out, gate_a, gate_i, decay, starts):
    rate = jax.nn.softplus(decay)
    log_step = -gate_scale * jax.nn.sigmoid(gate_a) * rate
    decay_step = jnp.where(starts, 0.0, jnp.exp(log_step))
    scaling = jnp.where(starts, 1.0, jnp.sqrt(-jnp.expm1(2.0 * log_step)))
    return (decay_step, conv_out * jax.nn.sigmoid(gate_i) * scaling)


def gated_gelu(values, split):
    return jax.nn.gelu(values[:, :split]) * values[:, split:]


def contract_last(left, right):
    return lax.dot_general(
        left, right, (((1,), (1,)), ((), ())), preferred_element_type=jnp.float32
    )


def contract_first(left, right):
    return lax.dot_general(
        left, right, (((0,), (0,)), ((), ())), preferred_element_type=jnp.float32
    )


def row_product(left, right):
    return contract_first(left, right)


def on_device(
    tokens,
    lengths,
    norm_gain,
    in_proj,
    conv_weight,
    conv_bias,
    gate_weight,
    gate_bias,
    decay,
    out_proj,
    mlp_gain,
    gate_up,
    down_proj,
    cotangent,
):
    inputs = tokens[0].astype(jnp.float32)
    tok_rows = inputs.shape[0]
    width = in_proj.shape[1] // 2
    ff_width = gate_up.shape[1] // 2
    block_width = width // NB
    kernel = conv_weight.shape[1]
    rim_rows = kernel - 1
    (
        gain_one_all,
        proj_all,
        conv_all,
        conv_bias_all,
        gate_all,
        gate_bias_all,
        decay_all,
        out_all,
        gain_two_all,
    ) = (
        lax.all_gather(norm_gain, ("bucket", "seq"), axis=0, tiled=True),
        lax.all_gather(in_proj, ("bucket", "seq"), axis=0, tiled=True),
        lax.all_gather(conv_weight, ("bucket", "seq"), axis=0, tiled=True),
        lax.all_gather(conv_bias, ("bucket", "seq"), axis=0, tiled=True),
        lax.all_gather(gate_weight, ("bucket", "seq"), axis=0, tiled=True),
        lax.all_gather(gate_bias, ("bucket", "seq"), axis=0, tiled=True),
        lax.all_gather(decay, ("bucket", "seq"), axis=0, tiled=True),
        lax.all_gather(out_proj, ("bucket", "seq"), axis=0, tiled=True),
        lax.all_gather(mlp_gain, ("bucket", "seq"), axis=0, tiled=True),
    )
    seq_index = lax.axis_index("seq")
    positions = seq_index * tok_rows + jnp.arange(tok_rows, dtype=jnp.int32)
    lengths_row = lengths[0]
    segment_ids, keep = segment_layout(lengths_row, positions)
    back_ids = segment_layout(lengths_row, positions - 1)[0]
    starts = (segment_ids != back_ids)[:, None]
    normed, norm_pull = jax.vjp(rms_scale, inputs, gain_one_all.astype(jnp.float32))
    normed_low = normed.astype(jnp.bfloat16)
    projected = jnp.dot(normed_low, proj_all, preferred_element_type=jnp.float32)
    mixer_in = projected[:, :width].astype(jnp.bfloat16)
    branch = projected[:, width:]
    rim = from_behind(mixer_in[tok_rows - rim_rows :], "seq", 1)
    extended = jnp.concatenate([rim, mixer_in], axis=0)
    conv_float = conv_all.astype(jnp.float32)
    lagged_terms = []
    convolved = jnp.zeros((tok_rows, width), jnp.float32) + conv_bias_all.astype(jnp.float32)
    for offset in range(kernel):
        earlier_ids = segment_layout(lengths_row, positions - offset)[0]
        lagged = jnp.where(
            (earlier_ids == segment_ids)[:, None],
            extended[rim_rows - offset : rim_rows - offset + tok_rows].astype(jnp.float32),
            0.0,
        )
        lagged_terms.append(lagged)
        convolved = convolved + lagged * conv_float[:, offset]
    conv_out = convolved.astype(jnp.bfloat16)
    gates = jnp.einsum(
        "tnc,ncd->tnd",
        conv_out.reshape(tok_rows, NB, block_width),
        gate_all.reshape(NB, block_width, 2 * block_width),
        preferred_element_type=jnp.float32,
    )
    gate_bias_float = gate_bias_all.astype(jnp.float32)
    gate_a = gates[:, :, :block_width].reshape(tok_rows, width) + gate_bias_float[:, 0]
    gate_i = gates[:, :, block_width:].reshape(tok_rows, width) + gate_bias_float[:, 1]
    (decay_step, normalized), lru_pull = jax.vjp(
        partial(lru_terms, starts=starts),
        conv_out.astype(jnp.float32),
        gate_a,
        gate_i,
        decay_all.astype(jnp.float32),
    )
    prefix_decay, prefix_state = lax.associative_scan(link, (decay_step, normalized), axis=0)
    carried = entering(
        (prefix_decay[-1], prefix_state[-1]),
        "seq",
        link,
        (jnp.ones((width,), jnp.float32), jnp.zeros((width,), jnp.float32)),
        False,
    )
    state_in = carried[1]
    hidden = prefix_state + prefix_decay * state_in
    branch_act, branch_pull = jax.vjp(jax.nn.gelu, branch)
    gated = (hidden * branch_act).astype(jnp.bfloat16)
    residual = inputs + jnp.dot(gated, out_all, preferred_element_type=jnp.float32)
    normed_two, norm_two_pull = jax.vjp(rms_scale, residual, gain_two_all.astype(jnp.float32))
    normed_two_low = normed_two.astype(jnp.bfloat16)
    gate_up_all, down_all = (
        lax.all_gather(gate_up, ("bucket", "seq"), axis=0, tiled=True),
        lax.all_gather(down_proj, ("bucket", "seq"), axis=0, tiled=True),
    )
    expanded = jnp.dot(normed_two_low, gate_up_all, preferred_element_type=jnp.float32)
    feed, feed_pull = jax.vjp(partial(gated_gelu, split=ff_width), expanded)
    feed_low = feed.astype(jnp.bfloat16)
    output_rows = residual + jnp.dot(feed_low, down_all, preferred_element_type=jnp.float32)
    mixed = (keep[:, None] * output_rows).astype(jnp.bfloat16)
    upstream = keep[:, None] * cotangent[0].astype(jnp.float32)
    upstream_low = upstream.astype(jnp.bfloat16)
    down_grad = lax.psum_scatter(
        row_product(feed_low, upstream_low), ("bucket", "seq"), scatter_dimension=0, tiled=True
    )
    feed_grad = contract_last(upstream_low, down_all)
    expanded_grad = feed_pull(feed_grad)[0].astype(jnp.bfloat16)
    gate_up_grad = lax.psum_scatter(
        row_product(normed_two_low, expanded_grad),
        ("bucket", "seq"),
        scatter_dimension=0,
        tiled=True,
    )
    normed_two_grad = contract_last(expanded_grad, gate_up_all)
    residual_part, gain_two_grad = norm_two_pull(normed_two_grad)
    residual_grad = upstream + residual_part
    residual_low = residual_grad.astype(jnp.bfloat16)
    out_grad = contract_first(gated, residual_low)
    gated_grad = contract_last(residual_low, out_all)
    hidden_grad = gated_grad * branch_act
    branch_grad = branch_pull(gated_grad * hidden)[0]
    next_decay = jnp.concatenate([decay_step[1:], jnp.ones((1, width), jnp.float32)], axis=0)
    suffix_decay, suffix_state = lax.associative_scan(
        link, (next_decay, hidden_grad), reverse=True, axis=0
    )
    returned = entering(
        (prefix_decay[-1], decay_step[0] * suffix_state[0]),
        "seq",
        link,
        (jnp.ones((width,), jnp.float32), jnp.zeros((width,), jnp.float32)),
        True,
    )
    incoming = returned[1]
    state_grad = suffix_state + suffix_decay * incoming
    state_before = jnp.concatenate([state_in[None, :], hidden[:-1]], axis=0)
    conv_grad_lru, gate_a_grad, gate_i_grad, decay_grad = lru_pull(
        (state_grad * state_before, state_grad)
    )
    gates_low = jnp.concatenate(
        [
            gate_a_grad.reshape(tok_rows, NB, block_width),
            gate_i_grad.reshape(tok_rows, NB, block_width),
        ],
        axis=2,
    ).astype(jnp.bfloat16)
    gate_grad = jnp.einsum(
        "tnc,tnd->ncd",
        conv_out.reshape(tok_rows, NB, block_width),
        gates_low,
        preferred_element_type=jnp.float32,
    ).reshape(width, 2 * block_width)
    bias_sums = jnp.sum(gates_low.astype(jnp.float32), axis=0)
    gate_bias_grad = jnp.stack(
        [bias_sums[:, :block_width].reshape(width), bias_sums[:, block_width:].reshape(width)],
        axis=1,
    )
    conv_grad_gates = jnp.einsum(
        "tnd,ncd->tnc",
        gates_low,
        gate_all.reshape(NB, block_width, 2 * block_width),
        preferred_element_type=jnp.float32,
    ).reshape(tok_rows, width)
    conv_low = (conv_grad_lru + conv_grad_gates).astype(jnp.bfloat16)
    head = from_behind(conv_low[:rim_rows], "seq", -1)
    trailing = jnp.concatenate([conv_low, head], axis=0)
    conv_low_float = conv_low.astype(jnp.float32)
    mixer_grad = jnp.zeros((tok_rows, width), jnp.float32)
    tap_grads = []
    for offset in range(kernel):
        later_ids = segment_layout(lengths_row, positions + offset)[0]
        ahead = jnp.where(
            (later_ids == segment_ids)[:, None],
            trailing[offset : offset + tok_rows].astype(jnp.float32),
            0.0,
        )
        mixer_grad = mixer_grad + ahead * conv_float[:, offset]
        tap_grads.append(jnp.sum(conv_low_float * lagged_terms[offset], axis=0))
    conv_weight_grad = jnp.stack(tap_grads, axis=1)
    conv_bias_grad = jnp.sum(conv_low_float, axis=0)
    proj_grad_low = jnp.concatenate([mixer_grad, branch_grad], axis=1).astype(jnp.bfloat16)
    in_proj_grad = contract_first(normed_low, proj_grad_low)
    normed_grad = contract_last(proj_grad_low, proj_all)
    input_part, gain_one_grad = norm_pull(normed_grad)
    token_grad = residual_grad + input_part
    summed = (
        lax.psum_scatter(gain_one_grad, ("bucket", "seq"), scatter_dimension=0, tiled=True),
        lax.psum_scatter(in_proj_grad, ("bucket", "seq"), scatter_dimension=0, tiled=True),
        lax.psum_scatter(conv_weight_grad, ("bucket", "seq"), scatter_dimension=0, tiled=True),
        lax.psum_scatter(conv_bias_grad, ("bucket", "seq"), scatter_dimension=0, tiled=True),
        lax.psum_scatter(gate_grad, ("bucket", "seq"), scatter_dimension=0, tiled=True),
        lax.psum_scatter(gate_bias_grad, ("bucket", "seq"), scatter_dimension=0, tiled=True),
        lax.psum_scatter(decay_grad, ("bucket", "seq"), scatter_dimension=0, tiled=True),
        lax.psum_scatter(out_grad, ("bucket", "seq"), scatter_dimension=0, tiled=True),
        lax.psum_scatter(gain_two_grad, ("bucket", "seq"), scatter_dimension=0, tiled=True),
    )
    return (
        mixed[None],
        token_grad[None],
        summed[0],
        summed[1],
        summed[2],
        summed[3],
        summed[4],
        summed[5],
        summed[6],
        summed[7],
        summed[8],
        gate_up_grad,
        down_grad,
    )


def swap_with(block, mask):
    route = [(i, i ^ mask) for i in range(lax.axis_size("seq"))]
    return lax.ppermute(block, "seq", route)


CORE, ACROSS_X, ACROSS_Y = 1, 2, 4


def split_row(rows):
    return rows // 32 * 16


def gather_chips(block, *others):
    split = split_row(block.shape[0])
    across_x, across_y = swap_with(block, ACROSS_X), swap_with(block, ACROSS_Y)
    if others:
        across_x, across_y, *others = lax.optimization_barrier((across_x, across_y, *others))
    both = [swap_with(across_y[:split], ACROSS_X), swap_with(across_x[split:], ACROSS_Y)]
    near = jnp.concatenate([block, across_x, across_y, *both]).reshape(4, *block.shape)
    return (near, *others) if others else near


def gather_chips_at_once(block):
    return jnp.stack(
        [block] + [swap_with(block, mask) for mask in (ACROSS_X, ACROSS_Y, ACROSS_X + ACROSS_Y)]
    )


def reduce_plane(near, far, late=None):
    other = swap_with(far, CORE)
    if late is not None:
        other, late = lax.optimization_barrier((other, late))
    rows = near.shape[1]
    split = split_row(rows)

    def total(place, span=slice(None)):
        return near[place, span].astype(jnp.float32) + other[place, span].astype(jnp.float32)

    both = total(3).astype(jnp.bfloat16)
    first = swap_with(both[:split], ACROSS_Y).astype(jnp.float32)
    second = swap_with(both[split:], ACROSS_X).astype(jnp.float32)
    across_x = jnp.concatenate([total(1, slice(split)) + first, total(1, slice(split, None))])
    across_y = jnp.concatenate([total(2, slice(split)), total(2, slice(split, None)) + second])
    across_x = swap_with(across_x.astype(jnp.bfloat16), ACROSS_X).astype(jnp.float32)
    across_y = swap_with(across_y.astype(jnp.bfloat16), ACROSS_Y).astype(jnp.float32)
    result = total(0) + across_x + across_y
    return result if late is None else (result, late)


def place_of(chunk, me, count):
    relative = jnp.bitwise_xor(chunk, me)
    return jnp.bitwise_and(relative, 1), jnp.right_shift(relative, 1)


def series_expm1(values):
    total = 1.0 + values * (1.0 / 7.0)
    for term in (6, 5, 4, 3, 2):
        total = 1.0 + values * (1.0 / term) * total
    return values * total


def segment_reach(info_ref, first, slots, shape, total):
    positions = first + lax.broadcasted_iota(jnp.int32, shape, 0)
    begin = jnp.zeros(shape, jnp.int32)
    finish = jnp.full(shape, total, jnp.int32)
    for slot in range(slots):
        end = info_ref[1 + slot]
        passed = positions >= end
        begin = jnp.where(passed, jnp.maximum(begin, end), begin)
        finish = jnp.where(passed, finish, jnp.minimum(finish, end))
    return positions - begin, finish - positions


def widen(mask, lanes):
    return jnp.concatenate([mask] * (lanes // mask.shape[1]), axis=1)


def gelu_parts(values):
    inner = 0.7978845608028654 * (values + 0.044715 * values * values * values)
    bent = jnp.tanh(inner)
    half = 0.5 * (1.0 + bent)
    slope = half + 0.5 * values * (1.0 - bent * bent) * 0.7978845608028654 * (
        1.0 + 3.0 * 0.044715 * values * values
    )
    return values * half, slope


ROWS = 8


def tiles_at_once(tiles):
    return max(size for size in range(1, GROUP + 1) if tiles % size == 0)


def group_tiles(index, group):
    return [index * group + member for member in range(group)]


GROUP = 11
TAP, BIAS, BIAS_A, BIAS_I, RATE = 0, 4, 5, 6, 7


def mixer_forward(
    taps,
    slots,
    info_ref,
    near_ref,
    far_ref,
    proj_ref,
    gate_ref,
    channel_ref,
    gated_ref,
    lagging_ref,
    conv_ref,
    branch_ref,
    gate_r_ref,
    gate_i_ref,
    hidden_ref,
    lag_edge_ref,
    hidden_edge_ref,
    proj_wide,
    projected,
    convolved,
    gates,
    carry,
    edge,
):
    chunk = pl.program_id(0)
    is_far, _ = place_of(chunk, info_ref[0], pl.num_programs(0))
    rows, lanes = convolved.shape
    tiles = rows // ROWS
    group = tiles_at_once(tiles)
    total = rows * pl.num_programs(0)

    @pl.when(chunk == 0)
    def _():
        carry[...] = jnp.zeros_like(carry)
        edge[...] = jnp.zeros_like(edge)
        channels = proj_ref.shape[1] // 2
        proj_wide[...] = jnp.zeros_like(proj_wide)
        proj_wide[:, :channels] = proj_ref[:, :channels]
        proj_wide[:, lanes : lanes + channels] = proj_ref[:, channels:]

    def project(normed_ref):
        product = jnp.dot(normed_ref[0], proj_wide[...], preferred_element_type=jnp.float32)
        low = product[:, :lanes].astype(jnp.bfloat16)
        lagging_ref[0] = low
        projected[:, :lanes] = low.astype(jnp.float32)
        branch_ref[0] = product[:, lanes:]

    pl.when(is_far == 0)(lambda: project(near_ref))
    pl.when(is_far == 1)(lambda: project(far_ref))
    place = lax.broadcasted_iota(jnp.int32, (ROWS, lanes), 0)

    def convolve(tile, before):
        for tile in group_tiles(tile, group):
            before = convolve_tile(tile, before)
        return before

    def convolve_tile(tile, before):
        at = pl.ds(pl.multiple_of(tile * ROWS, ROWS), ROWS)
        here = projected[at, :lanes]
        since, _ = segment_reach(info_ref, chunk * rows + tile * ROWS, slots, (ROWS, 128), total)
        value = channel_ref[BIAS : BIAS + 1, :] + here * channel_ref[TAP : TAP + 1, :]
        for lag in range(1, taps):
            moved = jnp.where(
                place < lag, pltpu.roll(before, lag, 0), pltpu.roll(here, lag, 0)
            )
            value = value + jnp.where(widen(since >= lag, lanes), moved, 0.0) * (
                channel_ref[TAP + lag : TAP + lag + 1, :]
            )
        convolved[at, :] = value
        return here

    last = lax.fori_loop(0, tiles // group, convolve, edge[...])
    edge[...] = last
    lag_edge_ref[0] = last
    conv_low = convolved[...].astype(jnp.bfloat16)
    conv_ref[0] = conv_low
    convolved[...] = conv_low.astype(jnp.float32)
    gates[...] = jnp.dot(conv_low, gate_ref[...], preferred_element_type=jnp.float32)

    def recur(tile, state):
        parts = [local_scan(tile) for tile in group_tiles(tile, group)]
        for at, value, decay in parts:
            hidden = value + decay * state
            state = jnp.broadcast_to(hidden[ROWS - 1 :], hidden.shape)
            hidden_ref[0, at, :] = hidden
            projected[at, :lanes] = hidden * projected[at, :lanes]
        hidden_edge_ref[0] = hidden
        return state

    def local_scan(tile):
        at = pl.ds(pl.multiple_of(tile * ROWS, ROWS), ROWS)
        since, _ = segment_reach(info_ref, chunk * rows + tile * ROWS, slots, (ROWS, 128), total)
        starts = widen(since == 0, lanes)
        gate_r = jax.nn.sigmoid(gates[at, :lanes] + channel_ref[BIAS_A : BIAS_A + 1, :])
        gate_i = jax.nn.sigmoid(gates[at, lanes:] + channel_ref[BIAS_I : BIAS_I + 1, :])
        gate_r_ref[0, at, :] = gate_r
        gate_i_ref[0, at, :] = gate_i
        less = series_expm1(-gate_scale * gate_r * channel_ref[RATE : RATE + 1, :])
        decay = jnp.where(starts, 0.0, 1.0 + less)
        scaling = jnp.where(starts, 1.0, jnp.sqrt(-less * (2.0 + less)))
        value = convolved[at, :] * gate_i * scaling
        for step in (1, 2, 4):
            inside = place >= step
            value = value + jnp.where(inside, decay * pltpu.roll(value, step, 0), 0.0)
            decay = jnp.where(inside, decay * pltpu.roll(decay, step, 0), decay)
        projected[at, :lanes] = gelu_parts(branch_ref[0, at, :])[0]
        return at, value, decay

    carry[...] = lax.fori_loop(0, tiles // group, recur, carry[...])
    gated_ref[0] = projected[:, :lanes].astype(jnp.bfloat16)


def mixer_backward(
    taps,
    slots,
    info_ref,
    near_ref,
    far_ref,
    out_ref,
    gate_ref,
    channel_ref,
    branch_ref,
    hidden_ref,
    gate_r_ref,
    gate_i_ref,
    conv_ref,
    lagging_ref,
    lag_edge_ref,
    hidden_edge_ref,
    projected_ref,
    gate_grad_ref,
    channel_grad_ref,
    coming,
    conv_part,
    lagged,
    gates,
    projected,
    conv_grad,
    grad_carry,
    decay_carry,
    sums,
):
    lap = pl.program_id(0)
    laps = pl.num_programs(0)
    chunk = laps - 1 - lap
    is_far, _ = place_of(chunk, info_ref[0], laps)
    rows, lanes = conv_part.shape
    tiles = rows // ROWS
    group = tiles_at_once(tiles)
    total = rows * laps

    @pl.when(lap == 0)
    def _():
        grad_carry[...] = jnp.zeros_like(grad_carry)
        decay_carry[...] = jnp.zeros_like(decay_carry)
        conv_grad[...] = jnp.zeros_like(conv_grad)
        sums[...] = jnp.zeros_like(sums)
        gate_grad_ref[...] = jnp.zeros_like(gate_grad_ref)

    def expand(down_ref):
        coming[...] = lax.dot_general(
            down_ref[0], out_ref[...], (((1,), (1,)), ((), ())), preferred_element_type=jnp.float32
        )

    pl.when(is_far == 0)(lambda: expand(near_ref))
    pl.when(is_far == 1)(lambda: expand(far_ref))
    lagged[...] = lagging_ref[0].astype(jnp.float32)
    conv_part[...] = conv_ref[0].astype(jnp.float32)
    place = lax.broadcasted_iota(jnp.int32, (ROWS, lanes), 0)
    first_chunk = chunk == 0

    def recur(step_index, carried):
        later_grad, later_decay, sum_a, sum_i, sum_rate = carried
        members = group_tiles(tiles // group - 1 - step_index, group)[::-1]
        parts = []
        for tile in members:
            part = local_scan(tile, later_decay)
            later_decay = part[-1]
            parts.append(part)
        for tile, (at, value, weight, _) in zip(members, parts):
            grad = value + weight * later_grad
            later_grad = jnp.broadcast_to(grad[:1], grad.shape)
            grad_a, grad_i, grad_rate = gate_grads(tile, at, grad)
            sum_a = sum_a + grad_a
            sum_i = sum_i + grad_i
            sum_rate = sum_rate - gate_scale * grad_rate
        return later_grad, later_decay, sum_a, sum_i, sum_rate

    def local_scan(tile, later_decay):
        at = pl.ds(pl.multiple_of(tile * ROWS, ROWS), ROWS)
        since, _ = segment_reach(info_ref, chunk * rows + tile * ROWS, slots, (ROWS, 128), total)
        starts = widen(since == 0, lanes)
        plain = 1.0 + series_expm1(-gate_scale * gate_r_ref[0, at, :] * channel_ref[RATE : RATE + 1, :])
        decay = jnp.where(starts, 0.0, plain)
        activated, slope = gelu_parts(branch_ref[0, at, :])
        down = coming[at, :]
        value = down * activated
        projected[at, lanes:] = down * hidden_ref[0, at, :] * slope
        weight = jnp.where(place == ROWS - 1, later_decay, pltpu.roll(decay, ROWS - 1, 0))
        for step in (1, 2, 4):
            inside = place < ROWS - step
            value = value + jnp.where(inside, weight * pltpu.roll(value, ROWS - step, 0), 0.0)
            weight = jnp.where(inside, weight * pltpu.roll(weight, ROWS - step, 0), weight)
        return at, value, weight, jnp.broadcast_to(decay[:1], decay.shape)

    def gate_grads(tile, at, grad):
        ahead = pl.ds(pl.multiple_of(jnp.maximum(tile - 1, 0) * ROWS, ROWS), ROWS)
        since, _ = segment_reach(info_ref, chunk * rows + tile * ROWS, slots, (ROWS, 128), total)
        starts = widen(since == 0, lanes)
        gate_r = gate_r_ref[0, at, :]
        gate_i = gate_i_ref[0, at, :]
        conv = conv_part[at, :]
        rate = channel_ref[RATE : RATE + 1, :]
        less = series_expm1(-gate_scale * gate_r * rate)
        plain = 1.0 + less
        root = jnp.sqrt(-less * (2.0 + less))
        earlier = jnp.where(
            tile == 0,
            jnp.where(first_chunk, 0.0, hidden_edge_ref[0]),
            hidden_ref[0, ahead, :],
        )
        before = jnp.where(
            place == 0, pltpu.roll(earlier, 1, 0), pltpu.roll(hidden_ref[0, at, :], 1, 0)
        )
        scaled = grad * jnp.where(starts, 1.0, root)
        conv_part[at, :] = scaled * gate_i
        grad_i = scaled * conv * gate_i * (1.0 - gate_i)
        grad_log = jnp.where(
            starts, 0.0, grad * plain * (before - conv * gate_i * plain / root)
        )
        grad_rate = grad_log * gate_r
        grad_a = -gate_scale * rate * grad_rate * (1.0 - gate_r)
        grad_a = grad_a.astype(jnp.bfloat16).astype(jnp.float32)
        grad_i = grad_i.astype(jnp.bfloat16).astype(jnp.float32)
        gates[at, :lanes] = grad_a
        gates[at, lanes:] = grad_i
        return grad_a, grad_i, grad_rate

    empty = jnp.zeros((ROWS, lanes), jnp.float32)
    grad_last, decay_last, sum_a, sum_i, sum_rate = lax.fori_loop(
        0, tiles // group, recur, (grad_carry[...], decay_carry[...], empty, empty, empty)
    )
    grad_carry[...] = grad_last
    decay_carry[...] = decay_last
    gates_low = gates[...].astype(jnp.bfloat16)
    gate_grad_ref[...] += lax.dot_general(
        conv_ref[0], gates_low, (((0,), (0,)), ((), ())), preferred_element_type=jnp.float32
    )
    from_gates = lax.dot_general(
        gates_low, gate_ref[...], (((1,), (1,)), ((), ())), preferred_element_type=jnp.float32
    )
    conv_grad[rows:, :] = conv_grad[:ROWS, :]
    conv_grad[:rows, :] = (conv_part[...] + from_gates).astype(jnp.bfloat16).astype(jnp.float32)

    def unconvolve(tile, carried):
        for tile in group_tiles(tile, group):
            carried = unconvolve_tile(tile, carried)
        return carried

    def unconvolve_tile(tile, carried):
        earlier, sum_bias, sum_taps = carried
        at = pl.ds(pl.multiple_of(tile * ROWS, ROWS), ROWS)
        beyond = pl.ds(pl.multiple_of((tile + 1) * ROWS, ROWS), ROWS)
        since, until = segment_reach(
            info_ref, chunk * rows + tile * ROWS, slots, (ROWS, 128), total
        )
        here = lagged[at, :]
        grad = conv_grad[at, :]
        later = conv_grad[beyond, :]
        value = grad * channel_ref[TAP : TAP + 1, :]
        new_taps = [sum_taps[0] + grad * here]
        for lag in range(1, taps):
            ahead = jnp.where(
                place < ROWS - lag, pltpu.roll(grad, ROWS - lag, 0), pltpu.roll(later, ROWS - lag, 0)
            )
            value = value + jnp.where(widen(until > lag, lanes), ahead, 0.0) * (
                channel_ref[TAP + lag : TAP + lag + 1, :]
            )
            moved = jnp.where(
                place < lag, pltpu.roll(earlier, lag, 0), pltpu.roll(here, lag, 0)
            )
            new_taps.append(
                sum_taps[lag] + grad * jnp.where(widen(since >= lag, lanes), moved, 0.0)
            )
        projected[at, :lanes] = value
        return here, sum_bias + grad, tuple(new_taps)

    _, sum_bias, sum_taps = lax.fori_loop(
        0, tiles // group, unconvolve, (lag_edge_ref[0], empty, (empty,) * taps)
    )
    low = projected[...].astype(jnp.bfloat16)
    channels = projected_ref.shape[2] // 2
    projected_ref[0, :, :channels] = low[:, :channels]
    projected_ref[0, :, channels:] = low[:, lanes : lanes + channels]
    for place_in, part in enumerate((*sum_taps, sum_bias, sum_a, sum_i, sum_rate)):
        sums[place_in] += part

    @pl.when(lap == laps - 1)
    def _():
        channel_grad_ref[...] = jnp.sum(sums[...], axis=1)


VMEM_LIMIT = 48 * 1024 * 1024


def run_forward(info, near, far, proj, gate, channels, taps, slots):
    chips, rows, depth = near.shape
    count = 2 * chips
    lanes = gate.shape[0]

    def at_chip(chunk, info_ref):
        return (place_of(chunk, info_ref[0], count)[1], 0, 0)

    def at_place(chunk, info_ref):
        is_far, chip = place_of(chunk, info_ref[0], count)
        return (is_far * chips + chip, 0, 0)

    def at_chunk(chunk, info_ref):
        return (chunk, 0, 0)

    def whole(chunk, info_ref):
        return (0, 0)

    def block(kind):
        return jax.ShapeDtypeStruct((count, rows, lanes), kind)

    wide = pl.BlockSpec((1, rows, depth), at_chip)
    narrow = pl.BlockSpec((1, rows, lanes), at_place)
    return pl.pallas_call(
        partial(mixer_forward, taps, slots),
        grid_spec=pltpu.PrefetchScalarGridSpec(
            num_scalar_prefetch=1,
            grid=(count,),
            in_specs=[
                wide,
                wide,
                pl.BlockSpec(proj.shape, whole),
                pl.BlockSpec(gate.shape, whole),
                pl.BlockSpec(channels.shape, whole),
            ],
            out_specs=[narrow] * 7
            + [pl.BlockSpec((1, ROWS, lanes), at_chunk)] * 2,
            scratch_shapes=[
                pltpu.VMEM((depth, 2 * lanes), jnp.bfloat16),
                pltpu.VMEM((rows, lanes), jnp.float32),
                pltpu.VMEM((rows, lanes), jnp.float32),
                pltpu.VMEM((rows, 2 * lanes), jnp.float32),
                pltpu.VMEM((ROWS, lanes), jnp.float32),
                pltpu.VMEM((ROWS, lanes), jnp.float32),
            ],
        ),
        out_shape=[
            block(jnp.bfloat16),
            block(jnp.bfloat16),
            block(jnp.bfloat16),
            block(jnp.float32),
            block(jnp.float32),
            block(jnp.float32),
            block(jnp.float32),
        ]
        + [jax.ShapeDtypeStruct((count, ROWS, lanes), jnp.float32)] * 2,
        compiler_params=pltpu.CompilerParams(
            dimension_semantics=("arbitrary",), vmem_limit_bytes=VMEM_LIMIT
        ),
        cost_estimate=pl.CostEstimate(flops=0, bytes_accessed=0, transcendentals=0),
        name="mixer_forward",
    )(info, near, far, proj, gate, channels)


def run_backward(info, near, far, out, gate, channels, saved, proj_columns, taps, slots):
    lagging, conv, branch, gate_r, gate_i, hidden, lag_edge, hidden_edge = saved
    chips, rows, depth = near.shape
    count = 2 * chips
    lanes = gate.shape[0]

    def at_chip(lap, info_ref):
        return (place_of(count - 1 - lap, info_ref[0], count)[1], 0, 0)

    def at_place(lap, info_ref):
        is_far, chip = place_of(count - 1 - lap, info_ref[0], count)
        return (is_far * chips + chip, 0, 0)

    def before(lap, info_ref):
        return (jnp.maximum(count - 2 - lap, 0), 0, 0)

    def whole(lap, info_ref):
        return (0, 0)

    wide = pl.BlockSpec((1, rows, depth), at_chip)
    narrow = pl.BlockSpec((1, rows, lanes), at_place)
    rim = pl.BlockSpec((1, ROWS, lanes), before)
    sums = taps + 4
    return pl.pallas_call(
        partial(mixer_backward, taps, slots),
        grid_spec=pltpu.PrefetchScalarGridSpec(
            num_scalar_prefetch=1,
            grid=(count,),
            in_specs=[
                wide,
                wide,
                pl.BlockSpec(out.shape, whole),
                pl.BlockSpec(gate.shape, whole),
                pl.BlockSpec(channels.shape, whole),
            ]
            + [narrow] * 6
            + [rim] * 2,
            out_specs=[
                pl.BlockSpec((1, rows, proj_columns), at_place),
                pl.BlockSpec((lanes, 2 * lanes), whole),
                pl.BlockSpec((sums, lanes), whole),
            ],
            scratch_shapes=[
                pltpu.VMEM((rows, lanes), jnp.float32),
                pltpu.VMEM((rows, lanes), jnp.float32),
                pltpu.VMEM((rows, lanes), jnp.float32),
                pltpu.VMEM((rows, 2 * lanes), jnp.float32),
                pltpu.VMEM((rows, 2 * lanes), jnp.float32),
                pltpu.VMEM((rows + ROWS, lanes), jnp.float32),
                pltpu.VMEM((ROWS, lanes), jnp.float32),
                pltpu.VMEM((ROWS, lanes), jnp.float32),
                pltpu.VMEM((sums, ROWS, lanes), jnp.float32),
            ],
        ),
        out_shape=[
            jax.ShapeDtypeStruct((count, rows, proj_columns), jnp.bfloat16),
            jax.ShapeDtypeStruct((lanes, 2 * lanes), jnp.float32),
            jax.ShapeDtypeStruct((sums, lanes), jnp.float32),
        ],
        compiler_params=pltpu.CompilerParams(
            dimension_semantics=("arbitrary",), vmem_limit_bytes=VMEM_LIMIT
        ),
        cost_estimate=pl.CostEstimate(flops=0, bytes_accessed=0, transcendentals=0),
        name="mixer_backward",
    )(
        info, near, far, out, gate, channels,
        branch, hidden, gate_r, gate_i, conv, lagging, lag_edge, hidden_edge,
    )


def deal_columns(moves, whole_ref, groups_ref):
    for group, inside, column, width in moves:
        groups_ref[group, :, inside : inside + width] = whole_ref[:, column : column + width]


def collect_columns(moves, groups_ref, weight_ref, whole_ref, lean_ref):
    for group, inside, column, width in moves:
        whole_ref[:, column : column + width] = groups_ref[
            group, :, inside : inside + width
        ].astype(jnp.float32)
    lean = jnp.zeros((weight_ref.shape[0], 128), jnp.float32)
    for column in range(0, weight_ref.shape[1], 128):
        span = slice(column, column + 128)
        lean = lean + whole_ref[:, span] * weight_ref[:, span].astype(jnp.float32)
    lean_ref[...] = jnp.sum(lean, axis=1, keepdims=True)


def hand_out(weight, moves):
    count = lax.axis_size("seq")
    rows, columns = weight.shape
    groups = pl.pallas_call(
        partial(deal_columns, moves),
        out_shape=jax.ShapeDtypeStruct((count, rows, columns // count), weight.dtype),
        compiler_params=pltpu.CompilerParams(vmem_limit_bytes=VMEM_LIMIT),
        name="deal_columns",
    )(weight)
    dealt = lax.all_to_all(groups, "seq", split_axis=0, concat_axis=0, tiled=True)
    return dealt.reshape(-1, columns // count)


def sum_planes(grad):
    return lax.psum_scatter(
        grad.astype(jnp.bfloat16), "bucket", scatter_dimension=0, tiled=True
    )


def hand_back(summed, weight, gain, moves):
    count = lax.axis_size("seq")
    rows, columns = weight.shape
    blocks = lax.all_to_all(
        summed.reshape(count, rows, columns // count), "seq", split_axis=0, concat_axis=0, tiled=True
    )
    whole, lean = pl.pallas_call(
        partial(collect_columns, moves),
        out_shape=[
            jax.ShapeDtypeStruct((rows, columns), jnp.float32),
            jax.ShapeDtypeStruct((rows, 1), jnp.float32),
        ],
        compiler_params=pltpu.CompilerParams(vmem_limit_bytes=VMEM_LIMIT),
        name="collect_columns",
    )(blocks, weight)
    return whole, lean[:, 0] / gain.astype(jnp.float32)


FOLD = 512


def fold_columns(values):
    return jnp.concatenate(
        [values[:, column : column + FOLD] for column in range(0, values.shape[1], FOLD)]
    )


def unfold_columns(folded, *shapes):
    wholes, row = [], 0
    for rows, columns in shapes:
        pieces = []
        for _ in range(0, columns, FOLD):
            pieces.append(folded[:, row : row + rows].reshape(-1, FOLD))
            row += rows
        wholes.append(jnp.concatenate(pieces, axis=1))
    return wholes


def pad_lanes(values, lanes):
    return jnp.pad(values, [(0, 0)] * (values.ndim - 1) + [(0, lanes - values.shape[-1])])


def contract_halves(left_near, left_far, right_near, right_far, kind=jnp.bfloat16):
    parts = [
        contract_first(left.reshape(-1, left.shape[-1]), right.reshape(-1, right.shape[-1]))
        for left, right in ((left_near, right_near), (left_far, right_far))
    ]
    return (parts[0] + parts[1]).astype(kind)


def by_channels(
    tokens,
    lengths,
    norm_gain,
    in_proj,
    conv_weight,
    conv_bias,
    gate_weight,
    gate_bias,
    decay,
    out_proj,
    mlp_gain,
    gate_up,
    down_proj,
    cotangent,
):
    planes = lax.axis_size("bucket")
    count = lax.axis_size("seq")
    me = lax.axis_index("seq")
    odd = jnp.bitwise_and(me, 1)
    inputs = tokens[0].astype(jnp.float32)
    rows, depth = inputs.shape
    own_rows = in_proj.shape[0]
    width = in_proj.shape[1] // 2
    block_width = width // NB
    held = planes // 2
    channels = held * block_width
    lanes = -(-channels // 128) * 128
    chunk_rows = conv_weight.shape[0]
    hidden_width = gate_up.shape[1] // 2 // count
    hidden_rows = down_proj.shape[0]
    taps = conv_weight.shape[1]
    slots = lengths.shape[1]

    by_row = jnp.concatenate(
        [out_proj, gate_weight, conv_weight, conv_bias[:, None], gate_bias, decay[:, None]], axis=1
    )
    by_row_width = by_row.shape[1]
    gains = jnp.pad(
        jnp.stack([norm_gain, mlp_gain], axis=1), [(0, chunk_rows - own_rows), (0, 0)]
    )
    by_row = jnp.concatenate([by_row, gains], axis=1)
    by_row = pad_lanes(by_row, -(-(by_row_width + 2) // 128) * 128)
    by_row, in_proj = lax.optimization_barrier((by_row, in_proj))
    by_row = lax.all_gather(by_row, "bucket", axis=0, tiled=False)
    proj_moves = [
        (
            2 * pair + side,
            (half * held + index) * block_width,
            half * width + ((side * held + index) * (count // 2) + pair) * block_width,
            block_width,
        )
        for pair in range(count // 2)
        for side in range(2)
        for half in range(2)
        for index in range(held)
    ]
    wide_moves = [
        (
            member,
            (half * planes + plane) * hidden_rows,
            half * planes * count * hidden_rows + (plane * count + member) * hidden_rows,
            hidden_rows,
        )
        for member in range(count)
        for half in range(2)
        for plane in range(planes)
    ]
    tokens_near = gather_chips(tokens[0])
    tokens_far = swap_with(tokens_near, CORE)
    proj_dealt = hand_out(in_proj, proj_moves)
    gains = by_row[:, :own_rows, by_row_width : by_row_width + 2]
    gains = lax.all_gather(gains.transpose(2, 0, 1), "seq", axis=2).astype(jnp.float32)
    gain_one, gain_two = gains.reshape(2, 1, depth)
    gate_up_late, proj_dealt = lax.optimization_barrier((gate_up, proj_dealt))
    wide_dealt = hand_out(gate_up_late, wide_moves)
    proj = lax.all_gather(proj_dealt, "bucket", axis=0, tiled=True)

    ends = jnp.cumsum(lengths[0]).astype(jnp.int32)
    info = jnp.concatenate([me[None].astype(jnp.int32), ends])

    positions = me * rows + jnp.arange(rows, dtype=jnp.int32)
    keep = (positions < ends[-1]).astype(jnp.float32)[:, None]
    upstream = keep * cotangent[0].astype(jnp.float32)
    scale_one = lax.rsqrt(jnp.mean(inputs * inputs, axis=1, keepdims=True) + norm_eps)
    kept = lax.dynamic_slice_in_dim(by_row, odd * held, held, 0)
    given = lax.dynamic_slice_in_dim(by_row, (1 - odd) * held, held, 0)
    taken = swap_with(given, 1)
    pair = jnp.where(
        odd == 0, jnp.stack([kept, taken], axis=1), jnp.stack([taken, kept], axis=1)
    )
    by_channel = pair.reshape(channels, -1)
    out = jnp.pad(by_channel[:, :depth], [(0, lanes - channels), (0, 0)])
    gate_columns = 2 * block_width
    gate_rows = by_channel[:, depth : depth + gate_columns]
    gate_blocks = []
    for index in range(held):
        part = gate_rows[index * block_width : (index + 1) * block_width]
        at = index * block_width
        gate_blocks.append(
            jnp.concatenate(
                [
                    jnp.pad(side, [(0, 0), (at, lanes - at - block_width)])
                    for side in (part[:, :block_width], part[:, block_width:])
                ],
                axis=1,
            )
        )
    gate = jnp.pad(jnp.concatenate(gate_blocks, axis=0), [(0, lanes - channels), (0, 0)])
    small = by_channel[:, depth + gate_columns : by_row_width].astype(jnp.float32).T
    decay_channel = small[taps + 3]
    rate = jnp.pad(jax.nn.softplus(decay_channel), (0, lanes - channels), constant_values=0.01)
    channel = jnp.concatenate([pad_lanes(small[: taps + 3], lanes), rate[None]], axis=0)

    def normalize(low):
        values = low.astype(jnp.float32)
        scale = lax.rsqrt(jnp.mean(values * values, axis=2, keepdims=True) + norm_eps)
        return (values * scale * gain_one).astype(jnp.bfloat16)

    upstream_low, wide_dealt = lax.optimization_barrier(
        (upstream.astype(jnp.bfloat16), wide_dealt)
    )
    upstream_near = gather_chips(upstream_low)
    upstream_far = swap_with(upstream_near, CORE)
    normed_near, normed_far = normalize(tokens_near), normalize(tokens_far)
    normed_near, normed_far, upstream_near = lax.optimization_barrier(
        (normed_near, normed_far, upstream_near)
    )
    feed_weights = lax.all_gather(
        jnp.concatenate([fold_columns(wide_dealt), fold_columns(down_proj)]), "bucket", axis=0
    )
    gated, *saved = run_forward(
        info, normed_near, normed_far, proj, gate, channel, taps, slots
    )
    mixed_far, mixed_near = (
        jnp.dot(part.reshape(-1, lanes), out, preferred_element_type=jnp.float32)
        .astype(jnp.bfloat16)
        .reshape(-1, rows, depth)
        for part in (gated[count // 2 :], gated[: count // 2])
    )
    residual = inputs + reduce_plane(mixed_near, mixed_far)
    scale_two = lax.rsqrt(jnp.mean(residual * residual, axis=1, keepdims=True) + norm_eps)
    normed_two = (residual * scale_two * gain_two).astype(jnp.bfloat16)
    two_near = gather_chips(normed_two)
    two_far = swap_with(two_near, CORE)
    wide, narrow = unfold_columns(feed_weights, wide_dealt.shape, down_proj.shape)
    halves = []
    for part in (two_near, two_far):
        expanded = jnp.dot(
            part.reshape(-1, depth), wide, preferred_element_type=jnp.float32
        )
        halves.append((expanded, gated_gelu(expanded, hidden_width).astype(jnp.bfloat16)))
    (expanded_near, feed_near), (expanded_far, feed_far) = halves

    feed_grads = [
        contract_last(part.reshape(-1, depth), narrow) for part in (upstream_near, upstream_far)
    ]
    down_part = contract_halves(feed_near, feed_far, upstream_near, upstream_far)
    down_grad = sum_planes(down_part).astype(jnp.float32)
    expanded_near, expanded_far, down_part = lax.optimization_barrier(
        (expanded_near, expanded_far, down_part)
    )

    def through_feed(expanded, feed_grad):
        _, feed_pull = jax.vjp(partial(gated_gelu, split=hidden_width), expanded)
        expanded_grad = feed_pull(feed_grad)[0].astype(jnp.bfloat16)
        part = contract_last(expanded_grad, wide).astype(jnp.bfloat16)
        return expanded_grad, part.reshape(-1, rows, depth)

    grad_far, part_far = through_feed(expanded_far, feed_grads[1])
    grad_near, part_near = through_feed(expanded_near, feed_grads[0])
    part_near, two_near, two_far, feed_near, feed_far = lax.optimization_barrier(
        (part_near, two_near, two_far, feed_near, feed_far)
    )
    normed_two_grad = reduce_plane(part_near, part_far)

    def norm_back(values, scale, gain, grad):
        scaled = grad * gain
        lean = jnp.mean(scaled * values, axis=1, keepdims=True)
        return scale * scaled - scale * scale * scale * lean * values

    residual_grad = upstream + norm_back(residual, scale_two, gain_two, normed_two_grad)
    wide_part = contract_halves(two_near, two_far, grad_near, grad_far)
    residual_grad, wide_part = lax.optimization_barrier((residual_grad, wide_part))
    wide_summed = sum_planes(wide_part)
    low_near = gather_chips(residual_grad.astype(jnp.bfloat16))
    low_near, down_grad = lax.optimization_barrier((low_near, down_grad))
    low_far = swap_with(low_near, CORE)
    output_parts = [
        jnp.dot(part, narrow, preferred_element_type=jnp.float32)
        .astype(jnp.bfloat16)
        .reshape(-1, rows, depth)
        for part in (feed_near, feed_far)
    ]
    output_near, output_far = output_parts
    output_far, low_near = lax.optimization_barrier((output_far, low_near))
    mixed = (keep * (residual + reduce_plane(output_near, output_far))).astype(jnp.bfloat16)

    proj_grad, gate_grad, channel_grad = run_backward(
        info, low_near, low_far, out, gate, channel, saved, 2 * channels, taps, slots
    )
    proj_grad, wide_summed = lax.optimization_barrier((proj_grad, wide_summed))
    proj_grad_near, proj_grad_far = proj_grad[: count // 2], proj_grad[count // 2 :]

    def through_proj(part):
        part = contract_last(part.reshape(-1, 2 * channels), proj).astype(jnp.bfloat16)
        return part.reshape(-1, rows, depth)

    proj_part = contract_halves(normed_near, normed_far, proj_grad_near, proj_grad_far)
    proj_grad_far, proj_grad_near, proj_part = lax.optimization_barrier(
        (proj_grad_far, proj_grad_near, proj_part)
    )
    part_far = through_proj(proj_grad_far)
    part_far, mixed = lax.optimization_barrier((part_far, mixed))
    normed_grad = reduce_plane(through_proj(proj_grad_near), part_far)

    out_grad = contract_halves(
        gated[: count // 2], gated[count // 2 :], low_near, low_far, jnp.float32
    )[:channels]
    gate_parts = []
    for index in range(held):
        at = index * block_width
        span = gate_grad[at : at + block_width]
        gate_parts.append(
            jnp.concatenate(
                [span[:, at : at + block_width], span[:, lanes + at : lanes + at + block_width]],
                axis=1,
            )
        )
    channel_grad = channel_grad[:, :channels]
    small_grad = jnp.concatenate(
        [
            channel_grad[: taps + 3],
            (channel_grad[taps + 3] * jax.nn.sigmoid(decay_channel))[None],
        ],
        axis=0,
    )
    by_row_grad = jnp.concatenate(
        [out_grad, jnp.concatenate(gate_parts, axis=0), small_grad.T], axis=1
    ).astype(jnp.bfloat16)
    by_row_grad = pad_lanes(by_row_grad, by_row.shape[2]).reshape(held, 2, chunk_rows, -1)
    kept = lax.dynamic_index_in_dim(by_row_grad, odd, 1, False)
    taken = swap_with(lax.dynamic_index_in_dim(by_row_grad, 1 - odd, 1, False), 1)
    by_row_grad = jnp.where(
        odd == 0, jnp.concatenate([kept, taken]), jnp.concatenate([taken, kept])
    ).reshape(planes * chunk_rows, -1)
    proj_part, wide_summed = lax.optimization_barrier((proj_part, wide_summed))
    proj_summed = sum_planes(proj_part)
    wide_summed, normed_grad = lax.optimization_barrier((wide_summed, normed_grad))
    token_grad = residual_grad + norm_back(inputs, scale_one, gain_one, normed_grad)
    gate_up_grad, mlp_gain_grad = hand_back(wide_summed, gate_up, mlp_gain, wide_moves)
    proj_summed, by_row_grad = lax.optimization_barrier((proj_summed, by_row_grad))
    in_proj_grad, norm_gain_grad = hand_back(proj_summed, in_proj, norm_gain, proj_moves)
    by_row_grad = sum_planes(by_row_grad).astype(jnp.float32)
    out_proj_grad = by_row_grad[:, :depth]
    gate_weight_grad = by_row_grad[:, depth : depth + gate_columns]
    small_grad = by_row_grad[:, depth + gate_columns : by_row_width]
    return (
        mixed[None],
        token_grad[None],
        norm_gain_grad,
        in_proj_grad,
        small_grad[:, :taps],
        small_grad[:, taps],
        gate_weight_grad,
        small_grad[:, taps + 1 : taps + 3],
        small_grad[:, taps + 3],
        out_proj_grad,
        mlp_gain_grad,
        gate_up_grad,
        down_grad,
    )


def solution(mesh):
    planes, count = mesh.shape["bucket"], mesh.shape["seq"]
    whole_blocks = count == 8 and planes % 2 == 0 and planes * count == 2 * NB
    return jax.shard_map(
        by_channels if whole_blocks else on_device,
        mesh=mesh,
        in_specs=(
            P("bucket", "seq", None),
            P("bucket", None),
            P(("bucket", "seq")),
            P(("bucket", "seq"), None),
            P(("bucket", "seq"), None),
            P(("bucket", "seq")),
            P(("bucket", "seq"), None),
            P(("bucket", "seq"), None),
            P(("bucket", "seq")),
            P(("bucket", "seq"), None),
            P(("bucket", "seq")),
            P(("bucket", "seq"), None),
            P(("bucket", "seq"), None),
            P("bucket", "seq", None),
        ),
        out_specs=(
            P("bucket", "seq", None),
            P("bucket", "seq", None),
            P(("bucket", "seq")),
            P(("bucket", "seq"), None),
            P(("bucket", "seq"), None),
            P(("bucket", "seq")),
            P(("bucket", "seq"), None),
            P(("bucket", "seq"), None),
            P(("bucket", "seq")),
            P(("bucket", "seq"), None),
            P(("bucket", "seq")),
            P(("bucket", "seq"), None),
            P(("bucket", "seq"), None),
        ),
        check_vma=False,
    )
```

```python
from functools import partial

import jax
import jax.numpy as jnp
from jax import lax
from jax.experimental import pallas as pl
from jax.experimental.pallas import tpu as pltpu
from jax.sharding import PartitionSpec as P

NB = 16


norm_eps = 1e-06
gate_scale = 8.0


def from_behind(block, axis, distance):
    devices = range(lax.axis_size(axis))
    route = [(i - distance, i) for i in devices if i - distance in devices]
    return lax.ppermute(block, axis, route)


def entering(part, axis, combine, identity, reverse):
    count = lax.axis_size(axis)
    place = lax.axis_index(axis)
    ahead = count - 1 - place if reverse else place
    gathered = jax.tree.map(lambda a: lax.all_gather(a, axis), part)
    state = jax.tree.map(lambda a, e: jnp.zeros_like(a) + jnp.asarray(e, a.dtype), part, identity)

    def one(lap, state):
        source = count - 1 - lap if reverse else lap
        return combine(
            state, jax.tree.map(lambda a: lax.dynamic_index_in_dim(a, source, 0, False), gathered)
        )

    return lax.fori_loop(0, ahead, one, state)


def rms_scale(values, gain):
    return values * lax.rsqrt(jnp.mean(values * values, axis=1, keepdims=True) + norm_eps) * gain


def link(earlier, later):
    return (earlier[0] * later[0], later[0] * earlier[1] + later[1])


def segment_layout(lengths_row, positions):
    ends = jnp.cumsum(lengths_row)
    segment_ids = jnp.sum((positions[:, None] >= ends[None, :]).astype(jnp.int32), axis=1)
    segment_ids = jnp.where(positions < 0, -1, segment_ids)
    keep = (positions < ends[-1]).astype(jnp.float32)
    return (segment_ids, keep)


def lru_terms(conv_out, gate_a, gate_i, decay, starts):
    rate = jax.nn.softplus(decay)
    log_step = -gate_scale * jax.nn.sigmoid(gate_a) * rate
    decay_step = jnp.where(starts, 0.0, jnp.exp(log_step))
    scaling = jnp.where(starts, 1.0, jnp.sqrt(-jnp.expm1(2.0 * log_step)))
    return (decay_step, conv_out * jax.nn.sigmoid(gate_i) * scaling)


def gated_gelu(values, split):
    return jax.nn.gelu(values[:, :split]) * values[:, split:]


def contract_last(left, right):
    return lax.dot_general(
        left, right, (((1,), (1,)), ((), ())), preferred_element_type=jnp.float32
    )


def contract_first(left, right):
    return lax.dot_general(
        left, right, (((0,), (0,)), ((), ())), preferred_element_type=jnp.float32
    )


def row_product(left, right):
    return contract_first(left, right)


def on_device(
    tokens,
    lengths,
    norm_gain,
    in_proj,
    conv_weight,
    conv_bias,
    gate_weight,
    gate_bias,
    decay,
    out_proj,
    mlp_gain,
    gate_up,
    down_proj,
    cotangent,
):
    inputs = tokens[0].astype(jnp.float32)
    tok_rows = inputs.shape[0]
    width = in_proj.shape[1] // 2
    ff_width = gate_up.shape[1] // 2
    block_width = width // NB
    kernel = conv_weight.shape[1]
    rim_rows = kernel - 1
    (
        gain_one_all,
        proj_all,
        conv_all,
        conv_bias_all,
        gate_all,
        gate_bias_all,
        decay_all,
        out_all,
        gain_two_all,
    ) = (
        lax.all_gather(norm_gain, ("bucket", "seq"), axis=0, tiled=True),
        lax.all_gather(in_proj, ("bucket", "seq"), axis=0, tiled=True),
        lax.all_gather(conv_weight, ("bucket", "seq"), axis=0, tiled=True),
        lax.all_gather(conv_bias, ("bucket", "seq"), axis=0, tiled=True),
        lax.all_gather(gate_weight, ("bucket", "seq"), axis=0, tiled=True),
        lax.all_gather(gate_bias, ("bucket", "seq"), axis=0, tiled=True),
        lax.all_gather(decay, ("bucket", "seq"), axis=0, tiled=True),
        lax.all_gather(out_proj, ("bucket", "seq"), axis=0, tiled=True),
        lax.all_gather(mlp_gain, ("bucket", "seq"), axis=0, tiled=True),
    )
    seq_index = lax.axis_index("seq")
    positions = seq_index * tok_rows + jnp.arange(tok_rows, dtype=jnp.int32)
    lengths_row = lengths[0]
    segment_ids, keep = segment_layout(lengths_row, positions)
    back_ids = segment_layout(lengths_row, positions - 1)[0]
    starts = (segment_ids != back_ids)[:, None]
    normed, norm_pull = jax.vjp(rms_scale, inputs, gain_one_all.astype(jnp.float32))
    normed_low = normed.astype(jnp.bfloat16)
    projected = jnp.dot(normed_low, proj_all, preferred_element_type=jnp.float32)
    mixer_in = projected[:, :width].astype(jnp.bfloat16)
    branch = projected[:, width:]
    rim = from_behind(mixer_in[tok_rows - rim_rows :], "seq", 1)
    extended = jnp.concatenate([rim, mixer_in], axis=0)
    conv_float = conv_all.astype(jnp.float32)
    lagged_terms = []
    convolved = jnp.zeros((tok_rows, width), jnp.float32) + conv_bias_all.astype(jnp.float32)
    for offset in range(kernel):
        earlier_ids = segment_layout(lengths_row, positions - offset)[0]
        lagged = jnp.where(
            (earlier_ids == segment_ids)[:, None],
            extended[rim_rows - offset : rim_rows - offset + tok_rows].astype(jnp.float32),
            0.0,
        )
        lagged_terms.append(lagged)
        convolved = convolved + lagged * conv_float[:, offset]
    conv_out = convolved.astype(jnp.bfloat16)
    gates = jnp.einsum(
        "tnc,ncd->tnd",
        conv_out.reshape(tok_rows, NB, block_width),
        gate_all.reshape(NB, block_width, 2 * block_width),
        preferred_element_type=jnp.float32,
    )
    gate_bias_float = gate_bias_all.astype(jnp.float32)
    gate_a = gates[:, :, :block_width].reshape(tok_rows, width) + gate_bias_float[:, 0]
    gate_i = gates[:, :, block_width:].reshape(tok_rows, width) + gate_bias_float[:, 1]
    (decay_step, normalized), lru_pull = jax.vjp(
        partial(lru_terms, starts=starts),
        conv_out.astype(jnp.float32),
        gate_a,
        gate_i,
        decay_all.astype(jnp.float32),
    )
    prefix_decay, prefix_state = lax.associative_scan(link, (decay_step, normalized), axis=0)
    carried = entering(
        (prefix_decay[-1], prefix_state[-1]),
        "seq",
        link,
        (jnp.ones((width,), jnp.float32), jnp.zeros((width,), jnp.float32)),
        False,
    )
    state_in = carried[1]
    hidden = prefix_state + prefix_decay * state_in
    branch_act, branch_pull = jax.vjp(jax.nn.gelu, branch)
    gated = (hidden * branch_act).astype(jnp.bfloat16)
    residual = inputs + jnp.dot(gated, out_all, preferred_element_type=jnp.float32)
    normed_two, norm_two_pull = jax.vjp(rms_scale, residual, gain_two_all.astype(jnp.float32))
    normed_two_low = normed_two.astype(jnp.bfloat16)
    gate_up_all, down_all = (
        lax.all_gather(gate_up, ("bucket", "seq"), axis=0, tiled=True),
        lax.all_gather(down_proj, ("bucket", "seq"), axis=0, tiled=True),
    )
    expanded = jnp.dot(normed_two_low, gate_up_all, preferred_element_type=jnp.float32)
    feed, feed_pull = jax.vjp(partial(gated_gelu, split=ff_width), expanded)
    feed_low = feed.astype(jnp.bfloat16)
    output_rows = residual + jnp.dot(feed_low, down_all, preferred_element_type=jnp.float32)
    mixed = (keep[:, None] * output_rows).astype(jnp.bfloat16)
    upstream = keep[:, None] * cotangent[0].astype(jnp.float32)
    upstream_low = upstream.astype(jnp.bfloat16)
    down_grad = lax.psum_scatter(
        row_product(feed_low, upstream_low), ("bucket", "seq"), scatter_dimension=0, tiled=True
    )
    feed_grad = contract_last(upstream_low, down_all)
    expanded_grad = feed_pull(feed_grad)[0].astype(jnp.bfloat16)
    gate_up_grad = lax.psum_scatter(
        row_product(normed_two_low, expanded_grad),
        ("bucket", "seq"),
        scatter_dimension=0,
        tiled=True,
    )
    normed_two_grad = contract_last(expanded_grad, gate_up_all)
    residual_part, gain_two_grad = norm_two_pull(normed_two_grad)
    residual_grad = upstream + residual_part
    residual_low = residual_grad.astype(jnp.bfloat16)
    out_grad = contract_first(gated, residual_low)
    gated_grad = contract_last(residual_low, out_all)
    hidden_grad = gated_grad * branch_act
    branch_grad = branch_pull(gated_grad * hidden)[0]
    next_decay = jnp.concatenate([decay_step[1:], jnp.ones((1, width), jnp.float32)], axis=0)
    suffix_decay, suffix_state = lax.associative_scan(
        link, (next_decay, hidden_grad), reverse=True, axis=0
    )
    returned = entering(
        (prefix_decay[-1], decay_step[0] * suffix_state[0]),
        "seq",
        link,
        (jnp.ones((width,), jnp.float32), jnp.zeros((width,), jnp.float32)),
        True,
    )
    incoming = returned[1]
    state_grad = suffix_state + suffix_decay * incoming
    state_before = jnp.concatenate([state_in[None, :], hidden[:-1]], axis=0)
    conv_grad_lru, gate_a_grad, gate_i_grad, decay_grad = lru_pull(
        (state_grad * state_before, state_grad)
    )
    gates_low = jnp.concatenate(
        [
            gate_a_grad.reshape(tok_rows, NB, block_width),
            gate_i_grad.reshape(tok_rows, NB, block_width),
        ],
        axis=2,
    ).astype(jnp.bfloat16)
    gate_grad = jnp.einsum(
        "tnc,tnd->ncd",
        conv_out.reshape(tok_rows, NB, block_width),
        gates_low,
        preferred_element_type=jnp.float32,
    ).reshape(width, 2 * block_width)
    bias_sums = jnp.sum(gates_low.astype(jnp.float32), axis=0)
    gate_bias_grad = jnp.stack(
        [bias_sums[:, :block_width].reshape(width), bias_sums[:, block_width:].reshape(width)],
        axis=1,
    )
    conv_grad_gates = jnp.einsum(
        "tnd,ncd->tnc",
        gates_low,
        gate_all.reshape(NB, block_width, 2 * block_width),
        preferred_element_type=jnp.float32,
    ).reshape(tok_rows, width)
    conv_low = (conv_grad_lru + conv_grad_gates).astype(jnp.bfloat16)
    head = from_behind(conv_low[:rim_rows], "seq", -1)
    trailing = jnp.concatenate([conv_low, head], axis=0)
    conv_low_float = conv_low.astype(jnp.float32)
    mixer_grad = jnp.zeros((tok_rows, width), jnp.float32)
    tap_grads = []
    for offset in range(kernel):
        later_ids = segment_layout(lengths_row, positions + offset)[0]
        ahead = jnp.where(
            (later_ids == segment_ids)[:, None],
            trailing[offset : offset + tok_rows].astype(jnp.float32),
            0.0,
        )
        mixer_grad = mixer_grad + ahead * conv_float[:, offset]
        tap_grads.append(jnp.sum(conv_low_float * lagged_terms[offset], axis=0))
    conv_weight_grad = jnp.stack(tap_grads, axis=1)
    conv_bias_grad = jnp.sum(conv_low_float, axis=0)
    proj_grad_low = jnp.concatenate([mixer_grad, branch_grad], axis=1).astype(jnp.bfloat16)
    in_proj_grad = contract_first(normed_low, proj_grad_low)
    normed_grad = contract_last(proj_grad_low, proj_all)
    input_part, gain_one_grad = norm_pull(normed_grad)
    token_grad = residual_grad + input_part
    summed = (
        lax.psum_scatter(gain_one_grad, ("bucket", "seq"), scatter_dimension=0, tiled=True),
        lax.psum_scatter(in_proj_grad, ("bucket", "seq"), scatter_dimension=0, tiled=True),
        lax.psum_scatter(conv_weight_grad, ("bucket", "seq"), scatter_dimension=0, tiled=True),
        lax.psum_scatter(conv_bias_grad, ("bucket", "seq"), scatter_dimension=0, tiled=True),
        lax.psum_scatter(gate_grad, ("bucket", "seq"), scatter_dimension=0, tiled=True),
        lax.psum_scatter(gate_bias_grad, ("bucket", "seq"), scatter_dimension=0, tiled=True),
        lax.psum_scatter(decay_grad, ("bucket", "seq"), scatter_dimension=0, tiled=True),
        lax.psum_scatter(out_grad, ("bucket", "seq"), scatter_dimension=0, tiled=True),
        lax.psum_scatter(gain_two_grad, ("bucket", "seq"), scatter_dimension=0, tiled=True),
    )
    return (
        mixed[None],
        token_grad[None],
        summed[0],
        summed[1],
        summed[2],
        summed[3],
        summed[4],
        summed[5],
        summed[6],
        summed[7],
        summed[8],
        gate_up_grad,
        down_grad,
    )


def swap_with(block, mask):
    route = [(i, i ^ mask) for i in range(lax.axis_size("seq"))]
    return lax.ppermute(block, "seq", route)


CORE, ACROSS_X, ACROSS_Y = 1, 2, 4


def split_row(rows):
    return rows // 32 * 16


def gather_chips(block, *others):
    split = split_row(block.shape[0])
    across_x, across_y = swap_with(block, ACROSS_X), swap_with(block, ACROSS_Y)
    if others:
        across_x, across_y, *others = lax.optimization_barrier((across_x, across_y, *others))
    both = [swap_with(across_y[:split], ACROSS_X), swap_with(across_x[split:], ACROSS_Y)]
    near = jnp.concatenate([block, across_x, across_y, *both]).reshape(4, *block.shape)
    return (near, *others) if others else near


def send_to_chips(across_x, across_y, across_both):
    return [
        swap_with(across_x, ACROSS_X),
        swap_with(across_y, ACROSS_Y),
        swap_with(across_both, ACROSS_X + ACROSS_Y),
    ]


def reduce_plane(near, far, *others, late=()):
    other = swap_with(far, CORE)
    rows = near.shape[1]
    split = split_row(rows)

    def total(place, span=slice(None)):
        return near[place, span].astype(jnp.float32) + other[place, span].astype(jnp.float32)

    both = total(3).astype(jnp.bfloat16)
    both, *others = lax.optimization_barrier((both, *others))
    first = swap_with(both[:split], ACROSS_Y).astype(jnp.float32)
    second = swap_with(both[split:], ACROSS_X).astype(jnp.float32)
    across_x = jnp.concatenate([total(1, slice(split)) + first, total(1, slice(split, None))])
    across_y = jnp.concatenate([total(2, slice(split)), total(2, slice(split, None)) + second])
    across_x, across_y = across_x.astype(jnp.bfloat16), across_y.astype(jnp.bfloat16)
    across_x, across_y, *late = lax.optimization_barrier((across_x, across_y, *late))
    others += late
    across_x = swap_with(across_x, ACROSS_X).astype(jnp.float32)
    across_y = swap_with(across_y, ACROSS_Y).astype(jnp.float32)
    result = total(0) + across_x + across_y
    return (result, *others) if others else result


def reduce_plane_at_once(near, far, *others):
    other = swap_with(far, CORE)

    def total(place):
        return near[place].astype(jnp.float32) + other[place].astype(jnp.float32)

    *parts, others = lax.optimization_barrier(
        (*(total(place).astype(jnp.bfloat16) for place in (1, 2, 3)), others)
    )
    sent = send_to_chips(*parts)

    def finish(*late):
        *parts, late = lax.optimization_barrier((*sent, late))
        result = total(0)
        for part in parts:
            result = result + part.astype(jnp.float32)
        return (result, *late) if late else result

    return (finish, *others)


def place_of(chunk, me, count):
    relative = jnp.bitwise_xor(chunk, me)
    return jnp.bitwise_and(relative, 1), jnp.right_shift(relative, 1)


def series_expm1(values):
    total = 1.0 + values * (1.0 / 7.0)
    for term in (6, 5, 4, 3, 2):
        total = 1.0 + values * (1.0 / term) * total
    return values * total


def segment_reach(info_ref, first, slots, shape, total):
    positions = first + lax.broadcasted_iota(jnp.int32, shape, 0)
    begin = jnp.zeros(shape, jnp.int32)
    finish = jnp.full(shape, total, jnp.int32)
    for slot in range(slots):
        end = info_ref[1 + slot]
        passed = positions >= end
        begin = jnp.where(passed, jnp.maximum(begin, end), begin)
        finish = jnp.where(passed, finish, jnp.minimum(finish, end))
    return positions - begin, finish - positions


def widen(mask, lanes):
    return jnp.concatenate([mask] * (lanes // mask.shape[1]), axis=1)


def gelu_parts(values):
    inner = 0.7978845608028654 * (values + 0.044715 * values * values * values)
    bent = jnp.tanh(inner)
    half = 0.5 * (1.0 + bent)
    slope = half + 0.5 * values * (1.0 - bent * bent) * 0.7978845608028654 * (
        1.0 + 3.0 * 0.044715 * values * values
    )
    return values * half, slope


ROWS = 8


def tiles_at_once(tiles):
    return max(size for size in range(1, GROUP + 1) if tiles % size == 0)


def group_tiles(index, group):
    return [index * group + member for member in range(group)]


GROUP = 11
TAP, BIAS, BIAS_A, BIAS_I, RATE = 0, 4, 5, 6, 7


def mixer_forward(
    taps,
    slots,
    info_ref,
    near_ref,
    far_ref,
    proj_ref,
    gate_ref,
    channel_ref,
    gated_ref,
    lagging_ref,
    conv_ref,
    act_ref,
    slope_ref,
    decay_ref,
    rate_part_ref,
    gate_i_part_ref,
    conv_part_ref,
    gate_r_ref,
    lag_edge_ref,
    proj_wide,
    projected,
    convolved,
    gates,
    carry,
    edge,
):
    chunk = pl.program_id(0)
    is_far, _ = place_of(chunk, info_ref[0], pl.num_programs(0))
    rows, lanes = convolved.shape
    tiles = rows // ROWS
    group = tiles_at_once(tiles)
    total = rows * pl.num_programs(0)

    @pl.when(chunk == 0)
    def _():
        carry[...] = jnp.zeros_like(carry)
        edge[...] = jnp.zeros_like(edge)
        channels = proj_ref.shape[1] // 2
        proj_wide[...] = jnp.zeros_like(proj_wide)
        proj_wide[:, :channels] = proj_ref[:, :channels]
        proj_wide[:, lanes : lanes + channels] = proj_ref[:, channels:]

    def project(normed_ref):
        product = jnp.dot(normed_ref[0], proj_wide[...], preferred_element_type=jnp.float32)
        low = product[:, :lanes].astype(jnp.bfloat16)
        lagging_ref[0] = low
        projected[:, :lanes] = low.astype(jnp.float32)
        projected[:, lanes:] = product[:, lanes:]

    pl.when(is_far == 0)(lambda: project(near_ref))
    pl.when(is_far == 1)(lambda: project(far_ref))
    place = lax.broadcasted_iota(jnp.int32, (ROWS, lanes), 0)

    def convolve(tile, before):
        for tile in group_tiles(tile, group):
            before = convolve_tile(tile, before)
        return before

    def convolve_tile(tile, before):
        at = pl.ds(pl.multiple_of(tile * ROWS, ROWS), ROWS)
        here = projected[at, :lanes]
        since, _ = segment_reach(info_ref, chunk * rows + tile * ROWS, slots, (ROWS, 128), total)
        value = channel_ref[BIAS : BIAS + 1, :] + here * channel_ref[TAP : TAP + 1, :]
        for lag in range(1, taps):
            moved = jnp.where(
                place < lag, pltpu.roll(before, lag, 0), pltpu.roll(here, lag, 0)
            )
            value = value + jnp.where(widen(since >= lag, lanes), moved, 0.0) * (
                channel_ref[TAP + lag : TAP + lag + 1, :]
            )
        convolved[at, :] = value
        return here

    last = lax.fori_loop(0, tiles // group, convolve, edge[...])
    edge[...] = last
    lag_edge_ref[0] = last
    conv_low = convolved[...].astype(jnp.bfloat16)
    conv_ref[0] = conv_low
    convolved[...] = conv_low.astype(jnp.float32)
    gates[...] = jnp.dot(conv_low, gate_ref[...], preferred_element_type=jnp.float32)

    def recur(tile, state):
        parts = [local_scan(tile) for tile in group_tiles(tile, group)]
        for at, value, decay, activated, slope, ratio, gate in parts:
            hidden = value + decay * state
            before = jnp.where(place == 0, state, pltpu.roll(hidden, 1, 0))
            state = jnp.broadcast_to(hidden[ROWS - 1 :], hidden.shape)
            projected[at, :lanes] = hidden * activated
            slope_ref[0, at, :] = hidden * slope
            rate_part_ref[0, at, :] = gate * (before - ratio)
        return state

    def local_scan(tile):
        at = pl.ds(pl.multiple_of(tile * ROWS, ROWS), ROWS)
        since, _ = segment_reach(info_ref, chunk * rows + tile * ROWS, slots, (ROWS, 128), total)
        starts = widen(since == 0, lanes)
        gate_r = jax.nn.sigmoid(gates[at, :lanes] + channel_ref[BIAS_A : BIAS_A + 1, :])
        gate_i = jax.nn.sigmoid(gates[at, lanes:] + channel_ref[BIAS_I : BIAS_I + 1, :])
        less = series_expm1(-gate_scale * gate_r * channel_ref[RATE : RATE + 1, :])
        plain = 1.0 + less
        root = jnp.sqrt(-less * (2.0 + less))
        decay = jnp.where(starts, 0.0, plain)
        scaling = jnp.where(starts, 1.0, root)
        conv = convolved[at, :]
        admitted = conv * gate_i
        value = admitted * scaling
        decay_ref[0, at, :] = decay
        conv_part_ref[0, at, :] = gate_i * scaling
        gate_i_part_ref[0, at, :] = value * (1.0 - gate_i)
        gate_r_ref[0, at, :] = 1.0 - gate_r
        ratio = admitted * plain / root
        gate = decay * gate_r
        for step in (1, 2, 4):
            inside = place >= step
            value = value + jnp.where(inside, decay * pltpu.roll(value, step, 0), 0.0)
            decay = jnp.where(inside, decay * pltpu.roll(decay, step, 0), decay)
        activated, slope = gelu_parts(projected[at, lanes:])
        act_ref[0, at, :] = activated
        return at, value, decay, activated, slope, ratio, gate

    carry[...] = lax.fori_loop(0, tiles // group, recur, carry[...])
    gated_ref[0] = projected[:, :lanes].astype(jnp.bfloat16)


def mixer_backward(
    taps,
    slots,
    info_ref,
    near_ref,
    far_ref,
    out_ref,
    gate_ref,
    channel_ref,
    act_ref,
    slope_ref,
    decay_ref,
    rate_part_ref,
    gate_i_part_ref,
    conv_part_ref,
    gate_r_ref,
    conv_ref,
    lagging_ref,
    lag_edge_ref,
    projected_ref,
    gate_grad_ref,
    channel_grad_ref,
    coming,
    conv_part,
    lagged,
    gates,
    projected,
    conv_grad,
    grad_carry,
    decay_carry,
    sums,
):
    lap = pl.program_id(0)
    laps = pl.num_programs(0)
    chunk = laps - 1 - lap
    is_far, _ = place_of(chunk, info_ref[0], laps)
    rows, lanes = conv_part.shape
    tiles = rows // ROWS
    group = tiles_at_once(tiles)
    total = rows * laps

    @pl.when(lap == 0)
    def _():
        grad_carry[...] = jnp.zeros_like(grad_carry)
        decay_carry[...] = jnp.zeros_like(decay_carry)
        conv_grad[...] = jnp.zeros_like(conv_grad)
        sums[...] = jnp.zeros_like(sums)
        gate_grad_ref[...] = jnp.zeros_like(gate_grad_ref)

    def expand(down_ref):
        coming[...] = lax.dot_general(
            down_ref[0], out_ref[...], (((1,), (1,)), ((), ())), preferred_element_type=jnp.float32
        )

    pl.when(is_far == 0)(lambda: expand(near_ref))
    pl.when(is_far == 1)(lambda: expand(far_ref))
    lagged[...] = lagging_ref[0].astype(jnp.float32)
    place = lax.broadcasted_iota(jnp.int32, (ROWS, lanes), 0)

    def recur(step_index, carried):
        later_grad, later_decay, sum_a, sum_i, sum_rate = carried
        members = group_tiles(tiles // group - 1 - step_index, group)[::-1]
        parts = []
        for tile in members:
            part = local_scan(tile, later_decay)
            later_decay = part[-1]
            parts.append(part)
        for at, value, weight, _ in parts:
            grad = value + weight * later_grad
            later_grad = jnp.broadcast_to(grad[:1], grad.shape)
            conv_part[at, :] = grad * conv_part_ref[0, at, :]
            grad_i = grad * gate_i_part_ref[0, at, :]
            grad_rate = grad * rate_part_ref[0, at, :]
            grad_a = (-gate_scale * channel_ref[RATE : RATE + 1, :]) * grad_rate * gate_r_ref[0, at, :]
            grad_a = grad_a.astype(jnp.bfloat16).astype(jnp.float32)
            grad_i = grad_i.astype(jnp.bfloat16).astype(jnp.float32)
            gates[at, :lanes] = grad_a
            gates[at, lanes:] = grad_i
            sum_a = sum_a + grad_a
            sum_i = sum_i + grad_i
            sum_rate = sum_rate - gate_scale * grad_rate
        return later_grad, later_decay, sum_a, sum_i, sum_rate

    def local_scan(tile, later_decay):
        at = pl.ds(pl.multiple_of(tile * ROWS, ROWS), ROWS)
        decay = decay_ref[0, at, :]
        down = coming[at, :]
        value = down * act_ref[0, at, :]
        projected[at, lanes:] = down * slope_ref[0, at, :]
        weight = jnp.where(place == ROWS - 1, later_decay, pltpu.roll(decay, ROWS - 1, 0))
        for step in (1, 2, 4):
            inside = place < ROWS - step
            value = value + jnp.where(inside, weight * pltpu.roll(value, ROWS - step, 0), 0.0)
            weight = jnp.where(inside, weight * pltpu.roll(weight, ROWS - step, 0), weight)
        return at, value, weight, jnp.broadcast_to(decay[:1], decay.shape)

    empty = jnp.zeros((ROWS, lanes), jnp.float32)
    grad_last, decay_last, sum_a, sum_i, sum_rate = lax.fori_loop(
        0, tiles // group, recur, (grad_carry[...], decay_carry[...], empty, empty, empty)
    )
    grad_carry[...] = grad_last
    decay_carry[...] = decay_last
    gates_low = gates[...].astype(jnp.bfloat16)
    gate_grad_ref[...] += lax.dot_general(
        conv_ref[0], gates_low, (((0,), (0,)), ((), ())), preferred_element_type=jnp.float32
    )
    from_gates = lax.dot_general(
        gates_low, gate_ref[...], (((1,), (1,)), ((), ())), preferred_element_type=jnp.float32
    )
    conv_grad[rows:, :] = conv_grad[:ROWS, :]
    conv_grad[:rows, :] = (conv_part[...] + from_gates).astype(jnp.bfloat16).astype(jnp.float32)

    def unconvolve(tile, carried):
        for tile in group_tiles(tile, group):
            carried = unconvolve_tile(tile, carried)
        return carried

    def unconvolve_tile(tile, carried):
        earlier, sum_bias, sum_taps = carried
        at = pl.ds(pl.multiple_of(tile * ROWS, ROWS), ROWS)
        beyond = pl.ds(pl.multiple_of((tile + 1) * ROWS, ROWS), ROWS)
        since, until = segment_reach(
            info_ref, chunk * rows + tile * ROWS, slots, (ROWS, 128), total
        )
        here = lagged[at, :]
        grad = conv_grad[at, :]
        later = conv_grad[beyond, :]
        value = grad * channel_ref[TAP : TAP + 1, :]
        new_taps = [sum_taps[0] + grad * here]
        for lag in range(1, taps):
            ahead = jnp.where(
                place < ROWS - lag, pltpu.roll(grad, ROWS - lag, 0), pltpu.roll(later, ROWS - lag, 0)
            )
            value = value + jnp.where(widen(until > lag, lanes), ahead, 0.0) * (
                channel_ref[TAP + lag : TAP + lag + 1, :]
            )
            moved = jnp.where(
                place < lag, pltpu.roll(earlier, lag, 0), pltpu.roll(here, lag, 0)
            )
            new_taps.append(
                sum_taps[lag] + grad * jnp.where(widen(since >= lag, lanes), moved, 0.0)
            )
        projected[at, :lanes] = value
        return here, sum_bias + grad, tuple(new_taps)

    _, sum_bias, sum_taps = lax.fori_loop(
        0, tiles // group, unconvolve, (lag_edge_ref[0], empty, (empty,) * taps)
    )
    low = projected[...].astype(jnp.bfloat16)
    channels = projected_ref.shape[2] // 2
    projected_ref[0, :, :channels] = low[:, :channels]
    projected_ref[0, :, channels:] = low[:, lanes : lanes + channels]
    for place_in, part in enumerate((*sum_taps, sum_bias, sum_a, sum_i, sum_rate)):
        sums[place_in] += part

    @pl.when(lap == laps - 1)
    def _():
        channel_grad_ref[...] = jnp.sum(sums[...], axis=1)


VMEM_LIMIT = 56 * 1024 * 1024


def run_forward(info, near, far, proj, gate, channels, taps, slots):
    chips, rows, depth = near.shape
    count = 2 * chips
    lanes = gate.shape[0]

    def at_chip(chunk, info_ref):
        return (place_of(chunk, info_ref[0], count)[1], 0, 0)

    def at_place(chunk, info_ref):
        is_far, chip = place_of(chunk, info_ref[0], count)
        return (is_far * chips + chip, 0, 0)

    def at_chunk(chunk, info_ref):
        return (chunk, 0, 0)

    def whole(chunk, info_ref):
        return (0, 0)

    def block(kind):
        return jax.ShapeDtypeStruct((count, rows, lanes), kind)

    wide = pl.BlockSpec((1, rows, depth), at_chip)
    narrow = pl.BlockSpec((1, rows, lanes), at_place)
    return pl.pallas_call(
        partial(mixer_forward, taps, slots),
        grid_spec=pltpu.PrefetchScalarGridSpec(
            num_scalar_prefetch=1,
            grid=(count,),
            in_specs=[
                wide,
                wide,
                pl.BlockSpec(proj.shape, whole),
                pl.BlockSpec(gate.shape, whole),
                pl.BlockSpec(channels.shape, whole),
            ],
            out_specs=[narrow] * 10 + [pl.BlockSpec((1, ROWS, lanes), at_chunk)],
            scratch_shapes=[
                pltpu.VMEM((depth, 2 * lanes), jnp.bfloat16),
                pltpu.VMEM((rows, 2 * lanes), jnp.float32),
                pltpu.VMEM((rows, lanes), jnp.float32),
                pltpu.VMEM((rows, 2 * lanes), jnp.float32),
                pltpu.VMEM((ROWS, lanes), jnp.float32),
                pltpu.VMEM((ROWS, lanes), jnp.float32),
            ],
        ),
        out_shape=[block(jnp.bfloat16)] * 3
        + [block(jnp.float32)] * 7
        + [jax.ShapeDtypeStruct((count, ROWS, lanes), jnp.float32)],
        compiler_params=pltpu.CompilerParams(
            dimension_semantics=("arbitrary",), vmem_limit_bytes=VMEM_LIMIT
        ),
        cost_estimate=pl.CostEstimate(flops=0, bytes_accessed=0, transcendentals=0),
        name="mixer_forward",
    )(info, near, far, proj, gate, channels)


def run_backward(info, near, far, out, gate, channels, saved, proj_columns, taps, slots):
    lagging, conv, *parts, lag_edge = saved
    chips, rows, depth = near.shape
    count = 2 * chips
    lanes = gate.shape[0]

    def at_chip(lap, info_ref):
        return (place_of(count - 1 - lap, info_ref[0], count)[1], 0, 0)

    def at_place(lap, info_ref):
        is_far, chip = place_of(count - 1 - lap, info_ref[0], count)
        return (is_far * chips + chip, 0, 0)

    def before(lap, info_ref):
        return (jnp.maximum(count - 2 - lap, 0), 0, 0)

    def whole(lap, info_ref):
        return (0, 0)

    wide = pl.BlockSpec((1, rows, depth), at_chip)
    narrow = pl.BlockSpec((1, rows, lanes), at_place)
    rim = pl.BlockSpec((1, ROWS, lanes), before)
    sums = taps + 4
    return pl.pallas_call(
        partial(mixer_backward, taps, slots),
        grid_spec=pltpu.PrefetchScalarGridSpec(
            num_scalar_prefetch=1,
            grid=(count,),
            in_specs=[
                wide,
                wide,
                pl.BlockSpec(out.shape, whole),
                pl.BlockSpec(gate.shape, whole),
                pl.BlockSpec(channels.shape, whole),
            ]
            + [narrow] * 9
            + [rim],
            out_specs=[
                pl.BlockSpec((1, rows, proj_columns), at_place),
                pl.BlockSpec((lanes, 2 * lanes), whole),
                pl.BlockSpec((sums, lanes), whole),
            ],
            scratch_shapes=[
                pltpu.VMEM((rows, lanes), jnp.float32),
                pltpu.VMEM((rows, lanes), jnp.float32),
                pltpu.VMEM((rows, lanes), jnp.float32),
                pltpu.VMEM((rows, 2 * lanes), jnp.float32),
                pltpu.VMEM((rows, 2 * lanes), jnp.float32),
                pltpu.VMEM((rows + ROWS, lanes), jnp.float32),
                pltpu.VMEM((ROWS, lanes), jnp.float32),
                pltpu.VMEM((ROWS, lanes), jnp.float32),
                pltpu.VMEM((sums, ROWS, lanes), jnp.float32),
            ],
        ),
        out_shape=[
            jax.ShapeDtypeStruct((count, rows, proj_columns), jnp.bfloat16),
            jax.ShapeDtypeStruct((lanes, 2 * lanes), jnp.float32),
            jax.ShapeDtypeStruct((sums, lanes), jnp.float32),
        ],
        compiler_params=pltpu.CompilerParams(
            dimension_semantics=("arbitrary",), vmem_limit_bytes=VMEM_LIMIT
        ),
        cost_estimate=pl.CostEstimate(flops=0, bytes_accessed=0, transcendentals=0),
        name="mixer_backward",
    )(info, near, far, out, gate, channels, *parts, conv, lagging, lag_edge)


def deal_columns(moves, whole_ref, groups_ref):
    for group, inside, column, width in moves:
        groups_ref[group, :, inside : inside + width] = whole_ref[:, column : column + width]


def collect_columns(moves, groups_ref, weight_ref, whole_ref, lean_ref):
    for group, inside, column, width in moves:
        whole_ref[:, column : column + width] = groups_ref[
            group, :, inside : inside + width
        ].astype(jnp.float32)
    lean = jnp.zeros((weight_ref.shape[0], 128), jnp.float32)
    for column in range(0, weight_ref.shape[1], 128):
        span = slice(column, column + 128)
        lean = lean + whole_ref[:, span] * weight_ref[:, span].astype(jnp.float32)
    lean_ref[...] = jnp.sum(lean, axis=1, keepdims=True)


def hand_out(weight, moves):
    count = lax.axis_size("seq")
    rows, columns = weight.shape
    groups = pl.pallas_call(
        partial(deal_columns, moves),
        out_shape=jax.ShapeDtypeStruct((count, rows, columns // count), weight.dtype),
        compiler_params=pltpu.CompilerParams(vmem_limit_bytes=VMEM_LIMIT),
        name="deal_columns",
    )(weight)
    dealt = lax.all_to_all(groups, "seq", split_axis=0, concat_axis=0, tiled=True)
    return dealt.reshape(-1, columns // count)


def sum_planes(grad):
    return lax.psum_scatter(
        grad.astype(jnp.bfloat16), "bucket", scatter_dimension=0, tiled=True
    )


def spread_rows(summed):
    count = lax.axis_size("seq")
    blocks = summed.reshape(count, -1, summed.shape[1])
    return lax.all_to_all(blocks, "seq", split_axis=0, concat_axis=0, tiled=True)


def hand_back(blocks, weight, gain, moves):
    rows, columns = weight.shape
    whole, lean = pl.pallas_call(
        partial(collect_columns, moves),
        out_shape=[
            jax.ShapeDtypeStruct((rows, columns), jnp.float32),
            jax.ShapeDtypeStruct((rows, 1), jnp.float32),
        ],
        compiler_params=pltpu.CompilerParams(vmem_limit_bytes=VMEM_LIMIT),
        name="collect_columns",
    )(blocks, weight)
    return whole, lean[:, 0] / gain.astype(jnp.float32)


FOLD = 512


def row_spans(rows):
    parts = max(count for count in (4, 3, 2, 1) if rows % (16 * count) == 0)
    return [slice(part * rows // parts, (part + 1) * rows // parts) for part in range(parts)]


def feed_forward(near_ref, far_ref, wide_ref, gate_part_ref, up_part_ref, feed_ref, normed_ref):
    half = FOLD // 2

    def expand(part_ref):
        for span in row_spans(part_ref.shape[0]):
            product = jnp.dot(
                part_ref[span, :], wide_ref[...], preferred_element_type=jnp.float32
            )
            activated, slope = gelu_parts(product[:, :half])
            up = product[:, half:]
            feed_ref[span, :] = (activated * up).astype(jnp.bfloat16)
            gate_part_ref[span, :] = slope * up
            up_part_ref[span, :] = activated

        @pl.when(pl.program_id(1) == 0)
        def _():
            normed_ref[...] = part_ref[...]

    pl.when(pl.program_id(0) == 0)(lambda: expand(near_ref))
    pl.when(pl.program_id(0) == 1)(lambda: expand(far_ref))


def run_feed_forward(near, far, wide):
    rows, depth = near.shape
    tiles = wide.shape[1] // FOLD
    half = FOLD // 2

    def whole(part, tile):
        return (0, 0)

    return pl.pallas_call(
        feed_forward,
        grid=(2, tiles),
        in_specs=[
            pl.BlockSpec((rows, depth), whole),
            pl.BlockSpec((rows, depth), whole),
            pl.BlockSpec((depth, FOLD), lambda part, tile: (0, tile)),
        ],
        out_specs=[pl.BlockSpec((rows, half), lambda part, tile: (part, tile))] * 3
        + [pl.BlockSpec((rows, depth), lambda part, tile: (part, 0))],
        out_shape=[
            jax.ShapeDtypeStruct((2 * rows, tiles * half), jnp.float32),
            jax.ShapeDtypeStruct((2 * rows, tiles * half), jnp.float32),
            jax.ShapeDtypeStruct((2 * rows, tiles * half), jnp.bfloat16),
            jax.ShapeDtypeStruct((2 * rows, depth), jnp.bfloat16),
        ],
        compiler_params=pltpu.CompilerParams(vmem_limit_bytes=VMEM_LIMIT),
        cost_estimate=pl.CostEstimate(
            flops=4 * rows * depth * tiles * FOLD, bytes_accessed=0, transcendentals=0
        ),
        name="feed_forward",
    )(near, far, wide)


def feed_backward(
    upstream_ref, planes_ref, gate_part_ref, up_part_ref, grad_ref, narrow_ref
):
    half = FOLD // 2
    planes = planes_ref.shape[0]
    tile_rows = half // planes
    tiles = planes_ref.shape[1] // tile_rows

    @pl.when(pl.program_id(0) == 0)
    def _():
        for tile in range(tiles):
            for plane in range(planes):
                target = (tile * planes + plane) * tile_rows
                narrow_ref[target : target + tile_rows, :] = planes_ref[
                    plane, tile * tile_rows : (tile + 1) * tile_rows, :
                ]

    feed_grad = lax.dot_general(
        upstream_ref[...],
        narrow_ref[...],
        (((1,), (1,)), ((), ())),
        preferred_element_type=jnp.float32,
    )
    for tile in range(tiles):
        span = slice(tile * half, (tile + 1) * half)
        part = feed_grad[:, span]
        grad_ref[:, tile * FOLD : tile * FOLD + half] = (part * gate_part_ref[:, span]).astype(
            jnp.bfloat16
        )
        grad_ref[:, tile * FOLD + half : (tile + 1) * FOLD] = (
            part * up_part_ref[:, span]
        ).astype(jnp.bfloat16)


def run_feed_backward(upstream, narrow, gate_part, up_part):
    rows, depth = upstream.shape
    planes, narrow_rows = narrow.shape[:2]
    width = gate_part.shape[1]
    steps = max(count for count in range(1, 7) if rows % (16 * count) == 0)
    block = rows // steps

    def at_step(step):
        return (step, 0)

    return pl.pallas_call(
        feed_backward,
        grid=(steps,),
        in_specs=[
            pl.BlockSpec((block, depth), at_step),
            pl.BlockSpec((planes, narrow_rows, depth), lambda step: (0, 0, 0)),
            pl.BlockSpec((block, width), at_step),
            pl.BlockSpec((block, width), at_step),
        ],
        out_specs=[
            pl.BlockSpec((block, 2 * width), at_step),
            pl.BlockSpec((width, depth), lambda step: (0, 0)),
        ],
        out_shape=[
            jax.ShapeDtypeStruct((rows, 2 * width), jnp.bfloat16),
            jax.ShapeDtypeStruct((width, depth), jnp.bfloat16),
        ],
        compiler_params=pltpu.CompilerParams(vmem_limit_bytes=VMEM_LIMIT),
        cost_estimate=pl.CostEstimate(
            flops=2 * rows * depth * width, bytes_accessed=0, transcendentals=0
        ),
        name="feed_backward",
    )(upstream, narrow, gate_part, up_part)


def pad_lanes(values, lanes):
    return jnp.pad(values, [(0, 0)] * (values.ndim - 1) + [(0, lanes - values.shape[-1])])


def contract_halves(left_near, left_far, right_near, right_far, kind=jnp.bfloat16):
    parts = [
        contract_first(left.reshape(-1, left.shape[-1]), right.reshape(-1, right.shape[-1]))
        for left, right in ((left_near, right_near), (left_far, right_far))
    ]
    return (parts[0] + parts[1]).astype(kind)


def by_channels(
    tokens,
    lengths,
    norm_gain,
    in_proj,
    conv_weight,
    conv_bias,
    gate_weight,
    gate_bias,
    decay,
    out_proj,
    mlp_gain,
    gate_up,
    down_proj,
    cotangent,
):
    planes = lax.axis_size("bucket")
    count = lax.axis_size("seq")
    me = lax.axis_index("seq")
    odd = jnp.bitwise_and(me, 1)
    inputs = tokens[0].astype(jnp.float32)
    rows, depth = inputs.shape
    own_rows = in_proj.shape[0]
    width = in_proj.shape[1] // 2
    block_width = width // NB
    held = planes // 2
    channels = held * block_width
    lanes = -(-channels // 128) * 128
    chunk_rows = conv_weight.shape[0]
    hidden_width = gate_up.shape[1] // 2 // count
    hidden_rows = down_proj.shape[0]
    taps = conv_weight.shape[1]
    slots = lengths.shape[1]

    by_row = jnp.concatenate(
        [out_proj, gate_weight, conv_weight, conv_bias[:, None], gate_bias, decay[:, None]], axis=1
    )
    by_row_width = by_row.shape[1]
    gains = jnp.pad(
        jnp.stack([norm_gain, mlp_gain], axis=1), [(0, chunk_rows - own_rows), (0, 0)]
    )
    by_row = jnp.concatenate([by_row, gains], axis=1)
    by_row = pad_lanes(by_row, -(-(by_row_width + 2) // 128) * 128)
    by_row, in_proj = lax.optimization_barrier((by_row, in_proj))
    by_row = lax.all_gather(by_row, "bucket", axis=0, tiled=False)
    proj_moves = [
        (
            2 * pair + side,
            (half * held + index) * block_width,
            half * width + ((side * held + index) * (count // 2) + pair) * block_width,
            block_width,
        )
        for pair in range(count // 2)
        for side in range(2)
        for half in range(2)
        for index in range(held)
    ]
    tile_rows = FOLD // 2 // planes
    tiles = hidden_rows // tile_rows
    wide_moves = [
        (
            member,
            ((tile * 2 + half) * planes + plane) * tile_rows,
            ((half * planes + plane) * count + member) * hidden_rows + tile * tile_rows,
            tile_rows,
        )
        for member in range(count)
        for tile in range(tiles)
        for half in range(2)
        for plane in range(planes)
    ]
    tokens_near, by_row = gather_chips(tokens[0], by_row)
    tokens_far = swap_with(tokens_near, CORE)
    proj_dealt = hand_out(in_proj, proj_moves)
    gains = by_row[:, :own_rows, by_row_width : by_row_width + 2]
    gains = lax.all_gather(gains.transpose(2, 0, 1), "seq", axis=2).astype(jnp.float32)
    gain_one, gain_two = gains.reshape(2, 1, depth)
    gate_up_late, proj_dealt = lax.optimization_barrier((gate_up, proj_dealt))
    wide_dealt = hand_out(gate_up_late, wide_moves)
    proj = lax.all_gather(proj_dealt, "bucket", axis=0, tiled=True)

    ends = jnp.cumsum(lengths[0]).astype(jnp.int32)
    info = jnp.concatenate([me[None].astype(jnp.int32), ends])

    positions = me * rows + jnp.arange(rows, dtype=jnp.int32)
    keep = (positions < ends[-1]).astype(jnp.float32)[:, None]
    upstream = keep * cotangent[0].astype(jnp.float32)
    scale_one = lax.rsqrt(jnp.mean(inputs * inputs, axis=1, keepdims=True) + norm_eps)
    kept = lax.dynamic_slice_in_dim(by_row, odd * held, held, 0)
    given = lax.dynamic_slice_in_dim(by_row, (1 - odd) * held, held, 0)
    taken = swap_with(given, 1)
    pair = jnp.where(
        odd == 0, jnp.stack([kept, taken], axis=1), jnp.stack([taken, kept], axis=1)
    )
    by_channel = pair.reshape(channels, -1)
    out = jnp.pad(by_channel[:, :depth], [(0, lanes - channels), (0, 0)])
    gate_columns = 2 * block_width
    gate_rows = by_channel[:, depth : depth + gate_columns]
    gate_blocks = []
    for index in range(held):
        part = gate_rows[index * block_width : (index + 1) * block_width]
        at = index * block_width
        gate_blocks.append(
            jnp.concatenate(
                [
                    jnp.pad(side, [(0, 0), (at, lanes - at - block_width)])
                    for side in (part[:, :block_width], part[:, block_width:])
                ],
                axis=1,
            )
        )
    gate = jnp.pad(jnp.concatenate(gate_blocks, axis=0), [(0, lanes - channels), (0, 0)])
    small = by_channel[:, depth + gate_columns : by_row_width].astype(jnp.float32).T
    decay_channel = small[taps + 3]
    rate = jnp.pad(jax.nn.softplus(decay_channel), (0, lanes - channels), constant_values=0.01)
    channel = jnp.concatenate([pad_lanes(small[: taps + 3], lanes), rate[None]], axis=0)

    def normalize(low):
        values = low.astype(jnp.float32)
        scale = lax.rsqrt(jnp.mean(values * values, axis=2, keepdims=True) + norm_eps)
        return (values * scale * gain_one).astype(jnp.bfloat16)

    wide_dealt, down_proj, gain_one = lax.optimization_barrier((wide_dealt, down_proj, gain_one))
    normed_near, normed_far = normalize(tokens_near), normalize(tokens_far)
    upstream_low, normed_near, normed_far = lax.optimization_barrier(
        (upstream.astype(jnp.bfloat16), normed_near, normed_far)
    )
    upstream_parts = send_to_chips(upstream_low, upstream_low, upstream_low)
    narrow = lax.all_gather(down_proj, "bucket", axis=0)
    wide = lax.all_gather(wide_dealt, "bucket", axis=0, tiled=True)
    gated, *saved = run_forward(
        info, normed_near, normed_far, proj, gate, channel, taps, slots
    )
    gated, *upstream_parts = lax.optimization_barrier((gated, *upstream_parts))
    upstream_near = jnp.stack([upstream_low, *upstream_parts])
    upstream_far = swap_with(upstream_near, CORE)
    gated_near, upstream_near = lax.optimization_barrier((gated[: count // 2], upstream_near))
    mixed_far, mixed_near = (
        jnp.dot(part.reshape(-1, lanes), out, preferred_element_type=jnp.float32)
        .astype(jnp.bfloat16)
        .reshape(-1, rows, depth)
        for part in (gated[count // 2 :], gated_near)
    )
    mixed, narrow = reduce_plane(mixed_near, mixed_far, late=(narrow,))
    residual = inputs + mixed
    scale_two = lax.rsqrt(jnp.mean(residual * residual, axis=1, keepdims=True) + norm_eps)
    normed_two = (residual * scale_two * gain_two).astype(jnp.bfloat16)
    two_near = gather_chips(normed_two)
    two_far = swap_with(two_near, CORE)
    upstream_all = jnp.concatenate([upstream_near, upstream_far]).reshape(-1, depth)
    two_far, upstream_all = lax.optimization_barrier((two_far, upstream_all))
    gate_part, up_part, feed, two_all = run_feed_forward(
        two_near.reshape(-1, depth), two_far.reshape(-1, depth), wide
    )
    half_rows = two_all.shape[0] // 2

    feed_grad, narrow = run_feed_backward(
        upstream_all,
        narrow,
        gate_part,
        up_part,
    )
    part_far = contract_last(feed_grad[half_rows:], wide).astype(jnp.bfloat16)
    part_near = contract_last(feed_grad[:half_rows], wide).astype(jnp.bfloat16)
    finish, two_all, feed, upstream_all = reduce_plane_at_once(
        part_near.reshape(-1, rows, depth),
        part_far.reshape(-1, rows, depth),
        two_all,
        feed,
        upstream_all,
    )
    normed_two_grad = finish()
    down_part = contract_first(feed, upstream_all).astype(jnp.bfloat16)
    down_part = (
        down_part.reshape(tiles, planes, tile_rows, depth)
        .transpose(1, 0, 2, 3)
        .reshape(hidden_width, depth)
    )
    down_grad = sum_planes(down_part).astype(jnp.float32)

    def norm_back(values, scale, gain, grad):
        scaled = grad * gain
        lean = jnp.mean(scaled * values, axis=1, keepdims=True)
        return scale * scaled - scale * scale * scale * lean * values

    residual_grad = upstream + norm_back(residual, scale_two, gain_two, normed_two_grad)
    wide_part = contract_first(two_all, feed_grad).astype(jnp.bfloat16)
    residual_grad, wide_part, down_part = lax.optimization_barrier(
        (residual_grad, wide_part, down_part)
    )
    wide_summed = sum_planes(wide_part)
    output_far, output_near = (
        jnp.dot(part, narrow, preferred_element_type=jnp.float32)
        .astype(jnp.bfloat16)
        .reshape(-1, rows, depth)
        for part in (feed[half_rows:], feed[:half_rows])
    )
    low_near, output_near, output_far, down_grad = gather_chips(
        residual_grad.astype(jnp.bfloat16), output_near, output_far, down_grad
    )
    output_sums = output_near.astype(jnp.float32) + swap_with(output_far, CORE).astype(jnp.float32)
    low_far = swap_with(low_near, CORE)
    low_far, *output_low = lax.optimization_barrier(
        (low_far, *(output_sums[place].astype(jnp.bfloat16) for place in (1, 2, 3)))
    )
    output_parts = send_to_chips(*output_low)
    proj_grad, gate_grad, channel_grad = run_backward(
        info, low_near, low_far, out, gate, channel, saved, 2 * channels, taps, slots
    )
    proj_grad_near, proj_grad_far = proj_grad[: count // 2], proj_grad[count // 2 :]

    def through_proj(part):
        part = contract_last(part.reshape(-1, 2 * channels), proj).astype(jnp.bfloat16)
        return part.reshape(-1, rows, depth)

    proj_part = contract_halves(normed_near, normed_far, proj_grad_near, proj_grad_far)
    proj_grad_far, proj_grad_near, proj_part, wide_summed, *output_parts = (
        lax.optimization_barrier(
            (proj_grad_far, proj_grad_near, proj_part, wide_summed, *output_parts)
        )
    )
    mixed = residual + output_sums[0]
    for part in output_parts:
        mixed = mixed + part.astype(jnp.float32)
    mixed = (keep * mixed).astype(jnp.bfloat16)
    part_far = through_proj(proj_grad_far)
    proj_summed = sum_planes(proj_part)
    part_near = through_proj(proj_grad_near)
    normed_grad, gated, mixed = reduce_plane(part_near, part_far, gated, mixed)

    out_grad = contract_halves(
        gated[: count // 2], gated[count // 2 :], low_near, low_far, jnp.float32
    )[:channels]
    gate_parts = []
    for index in range(held):
        at = index * block_width
        span = gate_grad[at : at + block_width]
        gate_parts.append(
            jnp.concatenate(
                [span[:, at : at + block_width], span[:, lanes + at : lanes + at + block_width]],
                axis=1,
            )
        )
    channel_grad = channel_grad[:, :channels]
    small_grad = jnp.concatenate(
        [
            channel_grad[: taps + 3],
            (channel_grad[taps + 3] * jax.nn.sigmoid(decay_channel))[None],
        ],
        axis=0,
    )
    by_row_grad = jnp.concatenate(
        [out_grad, jnp.concatenate(gate_parts, axis=0), small_grad.T], axis=1
    ).astype(jnp.bfloat16)
    by_row_grad = pad_lanes(by_row_grad, by_row.shape[2]).reshape(held, 2, chunk_rows, -1)
    kept = lax.dynamic_index_in_dim(by_row_grad, odd, 1, False)
    taken = swap_with(lax.dynamic_index_in_dim(by_row_grad, 1 - odd, 1, False), 1)
    by_row_grad = jnp.where(
        odd == 0, jnp.concatenate([kept, taken]), jnp.concatenate([taken, kept])
    ).reshape(planes * chunk_rows, -1)
    by_row_grad = sum_planes(by_row_grad)
    gate_up_grad, mlp_gain_grad = hand_back(spread_rows(wide_summed), gate_up, mlp_gain, wide_moves)
    in_proj_grad, norm_gain_grad = hand_back(spread_rows(proj_summed), in_proj, norm_gain, proj_moves)
    token_grad = residual_grad + norm_back(inputs, scale_one, gain_one, normed_grad)
    token_grad, by_row_grad = lax.optimization_barrier((token_grad, by_row_grad))
    by_row_grad = by_row_grad.astype(jnp.float32)
    out_proj_grad = by_row_grad[:, :depth]
    gate_weight_grad = by_row_grad[:, depth : depth + gate_columns]
    small_grad = by_row_grad[:, depth + gate_columns : by_row_width]
    return (
        mixed[None],
        token_grad[None],
        norm_gain_grad,
        in_proj_grad,
        small_grad[:, :taps],
        small_grad[:, taps],
        gate_weight_grad,
        small_grad[:, taps + 1 : taps + 3],
        small_grad[:, taps + 3],
        out_proj_grad,
        mlp_gain_grad,
        gate_up_grad,
        down_grad,
    )


def solution(mesh):
    planes, count = mesh.shape["bucket"], mesh.shape["seq"]
    whole_blocks = count == 8 and planes % 2 == 0 and planes * count == 2 * NB
    return jax.shard_map(
        by_channels if whole_blocks else on_device,
        mesh=mesh,
        in_specs=(
            P("bucket", "seq", None),
            P("bucket", None),
            P(("bucket", "seq")),
            P(("bucket", "seq"), None),
            P(("bucket", "seq"), None),
            P(("bucket", "seq")),
            P(("bucket", "seq"), None),
            P(("bucket", "seq"), None),
            P(("bucket", "seq")),
            P(("bucket", "seq"), None),
            P(("bucket", "seq")),
            P(("bucket", "seq"), None),
            P(("bucket", "seq"), None),
            P("bucket", "seq", None),
        ),
        out_specs=(
            P("bucket", "seq", None),
            P("bucket", "seq", None),
            P(("bucket", "seq")),
            P(("bucket", "seq"), None),
            P(("bucket", "seq"), None),
            P(("bucket", "seq")),
            P(("bucket", "seq"), None),
            P(("bucket", "seq"), None),
            P(("bucket", "seq")),
            P(("bucket", "seq"), None),
            P(("bucket", "seq")),
            P(("bucket", "seq"), None),
            P(("bucket", "seq"), None),
        ),
        check_vma=False,
    )
```

```python
from functools import partial

import jax
import jax.numpy as jnp
from jax import lax
from jax.experimental import pallas as pl
from jax.experimental.pallas import tpu as pltpu
from jax.sharding import PartitionSpec as P

NB = 16


norm_eps = 1e-06
gate_scale = 8.0


def from_behind(block, axis, distance):
    devices = range(lax.axis_size(axis))
    route = [(i - distance, i) for i in devices if i - distance in devices]
    return lax.ppermute(block, axis, route)


def entering(part, axis, combine, identity, reverse):
    count = lax.axis_size(axis)
    place = lax.axis_index(axis)
    ahead = count - 1 - place if reverse else place
    gathered = jax.tree.map(lambda a: lax.all_gather(a, axis), part)
    state = jax.tree.map(lambda a, e: jnp.zeros_like(a) + jnp.asarray(e, a.dtype), part, identity)

    def one(lap, state):
        source = count - 1 - lap if reverse else lap
        return combine(
            state, jax.tree.map(lambda a: lax.dynamic_index_in_dim(a, source, 0, False), gathered)
        )

    return lax.fori_loop(0, ahead, one, state)


def rms_scale(values, gain):
    return values * lax.rsqrt(jnp.mean(values * values, axis=1, keepdims=True) + norm_eps) * gain


def link(earlier, later):
    return (earlier[0] * later[0], later[0] * earlier[1] + later[1])


def segment_layout(lengths_row, positions):
    ends = jnp.cumsum(lengths_row)
    segment_ids = jnp.sum((positions[:, None] >= ends[None, :]).astype(jnp.int32), axis=1)
    segment_ids = jnp.where(positions < 0, -1, segment_ids)
    keep = (positions < ends[-1]).astype(jnp.float32)
    return (segment_ids, keep)


def lru_terms(conv_out, gate_a, gate_i, decay, starts):
    rate = jax.nn.softplus(decay)
    log_step = -gate_scale * jax.nn.sigmoid(gate_a) * rate
    decay_step = jnp.where(starts, 0.0, jnp.exp(log_step))
    scaling = jnp.where(starts, 1.0, jnp.sqrt(-jnp.expm1(2.0 * log_step)))
    return (decay_step, conv_out * jax.nn.sigmoid(gate_i) * scaling)


def gated_gelu(values, split):
    return jax.nn.gelu(values[:, :split]) * values[:, split:]


def contract_last(left, right):
    return lax.dot_general(
        left, right, (((1,), (1,)), ((), ())), preferred_element_type=jnp.float32
    )


def contract_first(left, right):
    return lax.dot_general(
        left, right, (((0,), (0,)), ((), ())), preferred_element_type=jnp.float32
    )


def row_product(left, right):
    return contract_first(left, right)


def on_device(
    tokens,
    lengths,
    norm_gain,
    in_proj,
    conv_weight,
    conv_bias,
    gate_weight,
    gate_bias,
    decay,
    out_proj,
    mlp_gain,
    gate_up,
    down_proj,
    cotangent,
):
    inputs = tokens[0].astype(jnp.float32)
    tok_rows = inputs.shape[0]
    width = in_proj.shape[1] // 2
    ff_width = gate_up.shape[1] // 2
    block_width = width // NB
    kernel = conv_weight.shape[1]
    rim_rows = kernel - 1
    (
        gain_one_all,
        proj_all,
        conv_all,
        conv_bias_all,
        gate_all,
        gate_bias_all,
        decay_all,
        out_all,
        gain_two_all,
    ) = (
        lax.all_gather(norm_gain, ("bucket", "seq"), axis=0, tiled=True),
        lax.all_gather(in_proj, ("bucket", "seq"), axis=0, tiled=True),
        lax.all_gather(conv_weight, ("bucket", "seq"), axis=0, tiled=True),
        lax.all_gather(conv_bias, ("bucket", "seq"), axis=0, tiled=True),
        lax.all_gather(gate_weight, ("bucket", "seq"), axis=0, tiled=True),
        lax.all_gather(gate_bias, ("bucket", "seq"), axis=0, tiled=True),
        lax.all_gather(decay, ("bucket", "seq"), axis=0, tiled=True),
        lax.all_gather(out_proj, ("bucket", "seq"), axis=0, tiled=True),
        lax.all_gather(mlp_gain, ("bucket", "seq"), axis=0, tiled=True),
    )
    seq_index = lax.axis_index("seq")
    positions = seq_index * tok_rows + jnp.arange(tok_rows, dtype=jnp.int32)
    lengths_row = lengths[0]
    segment_ids, keep = segment_layout(lengths_row, positions)
    back_ids = segment_layout(lengths_row, positions - 1)[0]
    starts = (segment_ids != back_ids)[:, None]
    normed, norm_pull = jax.vjp(rms_scale, inputs, gain_one_all.astype(jnp.float32))
    normed_low = normed.astype(jnp.bfloat16)
    projected = jnp.dot(normed_low, proj_all, preferred_element_type=jnp.float32)
    mixer_in = projected[:, :width].astype(jnp.bfloat16)
    branch = projected[:, width:]
    rim = from_behind(mixer_in[tok_rows - rim_rows :], "seq", 1)
    extended = jnp.concatenate([rim, mixer_in], axis=0)
    conv_float = conv_all.astype(jnp.float32)
    lagged_terms = []
    convolved = jnp.zeros((tok_rows, width), jnp.float32) + conv_bias_all.astype(jnp.float32)
    for offset in range(kernel):
        earlier_ids = segment_layout(lengths_row, positions - offset)[0]
        lagged = jnp.where(
            (earlier_ids == segment_ids)[:, None],
            extended[rim_rows - offset : rim_rows - offset + tok_rows].astype(jnp.float32),
            0.0,
        )
        lagged_terms.append(lagged)
        convolved = convolved + lagged * conv_float[:, offset]
    conv_out = convolved.astype(jnp.bfloat16)
    gates = jnp.einsum(
        "tnc,ncd->tnd",
        conv_out.reshape(tok_rows, NB, block_width),
        gate_all.reshape(NB, block_width, 2 * block_width),
        preferred_element_type=jnp.float32,
    )
    gate_bias_float = gate_bias_all.astype(jnp.float32)
    gate_a = gates[:, :, :block_width].reshape(tok_rows, width) + gate_bias_float[:, 0]
    gate_i = gates[:, :, block_width:].reshape(tok_rows, width) + gate_bias_float[:, 1]
    (decay_step, normalized), lru_pull = jax.vjp(
        partial(lru_terms, starts=starts),
        conv_out.astype(jnp.float32),
        gate_a,
        gate_i,
        decay_all.astype(jnp.float32),
    )
    prefix_decay, prefix_state = lax.associative_scan(link, (decay_step, normalized), axis=0)
    carried = entering(
        (prefix_decay[-1], prefix_state[-1]),
        "seq",
        link,
        (jnp.ones((width,), jnp.float32), jnp.zeros((width,), jnp.float32)),
        False,
    )
    state_in = carried[1]
    hidden = prefix_state + prefix_decay * state_in
    branch_act, branch_pull = jax.vjp(jax.nn.gelu, branch)
    gated = (hidden * branch_act).astype(jnp.bfloat16)
    residual = inputs + jnp.dot(gated, out_all, preferred_element_type=jnp.float32)
    normed_two, norm_two_pull = jax.vjp(rms_scale, residual, gain_two_all.astype(jnp.float32))
    normed_two_low = normed_two.astype(jnp.bfloat16)
    gate_up_all, down_all = (
        lax.all_gather(gate_up, ("bucket", "seq"), axis=0, tiled=True),
        lax.all_gather(down_proj, ("bucket", "seq"), axis=0, tiled=True),
    )
    expanded = jnp.dot(normed_two_low, gate_up_all, preferred_element_type=jnp.float32)
    feed, feed_pull = jax.vjp(partial(gated_gelu, split=ff_width), expanded)
    feed_low = feed.astype(jnp.bfloat16)
    output_rows = residual + jnp.dot(feed_low, down_all, preferred_element_type=jnp.float32)
    mixed = (keep[:, None] * output_rows).astype(jnp.bfloat16)
    upstream = keep[:, None] * cotangent[0].astype(jnp.float32)
    upstream_low = upstream.astype(jnp.bfloat16)
    down_grad = lax.psum_scatter(
        row_product(feed_low, upstream_low), ("bucket", "seq"), scatter_dimension=0, tiled=True
    )
    feed_grad = contract_last(upstream_low, down_all)
    expanded_grad = feed_pull(feed_grad)[0].astype(jnp.bfloat16)
    gate_up_grad = lax.psum_scatter(
        row_product(normed_two_low, expanded_grad),
        ("bucket", "seq"),
        scatter_dimension=0,
        tiled=True,
    )
    normed_two_grad = contract_last(expanded_grad, gate_up_all)
    residual_part, gain_two_grad = norm_two_pull(normed_two_grad)
    residual_grad = upstream + residual_part
    residual_low = residual_grad.astype(jnp.bfloat16)
    out_grad = contract_first(gated, residual_low)
    gated_grad = contract_last(residual_low, out_all)
    hidden_grad = gated_grad * branch_act
    branch_grad = branch_pull(gated_grad * hidden)[0]
    next_decay = jnp.concatenate([decay_step[1:], jnp.ones((1, width), jnp.float32)], axis=0)
    suffix_decay, suffix_state = lax.associative_scan(
        link, (next_decay, hidden_grad), reverse=True, axis=0
    )
    returned = entering(
        (prefix_decay[-1], decay_step[0] * suffix_state[0]),
        "seq",
        link,
        (jnp.ones((width,), jnp.float32), jnp.zeros((width,), jnp.float32)),
        True,
    )
    incoming = returned[1]
    state_grad = suffix_state + suffix_decay * incoming
    state_before = jnp.concatenate([state_in[None, :], hidden[:-1]], axis=0)
    conv_grad_lru, gate_a_grad, gate_i_grad, decay_grad = lru_pull(
        (state_grad * state_before, state_grad)
    )
    gates_low = jnp.concatenate(
        [
            gate_a_grad.reshape(tok_rows, NB, block_width),
            gate_i_grad.reshape(tok_rows, NB, block_width),
        ],
        axis=2,
    ).astype(jnp.bfloat16)
    gate_grad = jnp.einsum(
        "tnc,tnd->ncd",
        conv_out.reshape(tok_rows, NB, block_width),
        gates_low,
        preferred_element_type=jnp.float32,
    ).reshape(width, 2 * block_width)
    bias_sums = jnp.sum(gates_low.astype(jnp.float32), axis=0)
    gate_bias_grad = jnp.stack(
        [bias_sums[:, :block_width].reshape(width), bias_sums[:, block_width:].reshape(width)],
        axis=1,
    )
    conv_grad_gates = jnp.einsum(
        "tnd,ncd->tnc",
        gates_low,
        gate_all.reshape(NB, block_width, 2 * block_width),
        preferred_element_type=jnp.float32,
    ).reshape(tok_rows, width)
    conv_low = (conv_grad_lru + conv_grad_gates).astype(jnp.bfloat16)
    head = from_behind(conv_low[:rim_rows], "seq", -1)
    trailing = jnp.concatenate([conv_low, head], axis=0)
    conv_low_float = conv_low.astype(jnp.float32)
    mixer_grad = jnp.zeros((tok_rows, width), jnp.float32)
    tap_grads = []
    for offset in range(kernel):
        later_ids = segment_layout(lengths_row, positions + offset)[0]
        ahead = jnp.where(
            (later_ids == segment_ids)[:, None],
            trailing[offset : offset + tok_rows].astype(jnp.float32),
            0.0,
        )
        mixer_grad = mixer_grad + ahead * conv_float[:, offset]
        tap_grads.append(jnp.sum(conv_low_float * lagged_terms[offset], axis=0))
    conv_weight_grad = jnp.stack(tap_grads, axis=1)
    conv_bias_grad = jnp.sum(conv_low_float, axis=0)
    proj_grad_low = jnp.concatenate([mixer_grad, branch_grad], axis=1).astype(jnp.bfloat16)
    in_proj_grad = contract_first(normed_low, proj_grad_low)
    normed_grad = contract_last(proj_grad_low, proj_all)
    input_part, gain_one_grad = norm_pull(normed_grad)
    token_grad = residual_grad + input_part
    summed = (
        lax.psum_scatter(gain_one_grad, ("bucket", "seq"), scatter_dimension=0, tiled=True),
        lax.psum_scatter(in_proj_grad, ("bucket", "seq"), scatter_dimension=0, tiled=True),
        lax.psum_scatter(conv_weight_grad, ("bucket", "seq"), scatter_dimension=0, tiled=True),
        lax.psum_scatter(conv_bias_grad, ("bucket", "seq"), scatter_dimension=0, tiled=True),
        lax.psum_scatter(gate_grad, ("bucket", "seq"), scatter_dimension=0, tiled=True),
        lax.psum_scatter(gate_bias_grad, ("bucket", "seq"), scatter_dimension=0, tiled=True),
        lax.psum_scatter(decay_grad, ("bucket", "seq"), scatter_dimension=0, tiled=True),
        lax.psum_scatter(out_grad, ("bucket", "seq"), scatter_dimension=0, tiled=True),
        lax.psum_scatter(gain_two_grad, ("bucket", "seq"), scatter_dimension=0, tiled=True),
    )
    return (
        mixed[None],
        token_grad[None],
        summed[0],
        summed[1],
        summed[2],
        summed[3],
        summed[4],
        summed[5],
        summed[6],
        summed[7],
        summed[8],
        gate_up_grad,
        down_grad,
    )


def swap_with(block, mask):
    route = [(i, i ^ mask) for i in range(lax.axis_size("seq"))]
    return lax.ppermute(block, "seq", route)


CORE, ACROSS_X, ACROSS_Y = 1, 2, 4


def split_row(rows):
    return rows // 32 * 16


def gather_chips(block, *others):
    split = split_row(block.shape[0])
    across_x, across_y = swap_with(block, ACROSS_X), swap_with(block, ACROSS_Y)
    if others:
        across_x, across_y, *others = lax.optimization_barrier((across_x, across_y, *others))
    both = [swap_with(across_y[:split], ACROSS_X), swap_with(across_x[split:], ACROSS_Y)]
    near = jnp.concatenate([block, across_x, across_y, *both]).reshape(4, *block.shape)
    return (near, *others) if others else near


def send_to_chips(across_x, across_y, across_both):
    return [
        swap_with(across_x, ACROSS_X),
        swap_with(across_y, ACROSS_Y),
        swap_with(across_both, ACROSS_X + ACROSS_Y),
    ]


def reduce_plane(near, far, *others, late=()):
    other = swap_with(far, CORE)
    rows = near.shape[1]
    split = split_row(rows)

    def total(place, span=slice(None)):
        return near[place, span].astype(jnp.float32) + other[place, span].astype(jnp.float32)

    both = total(3).astype(jnp.bfloat16)
    both, *others = lax.optimization_barrier((both, *others))
    first = swap_with(both[:split], ACROSS_Y).astype(jnp.float32)
    second = swap_with(both[split:], ACROSS_X).astype(jnp.float32)
    across_x = jnp.concatenate([total(1, slice(split)) + first, total(1, slice(split, None))])
    across_y = jnp.concatenate([total(2, slice(split)), total(2, slice(split, None)) + second])
    across_x, across_y = across_x.astype(jnp.bfloat16), across_y.astype(jnp.bfloat16)
    across_x, across_y, *late = lax.optimization_barrier((across_x, across_y, *late))
    others += late
    across_x = swap_with(across_x, ACROSS_X).astype(jnp.float32)
    across_y = swap_with(across_y, ACROSS_Y).astype(jnp.float32)
    result = total(0) + across_x + across_y
    return (result, *others) if others else result


def reduce_plane_at_once(near, far, *others):
    other = swap_with(far, CORE)

    def total(place):
        return near[place].astype(jnp.float32) + other[place].astype(jnp.float32)

    *parts, others = lax.optimization_barrier(
        (*(total(place).astype(jnp.bfloat16) for place in (1, 2, 3)), others)
    )
    sent = send_to_chips(*parts)

    def finish(*late):
        *parts, late = lax.optimization_barrier((*sent, late))
        result = total(0)
        for part in parts:
            result = result + part.astype(jnp.float32)
        return (result, *late) if late else result

    return (finish, *others)


def place_of(chunk, me, count):
    relative = jnp.bitwise_xor(chunk, me)
    return jnp.bitwise_and(relative, 1), jnp.right_shift(relative, 1)


def series_expm1(values):
    total = 1.0 + values * (1.0 / 7.0)
    for term in (6, 5, 4, 3, 2):
        total = 1.0 + values * (1.0 / term) * total
    return values * total


def segment_reach(info_ref, first, slots, shape, total):
    positions = first + lax.broadcasted_iota(jnp.int32, shape, 0)
    begin = jnp.zeros(shape, jnp.int32)
    finish = jnp.full(shape, total, jnp.int32)
    for slot in range(slots):
        end = info_ref[1 + slot]
        passed = positions >= end
        begin = jnp.where(passed, jnp.maximum(begin, end), begin)
        finish = jnp.where(passed, finish, jnp.minimum(finish, end))
    return positions - begin, finish - positions


def widen(mask, lanes):
    return jnp.concatenate([mask] * (lanes // mask.shape[1]), axis=1)


def gelu_parts(values):
    inner = 0.7978845608028654 * (values + 0.044715 * values * values * values)
    bent = jnp.tanh(inner)
    half = 0.5 * (1.0 + bent)
    slope = half + 0.5 * values * (1.0 - bent * bent) * 0.7978845608028654 * (
        1.0 + 3.0 * 0.044715 * values * values
    )
    return values * half, slope


ROWS = 8


def tiles_at_once(tiles):
    return max(size for size in range(1, GROUP + 1) if tiles % size == 0)


def group_tiles(index, group):
    return [index * group + member for member in range(group)]


GROUP = 11
TAP, BIAS, BIAS_A, BIAS_I, RATE = 0, 4, 5, 6, 7


def mixer_forward(
    taps,
    slots,
    info_ref,
    near_ref,
    far_ref,
    proj_ref,
    gate_ref,
    channel_ref,
    gated_ref,
    lagging_ref,
    conv_ref,
    act_ref,
    slope_ref,
    decay_ref,
    rate_part_ref,
    gate_i_part_ref,
    conv_part_ref,
    gate_r_ref,
    lag_edge_ref,
    proj_wide,
    projected,
    convolved,
    gates,
    carry,
    edge,
):
    chunk = pl.program_id(0)
    is_far, _ = place_of(chunk, info_ref[0], pl.num_programs(0))
    rows, lanes = convolved.shape
    tiles = rows // ROWS
    group = tiles_at_once(tiles)
    total = rows * pl.num_programs(0)

    @pl.when(chunk == 0)
    def _():
        carry[...] = jnp.zeros_like(carry)
        edge[...] = jnp.zeros_like(edge)
        channels = proj_ref.shape[1] // 2
        proj_wide[...] = jnp.zeros_like(proj_wide)
        proj_wide[:, :channels] = proj_ref[:, :channels]
        proj_wide[:, lanes : lanes + channels] = proj_ref[:, channels:]

    def project(normed_ref):
        product = jnp.dot(normed_ref[0], proj_wide[...], preferred_element_type=jnp.float32)
        low = product[:, :lanes].astype(jnp.bfloat16)
        lagging_ref[0] = low
        projected[:, :lanes] = low.astype(jnp.float32)
        projected[:, lanes:] = product[:, lanes:]

    pl.when(is_far == 0)(lambda: project(near_ref))
    pl.when(is_far == 1)(lambda: project(far_ref))
    place = lax.broadcasted_iota(jnp.int32, (ROWS, lanes), 0)

    def convolve(tile, before):
        for tile in group_tiles(tile, group):
            before = convolve_tile(tile, before)
        return before

    def convolve_tile(tile, before):
        at = pl.ds(pl.multiple_of(tile * ROWS, ROWS), ROWS)
        here = projected[at, :lanes]
        since, _ = segment_reach(info_ref, chunk * rows + tile * ROWS, slots, (ROWS, 128), total)
        value = channel_ref[BIAS : BIAS + 1, :] + here * channel_ref[TAP : TAP + 1, :]
        for lag in range(1, taps):
            moved = jnp.where(
                place < lag, pltpu.roll(before, lag, 0), pltpu.roll(here, lag, 0)
            )
            value = value + jnp.where(widen(since >= lag, lanes), moved, 0.0) * (
                channel_ref[TAP + lag : TAP + lag + 1, :]
            )
        convolved[at, :] = value
        return here

    last = lax.fori_loop(0, tiles // group, convolve, edge[...])
    edge[...] = last
    lag_edge_ref[0] = last
    conv_low = convolved[...].astype(jnp.bfloat16)
    conv_ref[0] = conv_low
    convolved[...] = conv_low.astype(jnp.float32)
    gates[...] = jnp.dot(conv_low, gate_ref[...], preferred_element_type=jnp.float32)

    def recur(tile, state):
        parts = [local_scan(tile) for tile in group_tiles(tile, group)]
        for at, value, decay, activated, slope, ratio, gate in parts:
            hidden = value + decay * state
            before = jnp.where(place == 0, state, pltpu.roll(hidden, 1, 0))
            state = jnp.broadcast_to(hidden[ROWS - 1 :], hidden.shape)
            projected[at, :lanes] = hidden * activated
            slope_ref[0, at, :] = hidden * slope
            rate_part_ref[0, at, :] = gate * (before - ratio)
        return state

    def local_scan(tile):
        at = pl.ds(pl.multiple_of(tile * ROWS, ROWS), ROWS)
        since, _ = segment_reach(info_ref, chunk * rows + tile * ROWS, slots, (ROWS, 128), total)
        starts = widen(since == 0, lanes)
        gate_r = jax.nn.sigmoid(gates[at, :lanes] + channel_ref[BIAS_A : BIAS_A + 1, :])
        gate_i = jax.nn.sigmoid(gates[at, lanes:] + channel_ref[BIAS_I : BIAS_I + 1, :])
        less = series_expm1(-gate_scale * gate_r * channel_ref[RATE : RATE + 1, :])
        plain = 1.0 + less
        root = jnp.sqrt(-less * (2.0 + less))
        decay = jnp.where(starts, 0.0, plain)
        scaling = jnp.where(starts, 1.0, root)
        conv = convolved[at, :]
        admitted = conv * gate_i
        value = admitted * scaling
        decay_ref[0, at, :] = decay
        conv_part_ref[0, at, :] = gate_i * scaling
        gate_i_part_ref[0, at, :] = value * (1.0 - gate_i)
        gate_r_ref[0, at, :] = 1.0 - gate_r
        ratio = admitted * plain / root
        gate = decay * gate_r
        for step in (1, 2, 4):
            inside = place >= step
            value = value + jnp.where(inside, decay * pltpu.roll(value, step, 0), 0.0)
            decay = jnp.where(inside, decay * pltpu.roll(decay, step, 0), decay)
        activated, slope = gelu_parts(projected[at, lanes:])
        act_ref[0, at, :] = activated
        return at, value, decay, activated, slope, ratio, gate

    carry[...] = lax.fori_loop(0, tiles // group, recur, carry[...])
    gated_ref[0] = projected[:, :lanes].astype(jnp.bfloat16)


def mixer_backward(
    taps,
    slots,
    info_ref,
    near_ref,
    far_ref,
    out_ref,
    gate_ref,
    channel_ref,
    act_ref,
    slope_ref,
    decay_ref,
    rate_part_ref,
    gate_i_part_ref,
    conv_part_ref,
    gate_r_ref,
    conv_ref,
    lagging_ref,
    lag_edge_ref,
    projected_ref,
    gate_grad_ref,
    channel_grad_ref,
    coming,
    conv_part,
    lagged,
    gates,
    projected,
    conv_grad,
    grad_carry,
    decay_carry,
    sums,
):
    lap = pl.program_id(0)
    laps = pl.num_programs(0)
    chunk = laps - 1 - lap
    is_far, _ = place_of(chunk, info_ref[0], laps)
    rows, lanes = conv_part.shape
    tiles = rows // ROWS
    group = tiles_at_once(tiles)
    total = rows * laps

    @pl.when(lap == 0)
    def _():
        grad_carry[...] = jnp.zeros_like(grad_carry)
        decay_carry[...] = jnp.zeros_like(decay_carry)
        conv_grad[...] = jnp.zeros_like(conv_grad)
        sums[...] = jnp.zeros_like(sums)
        gate_grad_ref[...] = jnp.zeros_like(gate_grad_ref)

    def expand(down_ref):
        coming[...] = lax.dot_general(
            down_ref[0], out_ref[...], (((1,), (1,)), ((), ())), preferred_element_type=jnp.float32
        )

    pl.when(is_far == 0)(lambda: expand(near_ref))
    pl.when(is_far == 1)(lambda: expand(far_ref))
    lagged[...] = lagging_ref[0].astype(jnp.float32)
    place = lax.broadcasted_iota(jnp.int32, (ROWS, lanes), 0)

    def recur(step_index, carried):
        later_grad, later_decay, sum_a, sum_i, sum_rate = carried
        members = group_tiles(tiles // group - 1 - step_index, group)[::-1]
        parts = []
        for tile in members:
            part = local_scan(tile, later_decay)
            later_decay = part[-1]
            parts.append(part)
        for at, value, weight, _ in parts:
            grad = value + weight * later_grad
            later_grad = jnp.broadcast_to(grad[:1], grad.shape)
            conv_part[at, :] = grad * conv_part_ref[0, at, :]
            grad_i = grad * gate_i_part_ref[0, at, :]
            grad_rate = grad * rate_part_ref[0, at, :]
            grad_a = (-gate_scale * channel_ref[RATE : RATE + 1, :]) * grad_rate * gate_r_ref[0, at, :]
            grad_a = grad_a.astype(jnp.bfloat16).astype(jnp.float32)
            grad_i = grad_i.astype(jnp.bfloat16).astype(jnp.float32)
            gates[at, :lanes] = grad_a
            gates[at, lanes:] = grad_i
            sum_a = sum_a + grad_a
            sum_i = sum_i + grad_i
            sum_rate = sum_rate - gate_scale * grad_rate
        return later_grad, later_decay, sum_a, sum_i, sum_rate

    def local_scan(tile, later_decay):
        at = pl.ds(pl.multiple_of(tile * ROWS, ROWS), ROWS)
        decay = decay_ref[0, at, :]
        down = coming[at, :]
        value = down * act_ref[0, at, :]
        projected[at, lanes:] = down * slope_ref[0, at, :]
        weight = jnp.where(place == ROWS - 1, later_decay, pltpu.roll(decay, ROWS - 1, 0))
        for step in (1, 2, 4):
            inside = place < ROWS - step
            value = value + jnp.where(inside, weight * pltpu.roll(value, ROWS - step, 0), 0.0)
            weight = jnp.where(inside, weight * pltpu.roll(weight, ROWS - step, 0), weight)
        return at, value, weight, jnp.broadcast_to(decay[:1], decay.shape)

    empty = jnp.zeros((ROWS, lanes), jnp.float32)
    grad_last, decay_last, sum_a, sum_i, sum_rate = lax.fori_loop(
        0, tiles // group, recur, (grad_carry[...], decay_carry[...], empty, empty, empty)
    )
    grad_carry[...] = grad_last
    decay_carry[...] = decay_last
    gates_low = gates[...].astype(jnp.bfloat16)
    gate_grad_ref[...] += lax.dot_general(
        conv_ref[0], gates_low, (((0,), (0,)), ((), ())), preferred_element_type=jnp.float32
    )
    from_gates = lax.dot_general(
        gates_low, gate_ref[...], (((1,), (1,)), ((), ())), preferred_element_type=jnp.float32
    )
    conv_grad[rows:, :] = conv_grad[:ROWS, :]
    conv_grad[:rows, :] = (conv_part[...] + from_gates).astype(jnp.bfloat16).astype(jnp.float32)

    def unconvolve(tile, carried):
        for tile in group_tiles(tile, group):
            carried = unconvolve_tile(tile, carried)
        return carried

    def unconvolve_tile(tile, carried):
        earlier, sum_bias, sum_taps = carried
        at = pl.ds(pl.multiple_of(tile * ROWS, ROWS), ROWS)
        beyond = pl.ds(pl.multiple_of((tile + 1) * ROWS, ROWS), ROWS)
        since, until = segment_reach(
            info_ref, chunk * rows + tile * ROWS, slots, (ROWS, 128), total
        )
        here = lagged[at, :]
        grad = conv_grad[at, :]
        later = conv_grad[beyond, :]
        value = grad * channel_ref[TAP : TAP + 1, :]
        new_taps = [sum_taps[0] + grad * here]
        for lag in range(1, taps):
            ahead = jnp.where(
                place < ROWS - lag, pltpu.roll(grad, ROWS - lag, 0), pltpu.roll(later, ROWS - lag, 0)
            )
            value = value + jnp.where(widen(until > lag, lanes), ahead, 0.0) * (
                channel_ref[TAP + lag : TAP + lag + 1, :]
            )
            moved = jnp.where(
                place < lag, pltpu.roll(earlier, lag, 0), pltpu.roll(here, lag, 0)
            )
            new_taps.append(
                sum_taps[lag] + grad * jnp.where(widen(since >= lag, lanes), moved, 0.0)
            )
        projected[at, :lanes] = value
        return here, sum_bias + grad, tuple(new_taps)

    _, sum_bias, sum_taps = lax.fori_loop(
        0, tiles // group, unconvolve, (lag_edge_ref[0], empty, (empty,) * taps)
    )
    low = projected[...].astype(jnp.bfloat16)
    channels = projected_ref.shape[2] // 2
    projected_ref[0, :, :channels] = low[:, :channels]
    projected_ref[0, :, channels:] = low[:, lanes : lanes + channels]
    for place_in, part in enumerate((*sum_taps, sum_bias, sum_a, sum_i, sum_rate)):
        sums[place_in] += part

    @pl.when(lap == laps - 1)
    def _():
        channel_grad_ref[...] = jnp.sum(sums[...], axis=1)


VMEM_LIMIT = 56 * 1024 * 1024


def run_forward(info, near, far, proj, gate, channels, taps, slots):
    chips, rows, depth = near.shape
    count = 2 * chips
    lanes = gate.shape[0]

    def at_chip(chunk, info_ref):
        return (place_of(chunk, info_ref[0], count)[1], 0, 0)

    def at_place(chunk, info_ref):
        is_far, chip = place_of(chunk, info_ref[0], count)
        return (is_far * chips + chip, 0, 0)

    def at_chunk(chunk, info_ref):
        return (chunk, 0, 0)

    def whole(chunk, info_ref):
        return (0, 0)

    def block(kind):
        return jax.ShapeDtypeStruct((count, rows, lanes), kind)

    wide = pl.BlockSpec((1, rows, depth), at_chip)
    narrow = pl.BlockSpec((1, rows, lanes), at_place)
    return pl.pallas_call(
        partial(mixer_forward, taps, slots),
        grid_spec=pltpu.PrefetchScalarGridSpec(
            num_scalar_prefetch=1,
            grid=(count,),
            in_specs=[
                wide,
                wide,
                pl.BlockSpec(proj.shape, whole),
                pl.BlockSpec(gate.shape, whole),
                pl.BlockSpec(channels.shape, whole),
            ],
            out_specs=[narrow] * 10 + [pl.BlockSpec((1, ROWS, lanes), at_chunk)],
            scratch_shapes=[
                pltpu.VMEM((depth, 2 * lanes), jnp.bfloat16),
                pltpu.VMEM((rows, 2 * lanes), jnp.float32),
                pltpu.VMEM((rows, lanes), jnp.float32),
                pltpu.VMEM((rows, 2 * lanes), jnp.float32),
                pltpu.VMEM((ROWS, lanes), jnp.float32),
                pltpu.VMEM((ROWS, lanes), jnp.float32),
            ],
        ),
        out_shape=[block(jnp.bfloat16)] * 3
        + [block(jnp.float32)] * 7
        + [jax.ShapeDtypeStruct((count, ROWS, lanes), jnp.float32)],
        compiler_params=pltpu.CompilerParams(
            dimension_semantics=("arbitrary",), vmem_limit_bytes=VMEM_LIMIT
        ),
        cost_estimate=pl.CostEstimate(flops=0, bytes_accessed=0, transcendentals=0),
        name="mixer_forward",
    )(info, near, far, proj, gate, channels)


def run_backward(info, near, far, out, gate, channels, saved, proj_columns, taps, slots):
    lagging, conv, *parts, lag_edge = saved
    chips, rows, depth = near.shape
    count = 2 * chips
    lanes = gate.shape[0]

    def at_chip(lap, info_ref):
        return (place_of(count - 1 - lap, info_ref[0], count)[1], 0, 0)

    def at_place(lap, info_ref):
        is_far, chip = place_of(count - 1 - lap, info_ref[0], count)
        return (is_far * chips + chip, 0, 0)

    def before(lap, info_ref):
        return (jnp.maximum(count - 2 - lap, 0), 0, 0)

    def whole(lap, info_ref):
        return (0, 0)

    wide = pl.BlockSpec((1, rows, depth), at_chip)
    narrow = pl.BlockSpec((1, rows, lanes), at_place)
    rim = pl.BlockSpec((1, ROWS, lanes), before)
    sums = taps + 4
    return pl.pallas_call(
        partial(mixer_backward, taps, slots),
        grid_spec=pltpu.PrefetchScalarGridSpec(
            num_scalar_prefetch=1,
            grid=(count,),
            in_specs=[
                wide,
                wide,
                pl.BlockSpec(out.shape, whole),
                pl.BlockSpec(gate.shape, whole),
                pl.BlockSpec(channels.shape, whole),
            ]
            + [narrow] * 9
            + [rim],
            out_specs=[
                pl.BlockSpec((1, rows, proj_columns), at_place),
                pl.BlockSpec((lanes, 2 * lanes), whole),
                pl.BlockSpec((sums, lanes), whole),
            ],
            scratch_shapes=[
                pltpu.VMEM((rows, lanes), jnp.float32),
                pltpu.VMEM((rows, lanes), jnp.float32),
                pltpu.VMEM((rows, lanes), jnp.float32),
                pltpu.VMEM((rows, 2 * lanes), jnp.float32),
                pltpu.VMEM((rows, 2 * lanes), jnp.float32),
                pltpu.VMEM((rows + ROWS, lanes), jnp.float32),
                pltpu.VMEM((ROWS, lanes), jnp.float32),
                pltpu.VMEM((ROWS, lanes), jnp.float32),
                pltpu.VMEM((sums, ROWS, lanes), jnp.float32),
            ],
        ),
        out_shape=[
            jax.ShapeDtypeStruct((count, rows, proj_columns), jnp.bfloat16),
            jax.ShapeDtypeStruct((lanes, 2 * lanes), jnp.float32),
            jax.ShapeDtypeStruct((sums, lanes), jnp.float32),
        ],
        compiler_params=pltpu.CompilerParams(
            dimension_semantics=("arbitrary",), vmem_limit_bytes=VMEM_LIMIT
        ),
        cost_estimate=pl.CostEstimate(flops=0, bytes_accessed=0, transcendentals=0),
        name="mixer_backward",
    )(info, near, far, out, gate, channels, *parts, conv, lagging, lag_edge)


def proj_backward(part_ref, proj_ref, signal_ref, normed_ref):
    normed_ref[...] = lax.dot_general(
        part_ref[...], proj_ref[...], (((1,), (1,)), ((), ())), preferred_element_type=jnp.float32
    ).astype(jnp.bfloat16)


def run_proj_backward(part, proj, signal):
    rows, columns = part.shape
    steps = max(count for count in (3, 2, 1) if rows % (16 * count) == 0)
    return pl.pallas_call(
        proj_backward,
        grid=(steps,),
        in_specs=[
            pl.BlockSpec((rows // steps, columns), lambda step: (step, 0)),
            pl.BlockSpec(proj.shape, lambda step: (0, 0)),
            pl.BlockSpec(memory_space=pl.ANY),
        ],
        out_specs=pl.BlockSpec((rows // steps, proj.shape[0]), lambda step: (step, 0)),
        out_shape=jax.ShapeDtypeStruct((rows, proj.shape[0]), jnp.bfloat16),
        compiler_params=pltpu.CompilerParams(vmem_limit_bytes=VMEM_LIMIT),
        cost_estimate=pl.CostEstimate(
            flops=2 * rows * columns * proj.shape[0], bytes_accessed=0, transcendentals=0
        ),
        name="proj_backward",
    )(part, proj, signal)


def deal_columns(moves, whole_ref, groups_ref):
    for group, inside, column, width in moves:
        groups_ref[group, :, inside : inside + width] = whole_ref[:, column : column + width]


def collect_columns(moves, groups_ref, weight_ref, whole_ref, lean_ref):
    for group, inside, column, width in moves:
        whole_ref[:, column : column + width] = groups_ref[
            group, :, inside : inside + width
        ].astype(jnp.float32)
    lean = jnp.zeros((weight_ref.shape[0], 128), jnp.float32)
    for column in range(0, weight_ref.shape[1], 128):
        span = slice(column, column + 128)
        lean = lean + whole_ref[:, span] * weight_ref[:, span].astype(jnp.float32)
    lean_ref[...] = jnp.sum(lean, axis=1, keepdims=True)


def hand_out(weight, moves):
    count = lax.axis_size("seq")
    rows, columns = weight.shape
    groups = pl.pallas_call(
        partial(deal_columns, moves),
        out_shape=jax.ShapeDtypeStruct((count, rows, columns // count), weight.dtype),
        compiler_params=pltpu.CompilerParams(vmem_limit_bytes=VMEM_LIMIT),
        name="deal_columns",
    )(weight)
    dealt = lax.all_to_all(groups, "seq", split_axis=0, concat_axis=0, tiled=True)
    return dealt.reshape(-1, columns // count)


def sum_planes(grad):
    return lax.psum_scatter(
        grad.astype(jnp.bfloat16), "bucket", scatter_dimension=0, tiled=True
    )


def spread_rows(summed):
    count = lax.axis_size("seq")
    blocks = summed.reshape(count, -1, summed.shape[1])
    return lax.all_to_all(blocks, "seq", split_axis=0, concat_axis=0, tiled=True)


def hand_back(blocks, weight, gain, moves):
    rows, columns = weight.shape
    whole, lean = pl.pallas_call(
        partial(collect_columns, moves),
        out_shape=[
            jax.ShapeDtypeStruct((rows, columns), jnp.float32),
            jax.ShapeDtypeStruct((rows, 1), jnp.float32),
        ],
        compiler_params=pltpu.CompilerParams(vmem_limit_bytes=VMEM_LIMIT),
        name="collect_columns",
    )(blocks, weight)
    return whole, lean[:, 0] / gain.astype(jnp.float32)


FOLD = 512


def row_spans(rows):
    parts = max(count for count in (4, 3, 2, 1) if rows % (16 * count) == 0)
    return [slice(part * rows // parts, (part + 1) * rows // parts) for part in range(parts)]


def feed_forward(near_ref, far_ref, wide_ref, feed_grad_ref, feed_ref, grad_ref, normed_ref):
    half = FOLD // 2

    def expand(part_ref):
        for span in row_spans(part_ref.shape[0]):
            product = jnp.dot(
                part_ref[span, :], wide_ref[...], preferred_element_type=jnp.float32
            )
            activated, slope = gelu_parts(product[:, :half])
            up = product[:, half:]
            feed_ref[span, :] = (activated * up).astype(jnp.bfloat16)
            feed_grad = feed_grad_ref[span, :]
            grad_ref[span, :half] = (feed_grad * up * slope).astype(jnp.bfloat16)
            grad_ref[span, half:] = (feed_grad * activated).astype(jnp.bfloat16)

        @pl.when(pl.program_id(1) == 0)
        def _():
            normed_ref[...] = part_ref[...]

    pl.when(pl.program_id(0) == 0)(lambda: expand(near_ref))
    pl.when(pl.program_id(0) == 1)(lambda: expand(far_ref))


def run_feed_forward(near, far, wide, feed_grad):
    rows, depth = near.shape
    tiles = wide.shape[1] // FOLD
    half = FOLD // 2

    def whole(part, tile):
        return (0, 0)

    return pl.pallas_call(
        feed_forward,
        grid=(2, tiles),
        in_specs=[
            pl.BlockSpec((rows, depth), whole),
            pl.BlockSpec((rows, depth), whole),
            pl.BlockSpec((depth, FOLD), lambda part, tile: (0, tile)),
            pl.BlockSpec((rows, half), lambda part, tile: (part, tile)),
        ],
        out_specs=[
            pl.BlockSpec((rows, half), lambda part, tile: (part, tile)),
            pl.BlockSpec((rows, FOLD), lambda part, tile: (part, tile)),
            pl.BlockSpec((rows, depth), lambda part, tile: (part, 0)),
        ],
        out_shape=[
            jax.ShapeDtypeStruct((2 * rows, tiles * half), jnp.bfloat16),
            jax.ShapeDtypeStruct((2 * rows, tiles * FOLD), jnp.bfloat16),
            jax.ShapeDtypeStruct((2 * rows, depth), jnp.bfloat16),
        ],
        compiler_params=pltpu.CompilerParams(vmem_limit_bytes=VMEM_LIMIT),
        cost_estimate=pl.CostEstimate(
            flops=4 * rows * depth * tiles * FOLD, bytes_accessed=0, transcendentals=0
        ),
        name="feed_forward",
    )(near, far, wide, feed_grad)


def feed_backward(upstream_ref, planes_ref, feed_grad_ref, narrow_ref):
    planes = planes_ref.shape[0]
    tile_rows = FOLD // 2 // planes
    tiles = planes_ref.shape[1] // tile_rows

    @pl.when(pl.program_id(0) == 0)
    def _():
        for tile in range(tiles):
            for plane in range(planes):
                target = (tile * planes + plane) * tile_rows
                narrow_ref[target : target + tile_rows, :] = planes_ref[
                    plane, tile * tile_rows : (tile + 1) * tile_rows, :
                ]

    feed_grad_ref[...] = lax.dot_general(
        upstream_ref[...],
        narrow_ref[...],
        (((1,), (1,)), ((), ())),
        preferred_element_type=jnp.float32,
    )


def run_feed_backward(upstream, narrow):
    rows, depth = upstream.shape
    planes, narrow_rows = narrow.shape[:2]
    width = planes * narrow_rows
    steps = max(count for count in range(1, 7) if rows % (16 * count) == 0)
    block = rows // steps

    def at_step(step):
        return (step, 0)

    return pl.pallas_call(
        feed_backward,
        grid=(steps,),
        in_specs=[
            pl.BlockSpec((block, depth), at_step),
            pl.BlockSpec((planes, narrow_rows, depth), lambda step: (0, 0, 0)),
        ],
        out_specs=[
            pl.BlockSpec((block, width), at_step),
            pl.BlockSpec((width, depth), lambda step: (0, 0)),
        ],
        out_shape=[
            jax.ShapeDtypeStruct((rows, width), jnp.float32),
            jax.ShapeDtypeStruct((width, depth), jnp.bfloat16),
        ],
        compiler_params=pltpu.CompilerParams(vmem_limit_bytes=VMEM_LIMIT),
        cost_estimate=pl.CostEstimate(
            flops=2 * rows * depth * width, bytes_accessed=0, transcendentals=0
        ),
        name="feed_backward",
    )(upstream, narrow)


def pad_lanes(values, lanes):
    return jnp.pad(values, [(0, 0)] * (values.ndim - 1) + [(0, lanes - values.shape[-1])])


def contract_halves(left_near, left_far, right_near, right_far, kind=jnp.bfloat16):
    parts = [
        contract_first(left.reshape(-1, left.shape[-1]), right.reshape(-1, right.shape[-1]))
        for left, right in ((left_near, right_near), (left_far, right_far))
    ]
    return (parts[0] + parts[1]).astype(kind)


def by_channels(
    tokens,
    lengths,
    norm_gain,
    in_proj,
    conv_weight,
    conv_bias,
    gate_weight,
    gate_bias,
    decay,
    out_proj,
    mlp_gain,
    gate_up,
    down_proj,
    cotangent,
):
    planes = lax.axis_size("bucket")
    count = lax.axis_size("seq")
    me = lax.axis_index("seq")
    odd = jnp.bitwise_and(me, 1)
    inputs = tokens[0].astype(jnp.float32)
    rows, depth = inputs.shape
    own_rows = in_proj.shape[0]
    width = in_proj.shape[1] // 2
    block_width = width // NB
    held = planes // 2
    channels = held * block_width
    lanes = -(-channels // 128) * 128
    chunk_rows = conv_weight.shape[0]
    hidden_width = gate_up.shape[1] // 2 // count
    hidden_rows = down_proj.shape[0]
    taps = conv_weight.shape[1]
    slots = lengths.shape[1]

    by_row = jnp.concatenate(
        [out_proj, gate_weight, conv_weight, conv_bias[:, None], gate_bias, decay[:, None]], axis=1
    )
    by_row_width = by_row.shape[1]
    gains = jnp.pad(
        jnp.stack([norm_gain, mlp_gain], axis=1), [(0, chunk_rows - own_rows), (0, 0)]
    )
    by_row = jnp.concatenate([by_row, gains], axis=1)
    by_row = pad_lanes(by_row, -(-(by_row_width + 2) // 128) * 128)
    by_row, in_proj = lax.optimization_barrier((by_row, in_proj))
    by_row = lax.all_gather(by_row, "bucket", axis=0, tiled=False)
    proj_moves = [
        (
            2 * pair + side,
            (half * held + index) * block_width,
            half * width + ((side * held + index) * (count // 2) + pair) * block_width,
            block_width,
        )
        for pair in range(count // 2)
        for side in range(2)
        for half in range(2)
        for index in range(held)
    ]
    tile_rows = FOLD // 2 // planes
    tiles = hidden_rows // tile_rows
    wide_moves = [
        (
            member,
            ((tile * 2 + half) * planes + plane) * tile_rows,
            ((half * planes + plane) * count + member) * hidden_rows + tile * tile_rows,
            tile_rows,
        )
        for member in range(count)
        for tile in range(tiles)
        for half in range(2)
        for plane in range(planes)
    ]
    tokens_near, by_row = gather_chips(tokens[0], by_row)
    tokens_far = swap_with(tokens_near, CORE)
    proj_dealt = hand_out(in_proj, proj_moves)
    gains = by_row[:, :own_rows, by_row_width : by_row_width + 2]
    gains = lax.all_gather(gains.transpose(2, 0, 1), "seq", axis=2).astype(jnp.float32)
    gain_one, gain_two = gains.reshape(2, 1, depth)
    gate_up_late, proj_dealt = lax.optimization_barrier((gate_up, proj_dealt))
    wide_dealt = hand_out(gate_up_late, wide_moves)
    proj = lax.all_gather(proj_dealt, "bucket", axis=0, tiled=True)

    ends = jnp.cumsum(lengths[0]).astype(jnp.int32)
    info = jnp.concatenate([me[None].astype(jnp.int32), ends])

    positions = me * rows + jnp.arange(rows, dtype=jnp.int32)
    keep = (positions < ends[-1]).astype(jnp.float32)[:, None]
    upstream = keep * cotangent[0].astype(jnp.float32)
    scale_one = lax.rsqrt(jnp.mean(inputs * inputs, axis=1, keepdims=True) + norm_eps)
    kept = lax.dynamic_slice_in_dim(by_row, odd * held, held, 0)
    given = lax.dynamic_slice_in_dim(by_row, (1 - odd) * held, held, 0)
    taken = swap_with(given, 1)
    pair = jnp.where(
        odd == 0, jnp.stack([kept, taken], axis=1), jnp.stack([taken, kept], axis=1)
    )
    by_channel = pair.reshape(channels, -1)
    out = jnp.pad(by_channel[:, :depth], [(0, lanes - channels), (0, 0)])
    gate_columns = 2 * block_width
    gate_rows = by_channel[:, depth : depth + gate_columns]
    gate_blocks = []
    for index in range(held):
        part = gate_rows[index * block_width : (index + 1) * block_width]
        at = index * block_width
        gate_blocks.append(
            jnp.concatenate(
                [
                    jnp.pad(side, [(0, 0), (at, lanes - at - block_width)])
                    for side in (part[:, :block_width], part[:, block_width:])
                ],
                axis=1,
            )
        )
    gate = jnp.pad(jnp.concatenate(gate_blocks, axis=0), [(0, lanes - channels), (0, 0)])
    small = by_channel[:, depth + gate_columns : by_row_width].astype(jnp.float32).T
    decay_channel = small[taps + 3]
    rate = jnp.pad(jax.nn.softplus(decay_channel), (0, lanes - channels), constant_values=0.01)
    channel = jnp.concatenate([pad_lanes(small[: taps + 3], lanes), rate[None]], axis=0)

    def normalize(low):
        values = low.astype(jnp.float32)
        scale = lax.rsqrt(jnp.mean(values * values, axis=2, keepdims=True) + norm_eps)
        return (values * scale * gain_one).astype(jnp.bfloat16)

    wide_dealt, down_proj, gain_one = lax.optimization_barrier((wide_dealt, down_proj, gain_one))
    normed_near, normed_far = normalize(tokens_near), normalize(tokens_far)
    upstream_low, normed_near, normed_far = lax.optimization_barrier(
        (upstream.astype(jnp.bfloat16), normed_near, normed_far)
    )
    upstream_parts = send_to_chips(upstream_low, upstream_low, upstream_low)
    narrow = lax.all_gather(down_proj, "bucket", axis=0)
    wide = lax.all_gather(wide_dealt, "bucket", axis=0, tiled=True)
    gated, *saved = run_forward(
        info, normed_near, normed_far, proj, gate, channel, taps, slots
    )
    gated, *upstream_parts = lax.optimization_barrier((gated, *upstream_parts))
    upstream_near = jnp.stack([upstream_low, *upstream_parts])
    upstream_far = swap_with(upstream_near, CORE)
    gated_near, upstream_near = lax.optimization_barrier((gated[: count // 2], upstream_near))
    mixed_far, mixed_near = (
        jnp.dot(part.reshape(-1, lanes), out, preferred_element_type=jnp.float32)
        .astype(jnp.bfloat16)
        .reshape(-1, rows, depth)
        for part in (gated[count // 2 :], gated_near)
    )
    mixed, narrow = reduce_plane(mixed_near, mixed_far, late=(narrow,))
    residual = inputs + mixed
    scale_two = lax.rsqrt(jnp.mean(residual * residual, axis=1, keepdims=True) + norm_eps)
    normed_two = (residual * scale_two * gain_two).astype(jnp.bfloat16)
    two_near = gather_chips(normed_two)
    two_far = swap_with(two_near, CORE)
    upstream_all = jnp.concatenate([upstream_near, upstream_far]).reshape(-1, depth)
    feed_grad, narrow = run_feed_backward(upstream_all, narrow)
    feed, expanded_grad, two_all = run_feed_forward(
        two_near.reshape(-1, depth), two_far.reshape(-1, depth), wide, feed_grad
    )
    half_rows = two_all.shape[0] // 2

    down_part = contract_first(feed, upstream_all).astype(jnp.bfloat16)
    down_part = (
        down_part.reshape(tiles, planes, tile_rows, depth)
        .transpose(1, 0, 2, 3)
        .reshape(hidden_width, depth)
    )
    down_grad = sum_planes(down_part).astype(jnp.float32)
    part_far = contract_last(expanded_grad[half_rows:], wide).astype(jnp.bfloat16)
    part_near = contract_last(expanded_grad[:half_rows], wide).astype(jnp.bfloat16)
    normed_two_grad, two_all, feed = reduce_plane(
        part_near.reshape(-1, rows, depth), part_far.reshape(-1, rows, depth), two_all, feed
    )
    def norm_back(values, scale, gain, grad):
        scaled = grad * gain
        lean = jnp.mean(scaled * values, axis=1, keepdims=True)
        return scale * scaled - scale * scale * scale * lean * values

    residual_grad = upstream + norm_back(residual, scale_two, gain_two, normed_two_grad)
    wide_part = contract_first(two_all, expanded_grad).astype(jnp.bfloat16)
    residual_grad, wide_part, down_part = lax.optimization_barrier(
        (residual_grad, wide_part, down_part)
    )
    wide_summed = sum_planes(wide_part)
    output_far, output_near = (
        jnp.dot(part, narrow, preferred_element_type=jnp.float32)
        .astype(jnp.bfloat16)
        .reshape(-1, rows, depth)
        for part in (feed[half_rows:], feed[:half_rows])
    )
    low_near, output_near, output_far, down_grad = gather_chips(
        residual_grad.astype(jnp.bfloat16), output_near, output_far, down_grad
    )
    output_other = swap_with(output_far, CORE)
    output_sums = [
        output_near[place].astype(jnp.float32) + output_other[place].astype(jnp.float32)
        for place in range(4)
    ]
    low_far = swap_with(low_near, CORE)
    low_far, *output_low = lax.optimization_barrier(
        (low_far, *(output_sums[place].astype(jnp.bfloat16) for place in (1, 2, 3)))
    )
    output_parts = send_to_chips(*output_low)
    proj_grad, gate_grad, channel_grad = run_backward(
        info, low_near, low_far, out, gate, channel, saved, 2 * channels, taps, slots
    )
    proj_grad_near, proj_grad_far = proj_grad[: count // 2], proj_grad[count // 2 :]

    def through_proj(part):
        part = run_proj_backward(part.reshape(-1, 2 * channels), proj, signal)
        return part.reshape(-1, rows, depth)

    proj_part = contract_halves(normed_near, normed_far, proj_grad_near, proj_grad_far)
    proj_grad_far, proj_grad_near, proj_part, wide_summed = lax.optimization_barrier(
        (proj_grad_far, proj_grad_near, proj_part, wide_summed)
    )
    signal = swap_with(proj_part[:16, :128], CORE)
    part_far = through_proj(proj_grad_far)
    part_far, *output_parts = lax.optimization_barrier((part_far, *output_parts))
    mixed = residual + output_sums[0]
    for part in output_parts:
        mixed = mixed + part.astype(jnp.float32)
    mixed = (keep * mixed).astype(jnp.bfloat16)
    proj_summed = sum_planes(proj_part)
    part_near = through_proj(proj_grad_near)
    normed_grad, gated, mixed = reduce_plane(part_near, part_far, gated, mixed)

    out_grad = contract_halves(
        gated[: count // 2], gated[count // 2 :], low_near, low_far, jnp.float32
    )[:channels]
    gate_parts = []
    for index in range(held):
        at = index * block_width
        span = gate_grad[at : at + block_width]
        gate_parts.append(
            jnp.concatenate(
                [span[:, at : at + block_width], span[:, lanes + at : lanes + at + block_width]],
                axis=1,
            )
        )
    channel_grad = channel_grad[:, :channels]
    small_grad = jnp.concatenate(
        [
            channel_grad[: taps + 3],
            (channel_grad[taps + 3] * jax.nn.sigmoid(decay_channel))[None],
        ],
        axis=0,
    )
    by_row_grad = jnp.concatenate(
        [out_grad, jnp.concatenate(gate_parts, axis=0), small_grad.T], axis=1
    ).astype(jnp.bfloat16)
    by_row_grad = pad_lanes(by_row_grad, by_row.shape[2]).reshape(held, 2, chunk_rows, -1)
    kept = lax.dynamic_index_in_dim(by_row_grad, odd, 1, False)
    taken = swap_with(lax.dynamic_index_in_dim(by_row_grad, 1 - odd, 1, False), 1)
    by_row_grad = jnp.where(
        odd == 0, jnp.concatenate([kept, taken]), jnp.concatenate([taken, kept])
    ).reshape(planes * chunk_rows, -1)
    by_row_grad = sum_planes(by_row_grad)
    gate_up_grad, mlp_gain_grad = hand_back(spread_rows(wide_summed), gate_up, mlp_gain, wide_moves)
    in_proj_grad, norm_gain_grad = hand_back(spread_rows(proj_summed), in_proj, norm_gain, proj_moves)
    token_grad = residual_grad + norm_back(inputs, scale_one, gain_one, normed_grad)
    token_grad, by_row_grad = lax.optimization_barrier((token_grad, by_row_grad))
    by_row_grad = by_row_grad.astype(jnp.float32)
    out_proj_grad = by_row_grad[:, :depth]
    gate_weight_grad = by_row_grad[:, depth : depth + gate_columns]
    small_grad = by_row_grad[:, depth + gate_columns : by_row_width]
    return (
        mixed[None],
        token_grad[None],
        norm_gain_grad,
        in_proj_grad,
        small_grad[:, :taps],
        small_grad[:, taps],
        gate_weight_grad,
        small_grad[:, taps + 1 : taps + 3],
        small_grad[:, taps + 3],
        out_proj_grad,
        mlp_gain_grad,
        gate_up_grad,
        down_grad,
    )


def solution(mesh):
    planes, count = mesh.shape["bucket"], mesh.shape["seq"]
    whole_blocks = count == 8 and planes % 2 == 0 and planes * count == 2 * NB
    return jax.shard_map(
        by_channels if whole_blocks else on_device,
        mesh=mesh,
        in_specs=(
            P("bucket", "seq", None),
            P("bucket", None),
            P(("bucket", "seq")),
            P(("bucket", "seq"), None),
            P(("bucket", "seq"), None),
            P(("bucket", "seq")),
            P(("bucket", "seq"), None),
            P(("bucket", "seq"), None),
            P(("bucket", "seq")),
            P(("bucket", "seq"), None),
            P(("bucket", "seq")),
            P(("bucket", "seq"), None),
            P(("bucket", "seq"), None),
            P("bucket", "seq", None),
        ),
        out_specs=(
            P("bucket", "seq", None),
            P("bucket", "seq", None),
            P(("bucket", "seq")),
            P(("bucket", "seq"), None),
            P(("bucket", "seq"), None),
            P(("bucket", "seq")),
            P(("bucket", "seq"), None),
            P(("bucket", "seq"), None),
            P(("bucket", "seq")),
            P(("bucket", "seq"), None),
            P(("bucket", "seq")),
            P(("bucket", "seq"), None),
            P(("bucket", "seq"), None),
        ),
        check_vma=False,
    )
```

```python
from functools import partial

import jax
import jax.numpy as jnp
from jax import lax
from jax.experimental import pallas as pl
from jax.experimental.pallas import tpu as pltpu
from jax.sharding import PartitionSpec as P

NB = 16


norm_eps = 1e-06
gate_scale = 8.0


def from_behind(block, axis, distance):
    devices = range(lax.axis_size(axis))
    route = [(i - distance, i) for i in devices if i - distance in devices]
    return lax.ppermute(block, axis, route)


def entering(part, axis, combine, identity, reverse):
    count = lax.axis_size(axis)
    place = lax.axis_index(axis)
    ahead = count - 1 - place if reverse else place
    gathered = jax.tree.map(lambda a: lax.all_gather(a, axis), part)
    state = jax.tree.map(lambda a, e: jnp.zeros_like(a) + jnp.asarray(e, a.dtype), part, identity)

    def one(lap, state):
        source = count - 1 - lap if reverse else lap
        return combine(
            state, jax.tree.map(lambda a: lax.dynamic_index_in_dim(a, source, 0, False), gathered)
        )

    return lax.fori_loop(0, ahead, one, state)


def rms_scale(values, gain):
    return values * lax.rsqrt(jnp.mean(values * values, axis=1, keepdims=True) + norm_eps) * gain


def link(earlier, later):
    return (earlier[0] * later[0], later[0] * earlier[1] + later[1])


def segment_layout(lengths_row, positions):
    ends = jnp.cumsum(lengths_row)
    segment_ids = jnp.sum((positions[:, None] >= ends[None, :]).astype(jnp.int32), axis=1)
    segment_ids = jnp.where(positions < 0, -1, segment_ids)
    keep = (positions < ends[-1]).astype(jnp.float32)
    return (segment_ids, keep)


def lru_terms(conv_out, gate_a, gate_i, decay, starts):
    rate = jax.nn.softplus(decay)
    log_step = -gate_scale * jax.nn.sigmoid(gate_a) * rate
    decay_step = jnp.where(starts, 0.0, jnp.exp(log_step))
    scaling = jnp.where(starts, 1.0, jnp.sqrt(-jnp.expm1(2.0 * log_step)))
    return (decay_step, conv_out * jax.nn.sigmoid(gate_i) * scaling)


def gated_gelu(values, split):
    return jax.nn.gelu(values[:, :split]) * values[:, split:]


def contract_last(left, right):
    return lax.dot_general(
        left, right, (((1,), (1,)), ((), ())), preferred_element_type=jnp.float32
    )


def contract_first(left, right):
    return lax.dot_general(
        left, right, (((0,), (0,)), ((), ())), preferred_element_type=jnp.float32
    )


def row_product(left, right):
    return contract_first(left, right)


def on_device(
    tokens,
    lengths,
    norm_gain,
    in_proj,
    conv_weight,
    conv_bias,
    gate_weight,
    gate_bias,
    decay,
    out_proj,
    mlp_gain,
    gate_up,
    down_proj,
    cotangent,
):
    inputs = tokens[0].astype(jnp.float32)
    tok_rows = inputs.shape[0]
    width = in_proj.shape[1] // 2
    ff_width = gate_up.shape[1] // 2
    block_width = width // NB
    kernel = conv_weight.shape[1]
    rim_rows = kernel - 1
    (
        gain_one_all,
        proj_all,
        conv_all,
        conv_bias_all,
        gate_all,
        gate_bias_all,
        decay_all,
        out_all,
        gain_two_all,
    ) = (
        lax.all_gather(norm_gain, ("bucket", "seq"), axis=0, tiled=True),
        lax.all_gather(in_proj, ("bucket", "seq"), axis=0, tiled=True),
        lax.all_gather(conv_weight, ("bucket", "seq"), axis=0, tiled=True),
        lax.all_gather(conv_bias, ("bucket", "seq"), axis=0, tiled=True),
        lax.all_gather(gate_weight, ("bucket", "seq"), axis=0, tiled=True),
        lax.all_gather(gate_bias, ("bucket", "seq"), axis=0, tiled=True),
        lax.all_gather(decay, ("bucket", "seq"), axis=0, tiled=True),
        lax.all_gather(out_proj, ("bucket", "seq"), axis=0, tiled=True),
        lax.all_gather(mlp_gain, ("bucket", "seq"), axis=0, tiled=True),
    )
    seq_index = lax.axis_index("seq")
    positions = seq_index * tok_rows + jnp.arange(tok_rows, dtype=jnp.int32)
    lengths_row = lengths[0]
    segment_ids, keep = segment_layout(lengths_row, positions)
    back_ids = segment_layout(lengths_row, positions - 1)[0]
    starts = (segment_ids != back_ids)[:, None]
    normed, norm_pull = jax.vjp(rms_scale, inputs, gain_one_all.astype(jnp.float32))
    normed_low = normed.astype(jnp.bfloat16)
    projected = jnp.dot(normed_low, proj_all, preferred_element_type=jnp.float32)
    mixer_in = projected[:, :width].astype(jnp.bfloat16)
    branch = projected[:, width:]
    rim = from_behind(mixer_in[tok_rows - rim_rows :], "seq", 1)
    extended = jnp.concatenate([rim, mixer_in], axis=0)
    conv_float = conv_all.astype(jnp.float32)
    lagged_terms = []
    convolved = jnp.zeros((tok_rows, width), jnp.float32) + conv_bias_all.astype(jnp.float32)
    for offset in range(kernel):
        earlier_ids = segment_layout(lengths_row, positions - offset)[0]
        lagged = jnp.where(
            (earlier_ids == segment_ids)[:, None],
            extended[rim_rows - offset : rim_rows - offset + tok_rows].astype(jnp.float32),
            0.0,
        )
        lagged_terms.append(lagged)
        convolved = convolved + lagged * conv_float[:, offset]
    conv_out = convolved.astype(jnp.bfloat16)
    gates = jnp.einsum(
        "tnc,ncd->tnd",
        conv_out.reshape(tok_rows, NB, block_width),
        gate_all.reshape(NB, block_width, 2 * block_width),
        preferred_element_type=jnp.float32,
    )
    gate_bias_float = gate_bias_all.astype(jnp.float32)
    gate_a = gates[:, :, :block_width].reshape(tok_rows, width) + gate_bias_float[:, 0]
    gate_i = gates[:, :, block_width:].reshape(tok_rows, width) + gate_bias_float[:, 1]
    (decay_step, normalized), lru_pull = jax.vjp(
        partial(lru_terms, starts=starts),
        conv_out.astype(jnp.float32),
        gate_a,
        gate_i,
        decay_all.astype(jnp.float32),
    )
    prefix_decay, prefix_state = lax.associative_scan(link, (decay_step, normalized), axis=0)
    carried = entering(
        (prefix_decay[-1], prefix_state[-1]),
        "seq",
        link,
        (jnp.ones((width,), jnp.float32), jnp.zeros((width,), jnp.float32)),
        False,
    )
    state_in = carried[1]
    hidden = prefix_state + prefix_decay * state_in
    branch_act, branch_pull = jax.vjp(jax.nn.gelu, branch)
    gated = (hidden * branch_act).astype(jnp.bfloat16)
    residual = inputs + jnp.dot(gated, out_all, preferred_element_type=jnp.float32)
    normed_two, norm_two_pull = jax.vjp(rms_scale, residual, gain_two_all.astype(jnp.float32))
    normed_two_low = normed_two.astype(jnp.bfloat16)
    gate_up_all, down_all = (
        lax.all_gather(gate_up, ("bucket", "seq"), axis=0, tiled=True),
        lax.all_gather(down_proj, ("bucket", "seq"), axis=0, tiled=True),
    )
    expanded = jnp.dot(normed_two_low, gate_up_all, preferred_element_type=jnp.float32)
    feed, feed_pull = jax.vjp(partial(gated_gelu, split=ff_width), expanded)
    feed_low = feed.astype(jnp.bfloat16)
    output_rows = residual + jnp.dot(feed_low, down_all, preferred_element_type=jnp.float32)
    mixed = (keep[:, None] * output_rows).astype(jnp.bfloat16)
    upstream = keep[:, None] * cotangent[0].astype(jnp.float32)
    upstream_low = upstream.astype(jnp.bfloat16)
    down_grad = lax.psum_scatter(
        row_product(feed_low, upstream_low), ("bucket", "seq"), scatter_dimension=0, tiled=True
    )
    feed_grad = contract_last(upstream_low, down_all)
    expanded_grad = feed_pull(feed_grad)[0].astype(jnp.bfloat16)
    gate_up_grad = lax.psum_scatter(
        row_product(normed_two_low, expanded_grad),
        ("bucket", "seq"),
        scatter_dimension=0,
        tiled=True,
    )
    normed_two_grad = contract_last(expanded_grad, gate_up_all)
    residual_part, gain_two_grad = norm_two_pull(normed_two_grad)
    residual_grad = upstream + residual_part
    residual_low = residual_grad.astype(jnp.bfloat16)
    out_grad = contract_first(gated, residual_low)
    gated_grad = contract_last(residual_low, out_all)
    hidden_grad = gated_grad * branch_act
    branch_grad = branch_pull(gated_grad * hidden)[0]
    next_decay = jnp.concatenate([decay_step[1:], jnp.ones((1, width), jnp.float32)], axis=0)
    suffix_decay, suffix_state = lax.associative_scan(
        link, (next_decay, hidden_grad), reverse=True, axis=0
    )
    returned = entering(
        (prefix_decay[-1], decay_step[0] * suffix_state[0]),
        "seq",
        link,
        (jnp.ones((width,), jnp.float32), jnp.zeros((width,), jnp.float32)),
        True,
    )
    incoming = returned[1]
    state_grad = suffix_state + suffix_decay * incoming
    state_before = jnp.concatenate([state_in[None, :], hidden[:-1]], axis=0)
    conv_grad_lru, gate_a_grad, gate_i_grad, decay_grad = lru_pull(
        (state_grad * state_before, state_grad)
    )
    gates_low = jnp.concatenate(
        [
            gate_a_grad.reshape(tok_rows, NB, block_width),
            gate_i_grad.reshape(tok_rows, NB, block_width),
        ],
        axis=2,
    ).astype(jnp.bfloat16)
    gate_grad = jnp.einsum(
        "tnc,tnd->ncd",
        conv_out.reshape(tok_rows, NB, block_width),
        gates_low,
        preferred_element_type=jnp.float32,
    ).reshape(width, 2 * block_width)
    bias_sums = jnp.sum(gates_low.astype(jnp.float32), axis=0)
    gate_bias_grad = jnp.stack(
        [bias_sums[:, :block_width].reshape(width), bias_sums[:, block_width:].reshape(width)],
        axis=1,
    )
    conv_grad_gates = jnp.einsum(
        "tnd,ncd->tnc",
        gates_low,
        gate_all.reshape(NB, block_width, 2 * block_width),
        preferred_element_type=jnp.float32,
    ).reshape(tok_rows, width)
    conv_low = (conv_grad_lru + conv_grad_gates).astype(jnp.bfloat16)
    head = from_behind(conv_low[:rim_rows], "seq", -1)
    trailing = jnp.concatenate([conv_low, head], axis=0)
    conv_low_float = conv_low.astype(jnp.float32)
    mixer_grad = jnp.zeros((tok_rows, width), jnp.float32)
    tap_grads = []
    for offset in range(kernel):
        later_ids = segment_layout(lengths_row, positions + offset)[0]
        ahead = jnp.where(
            (later_ids == segment_ids)[:, None],
            trailing[offset : offset + tok_rows].astype(jnp.float32),
            0.0,
        )
        mixer_grad = mixer_grad + ahead * conv_float[:, offset]
        tap_grads.append(jnp.sum(conv_low_float * lagged_terms[offset], axis=0))
    conv_weight_grad = jnp.stack(tap_grads, axis=1)
    conv_bias_grad = jnp.sum(conv_low_float, axis=0)
    proj_grad_low = jnp.concatenate([mixer_grad, branch_grad], axis=1).astype(jnp.bfloat16)
    in_proj_grad = contract_first(normed_low, proj_grad_low)
    normed_grad = contract_last(proj_grad_low, proj_all)
    input_part, gain_one_grad = norm_pull(normed_grad)
    token_grad = residual_grad + input_part
    summed = (
        lax.psum_scatter(gain_one_grad, ("bucket", "seq"), scatter_dimension=0, tiled=True),
        lax.psum_scatter(in_proj_grad, ("bucket", "seq"), scatter_dimension=0, tiled=True),
        lax.psum_scatter(conv_weight_grad, ("bucket", "seq"), scatter_dimension=0, tiled=True),
        lax.psum_scatter(conv_bias_grad, ("bucket", "seq"), scatter_dimension=0, tiled=True),
        lax.psum_scatter(gate_grad, ("bucket", "seq"), scatter_dimension=0, tiled=True),
        lax.psum_scatter(gate_bias_grad, ("bucket", "seq"), scatter_dimension=0, tiled=True),
        lax.psum_scatter(decay_grad, ("bucket", "seq"), scatter_dimension=0, tiled=True),
        lax.psum_scatter(out_grad, ("bucket", "seq"), scatter_dimension=0, tiled=True),
        lax.psum_scatter(gain_two_grad, ("bucket", "seq"), scatter_dimension=0, tiled=True),
    )
    return (
        mixed[None],
        token_grad[None],
        summed[0],
        summed[1],
        summed[2],
        summed[3],
        summed[4],
        summed[5],
        summed[6],
        summed[7],
        summed[8],
        gate_up_grad,
        down_grad,
    )


def swap_with(block, mask):
    route = [(i, i ^ mask) for i in range(lax.axis_size("seq"))]
    return lax.ppermute(block, "seq", route)


CORE, ACROSS_X, ACROSS_Y = 1, 2, 4


def split_row(rows):
    return rows // 32 * 16


def gather_chips(block, *others):
    split = split_row(block.shape[0])
    across_x, across_y = swap_with(block, ACROSS_X), swap_with(block, ACROSS_Y)
    if others:
        across_x, across_y, *others = lax.optimization_barrier((across_x, across_y, *others))
    both = [swap_with(across_y[:split], ACROSS_X), swap_with(across_x[split:], ACROSS_Y)]
    near = jnp.concatenate([block, across_x, across_y, *both]).reshape(4, *block.shape)
    return (near, *others) if others else near


def send_to_chips(across_x, across_y, across_both):
    return [
        swap_with(across_x, ACROSS_X),
        swap_with(across_y, ACROSS_Y),
        swap_with(across_both, ACROSS_X + ACROSS_Y),
    ]


def reduce_plane(near, far, *others, late=()):
    other = swap_with(far, CORE)
    rows = near.shape[1]
    split = split_row(rows)

    def total(place, span=slice(None)):
        return near[place, span].astype(jnp.float32) + other[place, span].astype(jnp.float32)

    both = total(3).astype(jnp.bfloat16)
    both, *others = lax.optimization_barrier((both, *others))
    first = swap_with(both[:split], ACROSS_Y).astype(jnp.float32)
    second = swap_with(both[split:], ACROSS_X).astype(jnp.float32)
    across_x = jnp.concatenate([total(1, slice(split)) + first, total(1, slice(split, None))])
    across_y = jnp.concatenate([total(2, slice(split)), total(2, slice(split, None)) + second])
    across_x, across_y = across_x.astype(jnp.bfloat16), across_y.astype(jnp.bfloat16)
    across_x, across_y, *late = lax.optimization_barrier((across_x, across_y, *late))
    others += late
    across_x = swap_with(across_x, ACROSS_X).astype(jnp.float32)
    across_y = swap_with(across_y, ACROSS_Y).astype(jnp.float32)
    result = total(0) + across_x + across_y
    return (result, *others) if others else result


def reduce_plane_at_once(near, far, *others):
    other = swap_with(far, CORE)

    def total(place):
        return near[place].astype(jnp.float32) + other[place].astype(jnp.float32)

    *parts, others = lax.optimization_barrier(
        (*(total(place).astype(jnp.bfloat16) for place in (1, 2, 3)), others)
    )
    sent = send_to_chips(*parts)

    def finish(*late):
        *parts, late = lax.optimization_barrier((*sent, late))
        result = total(0)
        for part in parts:
            result = result + part.astype(jnp.float32)
        return (result, *late) if late else result

    return (finish, *others)


def split_mixer_rows(joined_ref, out_ref, gate_ref, small_ref):
    depth, gates = out_ref.shape[1], gate_ref.shape[1]
    joined = joined_ref[...].astype(jnp.float32)
    out_ref[...] = joined[:, :depth]
    gate_ref[...] = joined[:, depth : depth + gates]
    small_ref[...] = joined[:, depth + gates : depth + gates + small_ref.shape[1]]


def place_of(chunk, me, count):
    relative = jnp.bitwise_xor(chunk, me)
    return jnp.bitwise_and(relative, 1), jnp.right_shift(relative, 1)


def series_expm1(values):
    total = 1.0 + values * (1.0 / 7.0)
    for term in (6, 5, 4, 3, 2):
        total = 1.0 + values * (1.0 / term) * total
    return values * total


def segment_reach(info_ref, first, slots, shape, total):
    positions = first + lax.broadcasted_iota(jnp.int32, shape, 0)
    begin = jnp.zeros(shape, jnp.int32)
    finish = jnp.full(shape, total, jnp.int32)
    for slot in range(slots):
        end = info_ref[1 + slot]
        passed = positions >= end
        begin = jnp.where(passed, jnp.maximum(begin, end), begin)
        finish = jnp.where(passed, finish, jnp.minimum(finish, end))
    return positions - begin, finish - positions


def widen(mask, lanes):
    return jnp.concatenate([mask] * (lanes // mask.shape[1]), axis=1)


def gelu_parts(values):
    inner = 0.7978845608028654 * (values + 0.044715 * values * values * values)
    bent = jnp.tanh(inner)
    half = 0.5 * (1.0 + bent)
    slope = half + 0.5 * values * (1.0 - bent * bent) * 0.7978845608028654 * (
        1.0 + 3.0 * 0.044715 * values * values
    )
    return values * half, slope


ROWS = 8


def tiles_at_once(tiles):
    return max(size for size in range(1, GROUP + 1) if tiles % size == 0)


def group_tiles(index, group):
    return [index * group + member for member in range(group)]


GROUP = 11
TAP, BIAS, BIAS_A, BIAS_I, RATE = 0, 4, 5, 6, 7


def mixer_forward(
    taps,
    slots,
    info_ref,
    near_ref,
    far_ref,
    proj_ref,
    gate_ref,
    channel_ref,
    gated_ref,
    lagging_ref,
    conv_ref,
    act_ref,
    slope_ref,
    decay_ref,
    rate_part_ref,
    gate_i_part_ref,
    conv_part_ref,
    gate_r_ref,
    lag_edge_ref,
    proj_wide,
    projected,
    convolved,
    gates,
    carry,
    edge,
):
    chunk = pl.program_id(0)
    is_far, _ = place_of(chunk, info_ref[0], pl.num_programs(0))
    rows, lanes = convolved.shape
    tiles = rows // ROWS
    group = tiles_at_once(tiles)
    total = rows * pl.num_programs(0)

    @pl.when(chunk == 0)
    def _():
        carry[...] = jnp.zeros_like(carry)
        edge[...] = jnp.zeros_like(edge)
        channels = proj_ref.shape[1] // 2
        proj_wide[...] = jnp.zeros_like(proj_wide)
        proj_wide[:, :channels] = proj_ref[:, :channels]
        proj_wide[:, lanes : lanes + channels] = proj_ref[:, channels:]

    def project(normed_ref):
        product = jnp.dot(normed_ref[0], proj_wide[...], preferred_element_type=jnp.float32)
        low = product[:, :lanes].astype(jnp.bfloat16)
        lagging_ref[0] = low
        projected[:, :lanes] = low.astype(jnp.float32)
        projected[:, lanes:] = product[:, lanes:]

    pl.when(is_far == 0)(lambda: project(near_ref))
    pl.when(is_far == 1)(lambda: project(far_ref))
    place = lax.broadcasted_iota(jnp.int32, (ROWS, lanes), 0)

    def convolve(tile, before):
        for tile in group_tiles(tile, group):
            before = convolve_tile(tile, before)
        return before

    def convolve_tile(tile, before):
        at = pl.ds(pl.multiple_of(tile * ROWS, ROWS), ROWS)
        here = projected[at, :lanes]
        since, _ = segment_reach(info_ref, chunk * rows + tile * ROWS, slots, (ROWS, 128), total)
        value = channel_ref[BIAS : BIAS + 1, :] + here * channel_ref[TAP : TAP + 1, :]
        for lag in range(1, taps):
            moved = jnp.where(
                place < lag, pltpu.roll(before, lag, 0), pltpu.roll(here, lag, 0)
            )
            value = value + jnp.where(widen(since >= lag, lanes), moved, 0.0) * (
                channel_ref[TAP + lag : TAP + lag + 1, :]
            )
        convolved[at, :] = value
        return here

    last = lax.fori_loop(0, tiles // group, convolve, edge[...])
    edge[...] = last
    lag_edge_ref[0] = last
    conv_low = convolved[...].astype(jnp.bfloat16)
    conv_ref[0] = conv_low
    convolved[...] = conv_low.astype(jnp.float32)
    gates[...] = jnp.dot(conv_low, gate_ref[...], preferred_element_type=jnp.float32)

    def recur(tile, state):
        parts = [local_scan(tile) for tile in group_tiles(tile, group)]
        for at, value, decay, activated, slope, ratio, gate in parts:
            hidden = value + decay * state
            before = jnp.where(place == 0, state, pltpu.roll(hidden, 1, 0))
            state = jnp.broadcast_to(hidden[ROWS - 1 :], hidden.shape)
            projected[at, :lanes] = hidden * activated
            slope_ref[0, at, :] = hidden * slope
            rate_part_ref[0, at, :] = gate * (before - ratio)
        return state

    def local_scan(tile):
        at = pl.ds(pl.multiple_of(tile * ROWS, ROWS), ROWS)
        since, _ = segment_reach(info_ref, chunk * rows + tile * ROWS, slots, (ROWS, 128), total)
        starts = widen(since == 0, lanes)
        gate_r = jax.nn.sigmoid(gates[at, :lanes] + channel_ref[BIAS_A : BIAS_A + 1, :])
        gate_i = jax.nn.sigmoid(gates[at, lanes:] + channel_ref[BIAS_I : BIAS_I + 1, :])
        less = series_expm1(-gate_scale * gate_r * channel_ref[RATE : RATE + 1, :])
        plain = 1.0 + less
        root = jnp.sqrt(-less * (2.0 + less))
        decay = jnp.where(starts, 0.0, plain)
        scaling = jnp.where(starts, 1.0, root)
        conv = convolved[at, :]
        admitted = conv * gate_i
        value = admitted * scaling
        decay_ref[0, at, :] = decay
        conv_part_ref[0, at, :] = gate_i * scaling
        gate_i_part_ref[0, at, :] = value * (1.0 - gate_i)
        gate_r_ref[0, at, :] = 1.0 - gate_r
        ratio = admitted * plain / root
        gate = decay * gate_r
        for step in (1, 2, 4):
            inside = place >= step
            value = value + jnp.where(inside, decay * pltpu.roll(value, step, 0), 0.0)
            decay = jnp.where(inside, decay * pltpu.roll(decay, step, 0), decay)
        activated, slope = gelu_parts(projected[at, lanes:])
        act_ref[0, at, :] = activated
        return at, value, decay, activated, slope, ratio, gate

    carry[...] = lax.fori_loop(0, tiles // group, recur, carry[...])
    gated_ref[0] = projected[:, :lanes].astype(jnp.bfloat16)


def mixer_backward(
    taps,
    slots,
    info_ref,
    near_ref,
    far_ref,
    out_ref,
    gate_ref,
    channel_ref,
    act_ref,
    slope_ref,
    decay_ref,
    rate_part_ref,
    gate_i_part_ref,
    conv_part_ref,
    gate_r_ref,
    conv_ref,
    lagging_ref,
    lag_edge_ref,
    projected_near_ref,
    projected_far_ref,
    gate_grad_ref,
    channel_grad_ref,
    coming,
    conv_part,
    lagged,
    gates,
    projected,
    conv_grad,
    grad_carry,
    decay_carry,
    sums,
):
    lap = pl.program_id(0)
    laps = pl.num_programs(0)
    chunk = laps - 1 - lap
    is_far, _ = place_of(chunk, info_ref[0], laps)
    rows, lanes = conv_part.shape
    tiles = rows // ROWS
    group = tiles_at_once(tiles)
    total = rows * laps

    @pl.when(lap == 0)
    def _():
        grad_carry[...] = jnp.zeros_like(grad_carry)
        decay_carry[...] = jnp.zeros_like(decay_carry)
        conv_grad[...] = jnp.zeros_like(conv_grad)
        sums[...] = jnp.zeros_like(sums)
        gate_grad_ref[...] = jnp.zeros_like(gate_grad_ref)

    def expand(down_ref):
        coming[...] = lax.dot_general(
            down_ref[0], out_ref[...], (((1,), (1,)), ((), ())), preferred_element_type=jnp.float32
        )

    pl.when(is_far == 0)(lambda: expand(near_ref))
    pl.when(is_far == 1)(lambda: expand(far_ref))
    lagged[...] = lagging_ref[0].astype(jnp.float32)
    place = lax.broadcasted_iota(jnp.int32, (ROWS, lanes), 0)

    def recur(step_index, carried):
        later_grad, later_decay, sum_a, sum_i, sum_rate = carried
        members = group_tiles(tiles // group - 1 - step_index, group)[::-1]
        parts = []
        for tile in members:
            part = local_scan(tile, later_decay)
            later_decay = part[-1]
            parts.append(part)
        for at, value, weight, _ in parts:
            grad = value + weight * later_grad
            later_grad = jnp.broadcast_to(grad[:1], grad.shape)
            conv_part[at, :] = grad * conv_part_ref[0, at, :]
            grad_i = grad * gate_i_part_ref[0, at, :]
            grad_rate = grad * rate_part_ref[0, at, :]
            grad_a = (-gate_scale * channel_ref[RATE : RATE + 1, :]) * grad_rate * gate_r_ref[0, at, :]
            grad_a = grad_a.astype(jnp.bfloat16).astype(jnp.float32)
            grad_i = grad_i.astype(jnp.bfloat16).astype(jnp.float32)
            gates[at, :lanes] = grad_a
            gates[at, lanes:] = grad_i
            sum_a = sum_a + grad_a
            sum_i = sum_i + grad_i
            sum_rate = sum_rate - gate_scale * grad_rate
        return later_grad, later_decay, sum_a, sum_i, sum_rate

    def local_scan(tile, later_decay):
        at = pl.ds(pl.multiple_of(tile * ROWS, ROWS), ROWS)
        decay = decay_ref[0, at, :]
        down = coming[at, :]
        value = down * act_ref[0, at, :]
        projected[at, lanes:] = down * slope_ref[0, at, :]
        weight = jnp.where(place == ROWS - 1, later_decay, pltpu.roll(decay, ROWS - 1, 0))
        for step in (1, 2, 4):
            inside = place < ROWS - step
            value = value + jnp.where(inside, weight * pltpu.roll(value, ROWS - step, 0), 0.0)
            weight = jnp.where(inside, weight * pltpu.roll(weight, ROWS - step, 0), weight)
        return at, value, weight, jnp.broadcast_to(decay[:1], decay.shape)

    empty = jnp.zeros((ROWS, lanes), jnp.float32)
    grad_last, decay_last, sum_a, sum_i, sum_rate = lax.fori_loop(
        0, tiles // group, recur, (grad_carry[...], decay_carry[...], empty, empty, empty)
    )
    grad_carry[...] = grad_last
    decay_carry[...] = decay_last
    gates_low = gates[...].astype(jnp.bfloat16)
    gate_grad_ref[...] += lax.dot_general(
        conv_ref[0], gates_low, (((0,), (0,)), ((), ())), preferred_element_type=jnp.float32
    )
    from_gates = lax.dot_general(
        gates_low, gate_ref[...], (((1,), (1,)), ((), ())), preferred_element_type=jnp.float32
    )
    conv_grad[rows:, :] = conv_grad[:ROWS, :]
    conv_grad[:rows, :] = (conv_part[...] + from_gates).astype(jnp.bfloat16).astype(jnp.float32)

    def unconvolve(tile, carried):
        for tile in group_tiles(tile, group):
            carried = unconvolve_tile(tile, carried)
        return carried

    def unconvolve_tile(tile, carried):
        earlier, sum_bias, sum_taps = carried
        at = pl.ds(pl.multiple_of(tile * ROWS, ROWS), ROWS)
        beyond = pl.ds(pl.multiple_of((tile + 1) * ROWS, ROWS), ROWS)
        since, until = segment_reach(
            info_ref, chunk * rows + tile * ROWS, slots, (ROWS, 128), total
        )
        here = lagged[at, :]
        grad = conv_grad[at, :]
        later = conv_grad[beyond, :]
        value = grad * channel_ref[TAP : TAP + 1, :]
        new_taps = [sum_taps[0] + grad * here]
        for lag in range(1, taps):
            ahead = jnp.where(
                place < ROWS - lag, pltpu.roll(grad, ROWS - lag, 0), pltpu.roll(later, ROWS - lag, 0)
            )
            value = value + jnp.where(widen(until > lag, lanes), ahead, 0.0) * (
                channel_ref[TAP + lag : TAP + lag + 1, :]
            )
            moved = jnp.where(
                place < lag, pltpu.roll(earlier, lag, 0), pltpu.roll(here, lag, 0)
            )
            new_taps.append(
                sum_taps[lag] + grad * jnp.where(widen(since >= lag, lanes), moved, 0.0)
            )
        projected[at, :lanes] = value
        return here, sum_bias + grad, tuple(new_taps)

    _, sum_bias, sum_taps = lax.fori_loop(
        0, tiles // group, unconvolve, (lag_edge_ref[0], empty, (empty,) * taps)
    )
    low = projected[...].astype(jnp.bfloat16)

    def project_back(projected_ref):
        channels = projected_ref.shape[2] // 2
        projected_ref[0, :, :channels] = low[:, :channels]
        projected_ref[0, :, channels:] = low[:, lanes : lanes + channels]

    pl.when(is_far == 0)(lambda: project_back(projected_near_ref))
    pl.when(is_far == 1)(lambda: project_back(projected_far_ref))
    for place_in, part in enumerate((*sum_taps, sum_bias, sum_a, sum_i, sum_rate)):
        sums[place_in] += part

    @pl.when(lap == laps - 1)
    def _():
        channel_grad_ref[...] = jnp.sum(sums[...], axis=1)


VMEM_LIMIT = 56 * 1024 * 1024


def run_forward(info, near, far, proj, gate, channels, taps, slots):
    chips, rows, depth = near.shape
    count = 2 * chips
    lanes = gate.shape[0]

    def at_chip(chunk, info_ref):
        return (place_of(chunk, info_ref[0], count)[1], 0, 0)

    def at_place(chunk, info_ref):
        is_far, chip = place_of(chunk, info_ref[0], count)
        return (is_far * chips + chip, 0, 0)

    def at_chunk(chunk, info_ref):
        return (chunk, 0, 0)

    def whole(chunk, info_ref):
        return (0, 0)

    def block(kind):
        return jax.ShapeDtypeStruct((count, rows, lanes), kind)

    wide = pl.BlockSpec((1, rows, depth), at_chip)
    narrow = pl.BlockSpec((1, rows, lanes), at_place)
    return pl.pallas_call(
        partial(mixer_forward, taps, slots),
        grid_spec=pltpu.PrefetchScalarGridSpec(
            num_scalar_prefetch=1,
            grid=(count,),
            in_specs=[
                wide,
                wide,
                pl.BlockSpec(proj.shape, whole),
                pl.BlockSpec(gate.shape, whole),
                pl.BlockSpec(channels.shape, whole),
            ],
            out_specs=[narrow] * 10 + [pl.BlockSpec((1, ROWS, lanes), at_chunk)],
            scratch_shapes=[
                pltpu.VMEM((depth, 2 * lanes), jnp.bfloat16),
                pltpu.VMEM((rows, 2 * lanes), jnp.float32),
                pltpu.VMEM((rows, lanes), jnp.float32),
                pltpu.VMEM((rows, 2 * lanes), jnp.float32),
                pltpu.VMEM((ROWS, lanes), jnp.float32),
                pltpu.VMEM((ROWS, lanes), jnp.float32),
            ],
        ),
        out_shape=[block(jnp.bfloat16)] * 3
        + [block(jnp.float32)] * 7
        + [jax.ShapeDtypeStruct((count, ROWS, lanes), jnp.float32)],
        compiler_params=pltpu.CompilerParams(
            dimension_semantics=("arbitrary",), vmem_limit_bytes=VMEM_LIMIT
        ),
        cost_estimate=pl.CostEstimate(flops=0, bytes_accessed=0, transcendentals=0),
        name="mixer_forward",
    )(info, near, far, proj, gate, channels)


def run_backward(info, near, far, out, gate, channels, saved, proj_columns, taps, slots):
    lagging, conv, *parts, lag_edge = saved
    chips, rows, depth = near.shape
    count = 2 * chips
    lanes = gate.shape[0]

    def at_chip(lap, info_ref):
        return (place_of(count - 1 - lap, info_ref[0], count)[1], 0, 0)

    def at_place(lap, info_ref):
        is_far, chip = place_of(count - 1 - lap, info_ref[0], count)
        return (is_far * chips + chip, 0, 0)

    def before(lap, info_ref):
        return (jnp.maximum(count - 2 - lap, 0), 0, 0)

    def whole(lap, info_ref):
        return (0, 0)

    wide = pl.BlockSpec((1, rows, depth), at_chip)
    narrow = pl.BlockSpec((1, rows, lanes), at_place)
    rim = pl.BlockSpec((1, ROWS, lanes), before)
    sums = taps + 4
    return pl.pallas_call(
        partial(mixer_backward, taps, slots),
        grid_spec=pltpu.PrefetchScalarGridSpec(
            num_scalar_prefetch=1,
            grid=(count,),
            in_specs=[
                wide,
                wide,
                pl.BlockSpec(out.shape, whole),
                pl.BlockSpec(gate.shape, whole),
                pl.BlockSpec(channels.shape, whole),
            ]
            + [narrow] * 9
            + [rim],
            out_specs=[
                pl.BlockSpec((1, rows, proj_columns), at_chip),
                pl.BlockSpec((1, rows, proj_columns), at_chip),
                pl.BlockSpec((lanes, 2 * lanes), whole),
                pl.BlockSpec((sums, lanes), whole),
            ],
            scratch_shapes=[
                pltpu.VMEM((rows, lanes), jnp.float32),
                pltpu.VMEM((rows, lanes), jnp.float32),
                pltpu.VMEM((rows, lanes), jnp.float32),
                pltpu.VMEM((rows, 2 * lanes), jnp.float32),
                pltpu.VMEM((rows, 2 * lanes), jnp.float32),
                pltpu.VMEM((rows + ROWS, lanes), jnp.float32),
                pltpu.VMEM((ROWS, lanes), jnp.float32),
                pltpu.VMEM((ROWS, lanes), jnp.float32),
                pltpu.VMEM((sums, ROWS, lanes), jnp.float32),
            ],
        ),
        out_shape=[
            jax.ShapeDtypeStruct((chips, rows, proj_columns), jnp.bfloat16),
            jax.ShapeDtypeStruct((chips, rows, proj_columns), jnp.bfloat16),
            jax.ShapeDtypeStruct((lanes, 2 * lanes), jnp.float32),
            jax.ShapeDtypeStruct((sums, lanes), jnp.float32),
        ],
        compiler_params=pltpu.CompilerParams(
            dimension_semantics=("arbitrary",), vmem_limit_bytes=VMEM_LIMIT
        ),
        cost_estimate=pl.CostEstimate(flops=0, bytes_accessed=0, transcendentals=0),
        name="mixer_backward",
    )(info, near, far, out, gate, channels, *parts, conv, lagging, lag_edge)


def proj_backward(part_ref, proj_ref, signal_ref, normed_ref):
    normed_ref[...] = lax.dot_general(
        part_ref[...], proj_ref[...], (((1,), (1,)), ((), ())), preferred_element_type=jnp.float32
    ).astype(jnp.bfloat16)


def run_proj_backward(part, proj, signal):
    rows, columns = part.shape
    steps = max(count for count in (3, 2, 1) if rows % (16 * count) == 0)
    return pl.pallas_call(
        proj_backward,
        grid=(steps,),
        in_specs=[
            pl.BlockSpec((rows // steps, columns), lambda step: (step, 0)),
            pl.BlockSpec(proj.shape, lambda step: (0, 0)),
            pl.BlockSpec(memory_space=pl.ANY),
        ],
        out_specs=pl.BlockSpec((rows // steps, proj.shape[0]), lambda step: (step, 0)),
        out_shape=jax.ShapeDtypeStruct((rows, proj.shape[0]), jnp.bfloat16),
        compiler_params=pltpu.CompilerParams(vmem_limit_bytes=VMEM_LIMIT),
        cost_estimate=pl.CostEstimate(
            flops=0, bytes_accessed=0, transcendentals=0
        ),
        name="proj_backward",
    )(part, proj, signal)


def deal_columns(moves, whole_ref, groups_ref):
    for group, inside, column, width in moves:
        groups_ref[group, :, inside : inside + width] = whole_ref[:, column : column + width]


def collect_columns(moves, groups_ref, weight_ref, whole_ref, lean_ref):
    for group, inside, column, width in moves:
        whole_ref[:, column : column + width] = groups_ref[
            group, :, inside : inside + width
        ].astype(jnp.float32)
    lean = jnp.zeros((weight_ref.shape[0], 128), jnp.float32)
    for column in range(0, weight_ref.shape[1], 128):
        span = slice(column, column + 128)
        lean = lean + whole_ref[:, span] * weight_ref[:, span].astype(jnp.float32)
    lean_ref[...] = jnp.sum(lean, axis=1, keepdims=True)


def hand_out(weight, moves):
    count = lax.axis_size("seq")
    rows, columns = weight.shape
    groups = pl.pallas_call(
        partial(deal_columns, moves),
        out_shape=jax.ShapeDtypeStruct((count, rows, columns // count), weight.dtype),
        compiler_params=pltpu.CompilerParams(vmem_limit_bytes=VMEM_LIMIT),
        name="deal_columns",
    )(weight)
    dealt = lax.all_to_all(groups, "seq", split_axis=0, concat_axis=0, tiled=True)
    return dealt.reshape(-1, columns // count)


def sum_planes(grad):
    return lax.psum_scatter(
        grad.astype(jnp.bfloat16), "bucket", scatter_dimension=0, tiled=True
    )


def spread_rows(summed):
    count = lax.axis_size("seq")
    blocks = summed.reshape(count, -1, summed.shape[1])
    return lax.all_to_all(blocks, "seq", split_axis=0, concat_axis=0, tiled=True)


def hand_back(blocks, weight, gain, moves):
    rows, columns = weight.shape
    whole, lean = pl.pallas_call(
        partial(collect_columns, moves),
        out_shape=[
            jax.ShapeDtypeStruct((rows, columns), jnp.float32),
            jax.ShapeDtypeStruct((rows, 1), jnp.float32),
        ],
        compiler_params=pltpu.CompilerParams(vmem_limit_bytes=VMEM_LIMIT),
        name="collect_columns",
    )(blocks, weight)
    return whole, lean[:, 0] / gain.astype(jnp.float32)


FOLD = 512


def row_spans(rows):
    parts = max(count for count in (4, 3, 2, 1) if rows % (16 * count) == 0)
    return [slice(part * rows // parts, (part + 1) * rows // parts) for part in range(parts)]


def feed_forward(near_ref, far_ref, wide_ref, feed_grad_ref, feed_ref, grad_ref, normed_ref):
    half = FOLD // 2

    def expand(part_ref):
        for span in row_spans(part_ref.shape[0]):
            product = jnp.dot(
                part_ref[span, :], wide_ref[...], preferred_element_type=jnp.float32
            )
            activated, slope = gelu_parts(product[:, :half])
            up = product[:, half:]
            feed_ref[span, :] = (activated * up).astype(jnp.bfloat16)
            feed_grad = feed_grad_ref[span, :]
            grad_ref[span, :half] = (feed_grad * up * slope).astype(jnp.bfloat16)
            grad_ref[span, half:] = (feed_grad * activated).astype(jnp.bfloat16)

        @pl.when(pl.program_id(1) == 0)
        def _():
            normed_ref[...] = part_ref[...]

    pl.when(pl.program_id(0) == 0)(lambda: expand(near_ref))
    pl.when(pl.program_id(0) == 1)(lambda: expand(far_ref))


def run_feed_forward(near, far, wide, feed_grad):
    rows, depth = near.shape
    tiles = wide.shape[1] // FOLD
    half = FOLD // 2

    def whole(part, tile):
        return (0, 0)

    return pl.pallas_call(
        feed_forward,
        grid=(2, tiles),
        in_specs=[
            pl.BlockSpec((rows, depth), whole),
            pl.BlockSpec((rows, depth), whole),
            pl.BlockSpec((depth, FOLD), lambda part, tile: (0, tile)),
            pl.BlockSpec((rows, half), lambda part, tile: (part, tile)),
        ],
        out_specs=[
            pl.BlockSpec((rows, half), lambda part, tile: (part, tile)),
            pl.BlockSpec((rows, FOLD), lambda part, tile: (part, tile)),
            pl.BlockSpec((rows, depth), lambda part, tile: (part, 0)),
        ],
        out_shape=[
            jax.ShapeDtypeStruct((2 * rows, tiles * half), jnp.bfloat16),
            jax.ShapeDtypeStruct((2 * rows, tiles * FOLD), jnp.bfloat16),
            jax.ShapeDtypeStruct((2 * rows, depth), jnp.bfloat16),
        ],
        compiler_params=pltpu.CompilerParams(vmem_limit_bytes=VMEM_LIMIT),
        cost_estimate=pl.CostEstimate(
            flops=4 * rows * depth * tiles * FOLD, bytes_accessed=0, transcendentals=0
        ),
        name="feed_forward",
    )(near, far, wide, feed_grad)


def feed_backward(upstream_ref, planes_ref, feed_grad_ref, narrow_ref):
    planes = planes_ref.shape[0]
    tile_rows = FOLD // 2 // planes
    tiles = planes_ref.shape[1] // tile_rows

    @pl.when(pl.program_id(0) == 0)
    def _():
        for tile in range(tiles):
            for plane in range(planes):
                target = (tile * planes + plane) * tile_rows
                narrow_ref[target : target + tile_rows, :] = planes_ref[
                    plane, tile * tile_rows : (tile + 1) * tile_rows, :
                ]

    feed_grad_ref[...] = lax.dot_general(
        upstream_ref[...],
        narrow_ref[...],
        (((1,), (1,)), ((), ())),
        preferred_element_type=jnp.float32,
    )


def run_feed_backward(upstream, narrow):
    rows, depth = upstream.shape
    planes, narrow_rows = narrow.shape[:2]
    width = planes * narrow_rows
    steps = max(count for count in range(1, 7) if rows % (16 * count) == 0)
    block = rows // steps

    def at_step(step):
        return (step, 0)

    return pl.pallas_call(
        feed_backward,
        grid=(steps,),
        in_specs=[
            pl.BlockSpec((block, depth), at_step),
            pl.BlockSpec((planes, narrow_rows, depth), lambda step: (0, 0, 0)),
        ],
        out_specs=[
            pl.BlockSpec((block, width), at_step),
            pl.BlockSpec((width, depth), lambda step: (0, 0)),
        ],
        out_shape=[
            jax.ShapeDtypeStruct((rows, width), jnp.float32),
            jax.ShapeDtypeStruct((width, depth), jnp.bfloat16),
        ],
        compiler_params=pltpu.CompilerParams(vmem_limit_bytes=VMEM_LIMIT),
        cost_estimate=pl.CostEstimate(
            flops=2 * rows * depth * width, bytes_accessed=0, transcendentals=0
        ),
        name="feed_backward",
    )(upstream, narrow)


def pad_lanes(values, lanes):
    return jnp.pad(values, [(0, 0)] * (values.ndim - 1) + [(0, lanes - values.shape[-1])])


def contract_halves(left_near, left_far, right_near, right_far, kind=jnp.bfloat16):
    parts = [
        contract_first(left.reshape(-1, left.shape[-1]), right.reshape(-1, right.shape[-1]))
        for left, right in ((left_near, right_near), (left_far, right_far))
    ]
    return (parts[0] + parts[1]).astype(kind)


def by_channels(
    tokens,
    lengths,
    norm_gain,
    in_proj,
    conv_weight,
    conv_bias,
    gate_weight,
    gate_bias,
    decay,
    out_proj,
    mlp_gain,
    gate_up,
    down_proj,
    cotangent,
):
    planes = lax.axis_size("bucket")
    count = lax.axis_size("seq")
    me = lax.axis_index("seq")
    odd = jnp.bitwise_and(me, 1)
    inputs = tokens[0].astype(jnp.float32)
    rows, depth = inputs.shape
    own_rows = in_proj.shape[0]
    width = in_proj.shape[1] // 2
    block_width = width // NB
    held = planes // 2
    channels = held * block_width
    lanes = -(-channels // 128) * 128
    chunk_rows = conv_weight.shape[0]
    hidden_width = gate_up.shape[1] // 2 // count
    hidden_rows = down_proj.shape[0]
    taps = conv_weight.shape[1]
    slots = lengths.shape[1]

    by_row = jnp.concatenate(
        [out_proj, gate_weight, conv_weight, conv_bias[:, None], gate_bias, decay[:, None]], axis=1
    )
    by_row_width = by_row.shape[1]
    gains = jnp.pad(
        jnp.stack([norm_gain, mlp_gain], axis=1), [(0, chunk_rows - own_rows), (0, 0)]
    )
    by_row = jnp.concatenate([by_row, gains], axis=1)
    by_row = pad_lanes(by_row, -(-(by_row_width + 2) // 128) * 128)
    by_row, in_proj = lax.optimization_barrier((by_row, in_proj))
    by_row = lax.all_gather(by_row, "bucket", axis=0, tiled=False)
    proj_moves = [
        (
            2 * pair + side,
            (half * held + index) * block_width,
            half * width + ((side * held + index) * (count // 2) + pair) * block_width,
            block_width,
        )
        for pair in range(count // 2)
        for side in range(2)
        for half in range(2)
        for index in range(held)
    ]
    tile_rows = FOLD // 2 // planes
    tiles = hidden_rows // tile_rows
    wide_moves = [
        (
            member,
            ((tile * 2 + half) * planes + plane) * tile_rows,
            ((half * planes + plane) * count + member) * hidden_rows + tile * tile_rows,
            tile_rows,
        )
        for member in range(count)
        for tile in range(tiles)
        for half in range(2)
        for plane in range(planes)
    ]
    tokens_near, by_row = gather_chips(tokens[0], by_row)
    tokens_far = swap_with(tokens_near, CORE)
    proj_dealt = hand_out(in_proj, proj_moves)
    gains = by_row[:, :own_rows, by_row_width : by_row_width + 2]
    gains = lax.all_gather(gains.transpose(2, 0, 1), "seq", axis=2).astype(jnp.float32)
    gain_one, gain_two = gains.reshape(2, 1, depth)
    gate_up_late, proj_dealt = lax.optimization_barrier((gate_up, proj_dealt))
    wide_dealt = hand_out(gate_up_late, wide_moves)
    proj = lax.all_gather(proj_dealt, "bucket", axis=0, tiled=True)

    ends = jnp.cumsum(lengths[0]).astype(jnp.int32)
    info = jnp.concatenate([me[None].astype(jnp.int32), ends])

    positions = me * rows + jnp.arange(rows, dtype=jnp.int32)
    keep = (positions < ends[-1]).astype(jnp.float32)[:, None]
    upstream = keep * cotangent[0].astype(jnp.float32)
    scale_one = lax.rsqrt(jnp.mean(inputs * inputs, axis=1, keepdims=True) + norm_eps)
    kept = lax.dynamic_slice_in_dim(by_row, odd * held, held, 0)
    given = lax.dynamic_slice_in_dim(by_row, (1 - odd) * held, held, 0)
    taken = swap_with(given, 1)
    pair = jnp.where(
        odd == 0, jnp.stack([kept, taken], axis=1), jnp.stack([taken, kept], axis=1)
    )
    by_channel = pair.reshape(channels, -1)
    out = jnp.pad(by_channel[:, :depth], [(0, lanes - channels), (0, 0)])
    gate_columns = 2 * block_width
    gate_rows = by_channel[:, depth : depth + gate_columns]
    gate_blocks = []
    for index in range(held):
        part = gate_rows[index * block_width : (index + 1) * block_width]
        at = index * block_width
        gate_blocks.append(
            jnp.concatenate(
                [
                    jnp.pad(side, [(0, 0), (at, lanes - at - block_width)])
                    for side in (part[:, :block_width], part[:, block_width:])
                ],
                axis=1,
            )
        )
    gate = jnp.pad(jnp.concatenate(gate_blocks, axis=0), [(0, lanes - channels), (0, 0)])
    small = by_channel[:, depth + gate_columns : by_row_width].astype(jnp.float32).T
    decay_channel = small[taps + 3]
    rate = jnp.pad(jax.nn.softplus(decay_channel), (0, lanes - channels), constant_values=0.01)
    channel = jnp.concatenate([pad_lanes(small[: taps + 3], lanes), rate[None]], axis=0)

    def normalize(low):
        values = low.astype(jnp.float32)
        scale = lax.rsqrt(jnp.mean(values * values, axis=2, keepdims=True) + norm_eps)
        return (values * scale * gain_one).astype(jnp.bfloat16)

    wide_dealt, down_proj, gain_one = lax.optimization_barrier((wide_dealt, down_proj, gain_one))
    normed_near, normed_far = normalize(tokens_near), normalize(tokens_far)
    upstream_low, normed_near, normed_far = lax.optimization_barrier(
        (upstream.astype(jnp.bfloat16), normed_near, normed_far)
    )
    upstream_parts = send_to_chips(upstream_low, upstream_low, upstream_low)
    narrow = lax.all_gather(down_proj, "bucket", axis=0)
    wide = lax.all_gather(wide_dealt, "bucket", axis=0, tiled=True)
    gated, *saved = run_forward(
        info, normed_near, normed_far, proj, gate, channel, taps, slots
    )
    gated, *upstream_parts = lax.optimization_barrier((gated, *upstream_parts))
    upstream_near = jnp.stack([upstream_low, *upstream_parts])
    upstream_far = swap_with(upstream_near, CORE)
    gated_near, upstream_near = lax.optimization_barrier((gated[: count // 2], upstream_near))
    mixed_far, mixed_near = (
        jnp.dot(part.reshape(-1, lanes), out, preferred_element_type=jnp.float32)
        .astype(jnp.bfloat16)
        .reshape(-1, rows, depth)
        for part in (gated[count // 2 :], gated_near)
    )
    mixed, narrow = reduce_plane(mixed_near, mixed_far, late=(narrow,))
    residual = inputs + mixed
    scale_two = lax.rsqrt(jnp.mean(residual * residual, axis=1, keepdims=True) + norm_eps)
    normed_two = (residual * scale_two * gain_two).astype(jnp.bfloat16)
    two_near = gather_chips(normed_two)
    two_far = swap_with(two_near, CORE)
    upstream_all = jnp.concatenate([upstream_near, upstream_far]).reshape(-1, depth)
    feed_grad, narrow = run_feed_backward(upstream_all, narrow)
    feed, expanded_grad, two_all = run_feed_forward(
        two_near.reshape(-1, depth), two_far.reshape(-1, depth), wide, feed_grad
    )
    half_rows = two_all.shape[0] // 2

    down_part = contract_first(feed, upstream_all).astype(jnp.bfloat16)
    down_part = (
        down_part.reshape(tiles, planes, tile_rows, depth)
        .transpose(1, 0, 2, 3)
        .reshape(hidden_width, depth)
    )
    down_grad = sum_planes(down_part).astype(jnp.float32)
    part_far = contract_last(expanded_grad[half_rows:], wide).astype(jnp.bfloat16)
    part_near = contract_last(expanded_grad[:half_rows], wide).astype(jnp.bfloat16)
    normed_two_grad, two_all, feed = reduce_plane(
        part_near.reshape(-1, rows, depth), part_far.reshape(-1, rows, depth), two_all, feed
    )
    def norm_back(values, scale, gain, grad):
        scaled = grad * gain
        lean = jnp.mean(scaled * values, axis=1, keepdims=True)
        return scale * scaled - scale * scale * scale * lean * values

    residual_grad = upstream + norm_back(residual, scale_two, gain_two, normed_two_grad)
    wide_part = contract_first(two_all, expanded_grad).astype(jnp.bfloat16)
    residual_grad, wide_part, down_part = lax.optimization_barrier(
        (residual_grad, wide_part, down_part)
    )
    wide_summed = sum_planes(wide_part)
    output_far, output_near = (
        jnp.dot(part, narrow, preferred_element_type=jnp.float32)
        .astype(jnp.bfloat16)
        .reshape(-1, rows, depth)
        for part in (feed[half_rows:], feed[:half_rows])
    )
    low_near, output_near, output_far, down_grad = gather_chips(
        residual_grad.astype(jnp.bfloat16), output_near, output_far, down_grad
    )
    output_other = swap_with(output_far, CORE)
    output_sums = [
        output_near[place].astype(jnp.float32) + output_other[place].astype(jnp.float32)
        for place in range(4)
    ]
    low_far = swap_with(low_near, CORE)
    low_far, *output_low = lax.optimization_barrier(
        (low_far, *(output_sums[place].astype(jnp.bfloat16) for place in (1, 2, 3)))
    )
    output_parts = send_to_chips(*output_low)
    proj_grad_near, proj_grad_far, gate_grad, channel_grad = run_backward(
        info, low_near, low_far, out, gate, channel, saved, 2 * channels, taps, slots
    )

    def through_proj(part):
        part = run_proj_backward(part.reshape(-1, 2 * channels), proj, signal)
        return part.reshape(-1, rows, depth)

    proj_part = contract_halves(normed_near, normed_far, proj_grad_near, proj_grad_far)
    proj_grad_far, proj_grad_near, proj_part, wide_summed = lax.optimization_barrier(
        (proj_grad_far, proj_grad_near, proj_part, wide_summed)
    )
    signal = swap_with(proj_part[:16, :128], CORE)
    part_far = through_proj(proj_grad_far)
    part_far, *output_parts = lax.optimization_barrier((part_far, *output_parts))
    mixed = residual + output_sums[0]
    for part in output_parts:
        mixed = mixed + part.astype(jnp.float32)
    mixed = (keep * mixed).astype(jnp.bfloat16)
    proj_summed = sum_planes(proj_part)
    part_near = through_proj(proj_grad_near)
    normed_grad, gated, mixed = reduce_plane(part_near, part_far, gated, mixed)

    out_grad = contract_halves(
        gated[: count // 2], gated[count // 2 :], low_near, low_far, jnp.float32
    )[:channels]
    gate_parts = []
    for index in range(held):
        at = index * block_width
        span = gate_grad[at : at + block_width]
        gate_parts.append(
            jnp.concatenate(
                [span[:, at : at + block_width], span[:, lanes + at : lanes + at + block_width]],
                axis=1,
            )
        )
    channel_grad = channel_grad[:, :channels]
    small_grad = jnp.concatenate(
        [
            channel_grad[: taps + 3],
            (channel_grad[taps + 3] * jax.nn.sigmoid(decay_channel))[None],
        ],
        axis=0,
    )
    by_row_grad = jnp.concatenate(
        [out_grad, jnp.concatenate(gate_parts, axis=0), small_grad.T], axis=1
    ).astype(jnp.bfloat16)
    by_row_grad = pad_lanes(by_row_grad, by_row.shape[2]).reshape(held, 2, chunk_rows, -1)
    kept = lax.dynamic_index_in_dim(by_row_grad, odd, 1, False)
    taken = swap_with(lax.dynamic_index_in_dim(by_row_grad, 1 - odd, 1, False), 1)
    by_row_grad = jnp.where(
        odd == 0, jnp.concatenate([kept, taken]), jnp.concatenate([taken, kept])
    ).reshape(planes * chunk_rows, -1)
    by_row_grad = sum_planes(by_row_grad)
    gate_up_grad, mlp_gain_grad = hand_back(spread_rows(wide_summed), gate_up, mlp_gain, wide_moves)
    token_grad = residual_grad + norm_back(inputs, scale_one, gain_one, normed_grad)
    token_grad, proj_blocks = lax.optimization_barrier((token_grad, spread_rows(proj_summed)))
    in_proj_grad, norm_gain_grad = hand_back(proj_blocks, in_proj, norm_gain, proj_moves)
    by_row_grad = by_row_grad.astype(jnp.float32)
    out_proj_grad, gate_weight_grad, small_grad = pl.pallas_call(
        split_mixer_rows,
        out_shape=[
            jax.ShapeDtypeStruct((chunk_rows, columns), jnp.float32)
            for columns in (depth, gate_columns, taps + 4)
        ],
        name="split_mixer_rows",
    )(by_row_grad)
    return (
        mixed[None],
        token_grad[None],
        norm_gain_grad,
        in_proj_grad,
        small_grad[:, :taps],
        small_grad[:, taps],
        gate_weight_grad,
        small_grad[:, taps + 1 : taps + 3],
        small_grad[:, taps + 3],
        out_proj_grad,
        mlp_gain_grad,
        gate_up_grad,
        down_grad,
    )


def solution(mesh):
    planes, count = mesh.shape["bucket"], mesh.shape["seq"]
    whole_blocks = count == 8 and planes % 2 == 0 and planes * count == 2 * NB
    return jax.shard_map(
        by_channels if whole_blocks else on_device,
        mesh=mesh,
        in_specs=(
            P("bucket", "seq", None),
            P("bucket", None),
            P(("bucket", "seq")),
            P(("bucket", "seq"), None),
            P(("bucket", "seq"), None),
            P(("bucket", "seq")),
            P(("bucket", "seq"), None),
            P(("bucket", "seq"), None),
            P(("bucket", "seq")),
            P(("bucket", "seq"), None),
            P(("bucket", "seq")),
            P(("bucket", "seq"), None),
            P(("bucket", "seq"), None),
            P("bucket", "seq", None),
        ),
        out_specs=(
            P("bucket", "seq", None),
            P("bucket", "seq", None),
            P(("bucket", "seq")),
            P(("bucket", "seq"), None),
            P(("bucket", "seq"), None),
            P(("bucket", "seq")),
            P(("bucket", "seq"), None),
            P(("bucket", "seq"), None),
            P(("bucket", "seq")),
            P(("bucket", "seq"), None),
            P(("bucket", "seq")),
            P(("bucket", "seq"), None),
            P(("bucket", "seq"), None),
        ),
        check_vma=False,
    )
```

```python
from functools import partial

import jax
import jax.numpy as jnp
from jax import lax
from jax.experimental import pallas as pl
from jax.experimental.pallas import tpu as pltpu
from jax.sharding import PartitionSpec as P

NB = 16


norm_eps = 1e-06
gate_scale = 8.0


def from_behind(block, axis, distance):
    devices = range(lax.axis_size(axis))
    route = [(i - distance, i) for i in devices if i - distance in devices]
    return lax.ppermute(block, axis, route)


def entering(part, axis, combine, identity, reverse):
    count = lax.axis_size(axis)
    place = lax.axis_index(axis)
    ahead = count - 1 - place if reverse else place
    gathered = jax.tree.map(lambda a: lax.all_gather(a, axis), part)
    state = jax.tree.map(lambda a, e: jnp.zeros_like(a) + jnp.asarray(e, a.dtype), part, identity)

    def one(lap, state):
        source = count - 1 - lap if reverse else lap
        return combine(
            state, jax.tree.map(lambda a: lax.dynamic_index_in_dim(a, source, 0, False), gathered)
        )

    return lax.fori_loop(0, ahead, one, state)


def rms_scale(values, gain):
    return values * lax.rsqrt(jnp.mean(values * values, axis=1, keepdims=True) + norm_eps) * gain


def link(earlier, later):
    return (earlier[0] * later[0], later[0] * earlier[1] + later[1])


def segment_layout(lengths_row, positions):
    ends = jnp.cumsum(lengths_row)
    segment_ids = jnp.sum((positions[:, None] >= ends[None, :]).astype(jnp.int32), axis=1)
    segment_ids = jnp.where(positions < 0, -1, segment_ids)
    keep = (positions < ends[-1]).astype(jnp.float32)
    return (segment_ids, keep)


def lru_terms(conv_out, gate_a, gate_i, decay, starts):
    rate = jax.nn.softplus(decay)
    log_step = -gate_scale * jax.nn.sigmoid(gate_a) * rate
    decay_step = jnp.where(starts, 0.0, jnp.exp(log_step))
    scaling = jnp.where(starts, 1.0, jnp.sqrt(-jnp.expm1(2.0 * log_step)))
    return (decay_step, conv_out * jax.nn.sigmoid(gate_i) * scaling)


def gated_gelu(values, split):
    return jax.nn.gelu(values[:, :split]) * values[:, split:]


def contract_last(left, right):
    return lax.dot_general(
        left, right, (((1,), (1,)), ((), ())), preferred_element_type=jnp.float32
    )


def contract_first(left, right):
    return lax.dot_general(
        left, right, (((0,), (0,)), ((), ())), preferred_element_type=jnp.float32
    )


def row_product(left, right):
    return contract_first(left, right)


def on_device(
    tokens,
    lengths,
    norm_gain,
    in_proj,
    conv_weight,
    conv_bias,
    gate_weight,
    gate_bias,
    decay,
    out_proj,
    mlp_gain,
    gate_up,
    down_proj,
    cotangent,
):
    inputs = tokens[0].astype(jnp.float32)
    tok_rows = inputs.shape[0]
    width = in_proj.shape[1] // 2
    ff_width = gate_up.shape[1] // 2
    block_width = width // NB
    kernel = conv_weight.shape[1]
    rim_rows = kernel - 1
    (
        gain_one_all,
        proj_all,
        conv_all,
        conv_bias_all,
        gate_all,
        gate_bias_all,
        decay_all,
        out_all,
        gain_two_all,
    ) = (
        lax.all_gather(norm_gain, ("bucket", "seq"), axis=0, tiled=True),
        lax.all_gather(in_proj, ("bucket", "seq"), axis=0, tiled=True),
        lax.all_gather(conv_weight, ("bucket", "seq"), axis=0, tiled=True),
        lax.all_gather(conv_bias, ("bucket", "seq"), axis=0, tiled=True),
        lax.all_gather(gate_weight, ("bucket", "seq"), axis=0, tiled=True),
        lax.all_gather(gate_bias, ("bucket", "seq"), axis=0, tiled=True),
        lax.all_gather(decay, ("bucket", "seq"), axis=0, tiled=True),
        lax.all_gather(out_proj, ("bucket", "seq"), axis=0, tiled=True),
        lax.all_gather(mlp_gain, ("bucket", "seq"), axis=0, tiled=True),
    )
    seq_index = lax.axis_index("seq")
    positions = seq_index * tok_rows + jnp.arange(tok_rows, dtype=jnp.int32)
    lengths_row = lengths[0]
    segment_ids, keep = segment_layout(lengths_row, positions)
    back_ids = segment_layout(lengths_row, positions - 1)[0]
    starts = (segment_ids != back_ids)[:, None]
    normed, norm_pull = jax.vjp(rms_scale, inputs, gain_one_all.astype(jnp.float32))
    normed_low = normed.astype(jnp.bfloat16)
    projected = jnp.dot(normed_low, proj_all, preferred_element_type=jnp.float32)
    mixer_in = projected[:, :width].astype(jnp.bfloat16)
    branch = projected[:, width:]
    rim = from_behind(mixer_in[tok_rows - rim_rows :], "seq", 1)
    extended = jnp.concatenate([rim, mixer_in], axis=0)
    conv_float = conv_all.astype(jnp.float32)
    lagged_terms = []
    convolved = jnp.zeros((tok_rows, width), jnp.float32) + conv_bias_all.astype(jnp.float32)
    for offset in range(kernel):
        earlier_ids = segment_layout(lengths_row, positions - offset)[0]
        lagged = jnp.where(
            (earlier_ids == segment_ids)[:, None],
            extended[rim_rows - offset : rim_rows - offset + tok_rows].astype(jnp.float32),
            0.0,
        )
        lagged_terms.append(lagged)
        convolved = convolved + lagged * conv_float[:, offset]
    conv_out = convolved.astype(jnp.bfloat16)
    gates = jnp.einsum(
        "tnc,ncd->tnd",
        conv_out.reshape(tok_rows, NB, block_width),
        gate_all.reshape(NB, block_width, 2 * block_width),
        preferred_element_type=jnp.float32,
    )
    gate_bias_float = gate_bias_all.astype(jnp.float32)
    gate_a = gates[:, :, :block_width].reshape(tok_rows, width) + gate_bias_float[:, 0]
    gate_i = gates[:, :, block_width:].reshape(tok_rows, width) + gate_bias_float[:, 1]
    (decay_step, normalized), lru_pull = jax.vjp(
        partial(lru_terms, starts=starts),
        conv_out.astype(jnp.float32),
        gate_a,
        gate_i,
        decay_all.astype(jnp.float32),
    )
    prefix_decay, prefix_state = lax.associative_scan(link, (decay_step, normalized), axis=0)
    carried = entering(
        (prefix_decay[-1], prefix_state[-1]),
        "seq",
        link,
        (jnp.ones((width,), jnp.float32), jnp.zeros((width,), jnp.float32)),
        False,
    )
    state_in = carried[1]
    hidden = prefix_state + prefix_decay * state_in
    branch_act, branch_pull = jax.vjp(jax.nn.gelu, branch)
    gated = (hidden * branch_act).astype(jnp.bfloat16)
    residual = inputs + jnp.dot(gated, out_all, preferred_element_type=jnp.float32)
    normed_two, norm_two_pull = jax.vjp(rms_scale, residual, gain_two_all.astype(jnp.float32))
    normed_two_low = normed_two.astype(jnp.bfloat16)
    gate_up_all, down_all = (
        lax.all_gather(gate_up, ("bucket", "seq"), axis=0, tiled=True),
        lax.all_gather(down_proj, ("bucket", "seq"), axis=0, tiled=True),
    )
    expanded = jnp.dot(normed_two_low, gate_up_all, preferred_element_type=jnp.float32)
    feed, feed_pull = jax.vjp(partial(gated_gelu, split=ff_width), expanded)
    feed_low = feed.astype(jnp.bfloat16)
    output_rows = residual + jnp.dot(feed_low, down_all, preferred_element_type=jnp.float32)
    mixed = (keep[:, None] * output_rows).astype(jnp.bfloat16)
    upstream = keep[:, None] * cotangent[0].astype(jnp.float32)
    upstream_low = upstream.astype(jnp.bfloat16)
    down_grad = lax.psum_scatter(
        row_product(feed_low, upstream_low), ("bucket", "seq"), scatter_dimension=0, tiled=True
    )
    feed_grad = contract_last(upstream_low, down_all)
    expanded_grad = feed_pull(feed_grad)[0].astype(jnp.bfloat16)
    gate_up_grad = lax.psum_scatter(
        row_product(normed_two_low, expanded_grad),
        ("bucket", "seq"),
        scatter_dimension=0,
        tiled=True,
    )
    normed_two_grad = contract_last(expanded_grad, gate_up_all)
    residual_part, gain_two_grad = norm_two_pull(normed_two_grad)
    residual_grad = upstream + residual_part
    residual_low = residual_grad.astype(jnp.bfloat16)
    out_grad = contract_first(gated, residual_low)
    gated_grad = contract_last(residual_low, out_all)
    hidden_grad = gated_grad * branch_act
    branch_grad = branch_pull(gated_grad * hidden)[0]
    next_decay = jnp.concatenate([decay_step[1:], jnp.ones((1, width), jnp.float32)], axis=0)
    suffix_decay, suffix_state = lax.associative_scan(
        link, (next_decay, hidden_grad), reverse=True, axis=0
    )
    returned = entering(
        (prefix_decay[-1], decay_step[0] * suffix_state[0]),
        "seq",
        link,
        (jnp.ones((width,), jnp.float32), jnp.zeros((width,), jnp.float32)),
        True,
    )
    incoming = returned[1]
    state_grad = suffix_state + suffix_decay * incoming
    state_before = jnp.concatenate([state_in[None, :], hidden[:-1]], axis=0)
    conv_grad_lru, gate_a_grad, gate_i_grad, decay_grad = lru_pull(
        (state_grad * state_before, state_grad)
    )
    gates_low = jnp.concatenate(
        [
            gate_a_grad.reshape(tok_rows, NB, block_width),
            gate_i_grad.reshape(tok_rows, NB, block_width),
        ],
        axis=2,
    ).astype(jnp.bfloat16)
    gate_grad = jnp.einsum(
        "tnc,tnd->ncd",
        conv_out.reshape(tok_rows, NB, block_width),
        gates_low,
        preferred_element_type=jnp.float32,
    ).reshape(width, 2 * block_width)
    bias_sums = jnp.sum(gates_low.astype(jnp.float32), axis=0)
    gate_bias_grad = jnp.stack(
        [bias_sums[:, :block_width].reshape(width), bias_sums[:, block_width:].reshape(width)],
        axis=1,
    )
    conv_grad_gates = jnp.einsum(
        "tnd,ncd->tnc",
        gates_low,
        gate_all.reshape(NB, block_width, 2 * block_width),
        preferred_element_type=jnp.float32,
    ).reshape(tok_rows, width)
    conv_low = (conv_grad_lru + conv_grad_gates).astype(jnp.bfloat16)
    head = from_behind(conv_low[:rim_rows], "seq", -1)
    trailing = jnp.concatenate([conv_low, head], axis=0)
    conv_low_float = conv_low.astype(jnp.float32)
    mixer_grad = jnp.zeros((tok_rows, width), jnp.float32)
    tap_grads = []
    for offset in range(kernel):
        later_ids = segment_layout(lengths_row, positions + offset)[0]
        ahead = jnp.where(
            (later_ids == segment_ids)[:, None],
            trailing[offset : offset + tok_rows].astype(jnp.float32),
            0.0,
        )
        mixer_grad = mixer_grad + ahead * conv_float[:, offset]
        tap_grads.append(jnp.sum(conv_low_float * lagged_terms[offset], axis=0))
    conv_weight_grad = jnp.stack(tap_grads, axis=1)
    conv_bias_grad = jnp.sum(conv_low_float, axis=0)
    proj_grad_low = jnp.concatenate([mixer_grad, branch_grad], axis=1).astype(jnp.bfloat16)
    in_proj_grad = contract_first(normed_low, proj_grad_low)
    normed_grad = contract_last(proj_grad_low, proj_all)
    input_part, gain_one_grad = norm_pull(normed_grad)
    token_grad = residual_grad + input_part
    summed = (
        lax.psum_scatter(gain_one_grad, ("bucket", "seq"), scatter_dimension=0, tiled=True),
        lax.psum_scatter(in_proj_grad, ("bucket", "seq"), scatter_dimension=0, tiled=True),
        lax.psum_scatter(conv_weight_grad, ("bucket", "seq"), scatter_dimension=0, tiled=True),
        lax.psum_scatter(conv_bias_grad, ("bucket", "seq"), scatter_dimension=0, tiled=True),
        lax.psum_scatter(gate_grad, ("bucket", "seq"), scatter_dimension=0, tiled=True),
        lax.psum_scatter(gate_bias_grad, ("bucket", "seq"), scatter_dimension=0, tiled=True),
        lax.psum_scatter(decay_grad, ("bucket", "seq"), scatter_dimension=0, tiled=True),
        lax.psum_scatter(out_grad, ("bucket", "seq"), scatter_dimension=0, tiled=True),
        lax.psum_scatter(gain_two_grad, ("bucket", "seq"), scatter_dimension=0, tiled=True),
    )
    return (
        mixed[None],
        token_grad[None],
        summed[0],
        summed[1],
        summed[2],
        summed[3],
        summed[4],
        summed[5],
        summed[6],
        summed[7],
        summed[8],
        gate_up_grad,
        down_grad,
    )


def swap_with(block, mask):
    route = [(i, i ^ mask) for i in range(lax.axis_size("seq"))]
    return lax.ppermute(block, "seq", route)


CORE, ACROSS_X, ACROSS_Y = 1, 2, 4


def split_row(rows):
    return rows // 32 * 16


def gather_chips(block, *others):
    split = split_row(block.shape[0])
    across_x, across_y = swap_with(block, ACROSS_X), swap_with(block, ACROSS_Y)
    if others:
        across_x, across_y, *others = lax.optimization_barrier((across_x, across_y, *others))
    both = [swap_with(across_y[:split], ACROSS_X), swap_with(across_x[split:], ACROSS_Y)]
    near = jnp.concatenate([block, across_x, across_y, *both]).reshape(4, *block.shape)
    return (near, *others) if others else near


def send_to_chips(across_x, across_y, across_both):
    return [
        swap_with(across_x, ACROSS_X),
        swap_with(across_y, ACROSS_Y),
        swap_with(across_both, ACROSS_X + ACROSS_Y),
    ]


def reduce_plane(near, far, *others, late=()):
    other = swap_with(far, CORE)
    rows = near.shape[1]
    split = split_row(rows)

    def total(place, span=slice(None)):
        return near[place, span].astype(jnp.float32) + other[place, span].astype(jnp.float32)

    both = total(3).astype(jnp.bfloat16)
    both, *others = lax.optimization_barrier((both, *others))
    first = swap_with(both[:split], ACROSS_Y).astype(jnp.float32)
    second = swap_with(both[split:], ACROSS_X).astype(jnp.float32)
    across_x = jnp.concatenate([total(1, slice(split)) + first, total(1, slice(split, None))])
    across_y = jnp.concatenate([total(2, slice(split)), total(2, slice(split, None)) + second])
    across_x, across_y = across_x.astype(jnp.bfloat16), across_y.astype(jnp.bfloat16)
    across_x, across_y, *late = lax.optimization_barrier((across_x, across_y, *late))
    others += late
    across_x = swap_with(across_x, ACROSS_X).astype(jnp.float32)
    across_y = swap_with(across_y, ACROSS_Y).astype(jnp.float32)
    result = total(0) + across_x + across_y
    return (result, *others) if others else result


def reduce_plane_at_once(near, far, *others):
    other = swap_with(far, CORE)

    def total(place):
        return near[place].astype(jnp.float32) + other[place].astype(jnp.float32)

    *parts, others = lax.optimization_barrier(
        (*(total(place).astype(jnp.bfloat16) for place in (1, 2, 3)), others)
    )
    sent = send_to_chips(*parts)

    def finish(*late):
        *parts, late = lax.optimization_barrier((*sent, late))
        result = total(0)
        for part in parts:
            result = result + part.astype(jnp.float32)
        return (result, *late) if late else result

    return (finish, *others)


def split_mixer_rows(joined_ref, out_ref, gate_ref, *small_refs):
    depth, gates = out_ref.shape[1], gate_ref.shape[1]
    joined = joined_ref[...].astype(jnp.float32)
    out_ref[...] = joined[:, :depth]
    gate_ref[...] = joined[:, depth : depth + gates]
    first = (depth + gates) // 128 * 128
    turned = joined[:, first : first + 128].T
    row = depth + gates - first
    for small_ref in small_refs:
        small_ref[...] = turned[row : row + small_ref.shape[0]]
        row += small_ref.shape[0]


def place_of(chunk, me, count):
    relative = jnp.bitwise_xor(chunk, me)
    return jnp.bitwise_and(relative, 1), jnp.right_shift(relative, 1)


def series_expm1(values):
    total = 1.0 + values * (1.0 / 7.0)
    for term in (6, 5, 4, 3, 2):
        total = 1.0 + values * (1.0 / term) * total
    return values * total


def segment_reach(info_ref, first, slots, shape, total):
    positions = first + lax.broadcasted_iota(jnp.int32, shape, 0)
    begin = jnp.zeros(shape, jnp.int32)
    finish = jnp.full(shape, total, jnp.int32)
    for slot in range(slots):
        end = info_ref[1 + slot]
        passed = positions >= end
        begin = jnp.where(passed, jnp.maximum(begin, end), begin)
        finish = jnp.where(passed, finish, jnp.minimum(finish, end))
    return positions - begin, finish - positions


def widen(mask, lanes):
    return jnp.concatenate([mask] * (lanes // mask.shape[1]), axis=1)


def gelu_parts(values):
    inner = 0.7978845608028654 * (values + 0.044715 * values * values * values)
    bent = jnp.tanh(inner)
    half = 0.5 * (1.0 + bent)
    slope = half + 0.5 * values * (1.0 - bent * bent) * 0.7978845608028654 * (
        1.0 + 3.0 * 0.044715 * values * values
    )
    return values * half, slope


ROWS = 8


def tiles_at_once(tiles):
    return max(size for size in range(1, GROUP + 1) if tiles % size == 0)


def group_tiles(index, group):
    return [index * group + member for member in range(group)]


GROUP = 11
TAP, BIAS, BIAS_A, BIAS_I, RATE = 0, 4, 5, 6, 7


def mixer_forward(
    taps,
    slots,
    info_ref,
    near_ref,
    far_ref,
    proj_ref,
    gate_ref,
    channel_ref,
    gated_ref,
    lagging_ref,
    conv_ref,
    act_ref,
    slope_ref,
    decay_ref,
    rate_part_ref,
    gate_i_part_ref,
    conv_part_ref,
    gate_r_ref,
    lag_edge_ref,
    proj_wide,
    projected,
    convolved,
    gates,
    carry,
    edge,
):
    chunk = pl.program_id(0)
    is_far, _ = place_of(chunk, info_ref[0], pl.num_programs(0))
    rows, lanes = convolved.shape
    tiles = rows // ROWS
    group = tiles_at_once(tiles)
    total = rows * pl.num_programs(0)

    @pl.when(chunk == 0)
    def _():
        carry[...] = jnp.zeros_like(carry)
        edge[...] = jnp.zeros_like(edge)
        channels = proj_ref.shape[1] // 2
        proj_wide[...] = jnp.zeros_like(proj_wide)
        proj_wide[:, :channels] = proj_ref[:, :channels]
        proj_wide[:, lanes : lanes + channels] = proj_ref[:, channels:]

    def project(normed_ref):
        product = jnp.dot(normed_ref[0], proj_wide[...], preferred_element_type=jnp.float32)
        low = product[:, :lanes].astype(jnp.bfloat16)
        lagging_ref[0] = low
        projected[:, :lanes] = low.astype(jnp.float32)
        projected[:, lanes:] = product[:, lanes:]

    pl.when(is_far == 0)(lambda: project(near_ref))
    pl.when(is_far == 1)(lambda: project(far_ref))
    place = lax.broadcasted_iota(jnp.int32, (ROWS, lanes), 0)

    def convolve(tile, before):
        for tile in group_tiles(tile, group):
            before = convolve_tile(tile, before)
        return before

    def convolve_tile(tile, before):
        at = pl.ds(pl.multiple_of(tile * ROWS, ROWS), ROWS)
        here = projected[at, :lanes]
        since, _ = segment_reach(info_ref, chunk * rows + tile * ROWS, slots, (ROWS, 128), total)
        value = channel_ref[BIAS : BIAS + 1, :] + here * channel_ref[TAP : TAP + 1, :]
        for lag in range(1, taps):
            moved = jnp.where(
                place < lag, pltpu.roll(before, lag, 0), pltpu.roll(here, lag, 0)
            )
            value = value + jnp.where(widen(since >= lag, lanes), moved, 0.0) * (
                channel_ref[TAP + lag : TAP + lag + 1, :]
            )
        convolved[at, :] = value
        return here

    last = lax.fori_loop(0, tiles // group, convolve, edge[...])
    edge[...] = last
    lag_edge_ref[0] = last
    conv_low = convolved[...].astype(jnp.bfloat16)
    conv_ref[0] = conv_low
    convolved[...] = conv_low.astype(jnp.float32)
    gates[...] = jnp.dot(conv_low, gate_ref[...], preferred_element_type=jnp.float32)

    def recur(tile, state):
        parts = [local_scan(tile) for tile in group_tiles(tile, group)]
        for at, value, decay, activated, slope, ratio, gate in parts:
            hidden = value + decay * state
            before = jnp.where(place == 0, state, pltpu.roll(hidden, 1, 0))
            state = jnp.broadcast_to(hidden[ROWS - 1 :], hidden.shape)
            projected[at, :lanes] = hidden * activated
            slope_ref[0, at, :] = hidden * slope
            rate_part_ref[0, at, :] = gate * (before - ratio)
        return state

    def local_scan(tile):
        at = pl.ds(pl.multiple_of(tile * ROWS, ROWS), ROWS)
        since, _ = segment_reach(info_ref, chunk * rows + tile * ROWS, slots, (ROWS, 128), total)
        starts = widen(since == 0, lanes)
        gate_r = jax.nn.sigmoid(gates[at, :lanes] + channel_ref[BIAS_A : BIAS_A + 1, :])
        gate_i = jax.nn.sigmoid(gates[at, lanes:] + channel_ref[BIAS_I : BIAS_I + 1, :])
        less = series_expm1(-gate_scale * gate_r * channel_ref[RATE : RATE + 1, :])
        plain = 1.0 + less
        root = jnp.sqrt(jnp.maximum(-less * (2.0 + less), 1e-37))
        decay = jnp.where(starts, 0.0, plain)
        scaling = jnp.where(starts, 1.0, root)
        conv = convolved[at, :]
        admitted = conv * gate_i
        value = admitted * scaling
        decay_ref[0, at, :] = decay
        conv_part_ref[0, at, :] = gate_i * scaling
        gate_i_part_ref[0, at, :] = value * (1.0 - gate_i)
        gate_r_ref[0, at, :] = 1.0 - gate_r
        ratio = admitted * plain / root
        gate = decay * gate_r
        for step in (1, 2, 4):
            inside = place >= step
            value = value + jnp.where(inside, decay * pltpu.roll(value, step, 0), 0.0)
            decay = jnp.where(inside, decay * pltpu.roll(decay, step, 0), decay)
        activated, slope = gelu_parts(projected[at, lanes:])
        act_ref[0, at, :] = activated
        return at, value, decay, activated, slope, ratio, gate

    carry[...] = lax.fori_loop(0, tiles // group, recur, carry[...])
    gated_ref[0] = projected[:, :lanes].astype(jnp.bfloat16)


def mixer_backward(
    taps,
    slots,
    info_ref,
    near_ref,
    far_ref,
    out_ref,
    gate_ref,
    channel_ref,
    act_ref,
    slope_ref,
    decay_ref,
    rate_part_ref,
    gate_i_part_ref,
    conv_part_ref,
    gate_r_ref,
    conv_ref,
    lagging_ref,
    lag_edge_ref,
    projected_near_ref,
    projected_far_ref,
    gate_grad_ref,
    channel_grad_ref,
    coming,
    conv_part,
    lagged,
    gates,
    projected,
    conv_grad,
    grad_carry,
    decay_carry,
    sums,
):
    lap = pl.program_id(0)
    laps = pl.num_programs(0)
    chunk = laps - 1 - lap
    is_far, _ = place_of(chunk, info_ref[0], laps)
    rows, lanes = conv_part.shape
    tiles = rows // ROWS
    group = tiles_at_once(tiles)
    total = rows * laps

    @pl.when(lap == 0)
    def _():
        grad_carry[...] = jnp.zeros_like(grad_carry)
        decay_carry[...] = jnp.zeros_like(decay_carry)
        conv_grad[...] = jnp.zeros_like(conv_grad)
        sums[...] = jnp.zeros_like(sums)
        gate_grad_ref[...] = jnp.zeros_like(gate_grad_ref)

    def expand(down_ref):
        coming[...] = lax.dot_general(
            down_ref[0], out_ref[...], (((1,), (1,)), ((), ())), preferred_element_type=jnp.float32
        )

    pl.when(is_far == 0)(lambda: expand(near_ref))
    pl.when(is_far == 1)(lambda: expand(far_ref))
    lagged[...] = lagging_ref[0].astype(jnp.float32)
    place = lax.broadcasted_iota(jnp.int32, (ROWS, lanes), 0)

    def recur(step_index, carried):
        later_grad, later_decay, sum_a, sum_i, sum_rate = carried
        members = group_tiles(tiles // group - 1 - step_index, group)[::-1]
        parts = []
        for tile in members:
            part = local_scan(tile, later_decay)
            later_decay = part[-1]
            parts.append(part)
        for at, value, weight, _ in parts:
            grad = value + weight * later_grad
            later_grad = jnp.broadcast_to(grad[:1], grad.shape)
            conv_part[at, :] = grad * conv_part_ref[0, at, :]
            grad_i = grad * gate_i_part_ref[0, at, :]
            grad_rate = grad * rate_part_ref[0, at, :]
            grad_a = (-gate_scale * channel_ref[RATE : RATE + 1, :]) * grad_rate * gate_r_ref[0, at, :]
            grad_a = grad_a.astype(jnp.bfloat16).astype(jnp.float32)
            grad_i = grad_i.astype(jnp.bfloat16).astype(jnp.float32)
            gates[at, :lanes] = grad_a
            gates[at, lanes:] = grad_i
            sum_a = sum_a + grad_a
            sum_i = sum_i + grad_i
            sum_rate = sum_rate - gate_scale * grad_rate
        return later_grad, later_decay, sum_a, sum_i, sum_rate

    def local_scan(tile, later_decay):
        at = pl.ds(pl.multiple_of(tile * ROWS, ROWS), ROWS)
        decay = decay_ref[0, at, :]
        down = coming[at, :]
        value = down * act_ref[0, at, :]
        projected[at, lanes:] = down * slope_ref[0, at, :]
        weight = jnp.where(place == ROWS - 1, later_decay, pltpu.roll(decay, ROWS - 1, 0))
        for step in (1, 2, 4):
            inside = place < ROWS - step
            value = value + jnp.where(inside, weight * pltpu.roll(value, ROWS - step, 0), 0.0)
            weight = jnp.where(inside, weight * pltpu.roll(weight, ROWS - step, 0), weight)
        return at, value, weight, jnp.broadcast_to(decay[:1], decay.shape)

    empty = jnp.zeros((ROWS, lanes), jnp.float32)
    grad_last, decay_last, sum_a, sum_i, sum_rate = lax.fori_loop(
        0, tiles // group, recur, (grad_carry[...], decay_carry[...], empty, empty, empty)
    )
    grad_carry[...] = grad_last
    decay_carry[...] = decay_last
    gates_low = gates[...].astype(jnp.bfloat16)
    gate_grad_ref[...] += lax.dot_general(
        conv_ref[0], gates_low, (((0,), (0,)), ((), ())), preferred_element_type=jnp.float32
    )
    from_gates = lax.dot_general(
        gates_low, gate_ref[...], (((1,), (1,)), ((), ())), preferred_element_type=jnp.float32
    )
    conv_grad[rows:, :] = conv_grad[:ROWS, :]
    conv_grad[:rows, :] = (conv_part[...] + from_gates).astype(jnp.bfloat16).astype(jnp.float32)

    def unconvolve(tile, carried):
        for tile in group_tiles(tile, group):
            carried = unconvolve_tile(tile, carried)
        return carried

    def unconvolve_tile(tile, carried):
        earlier, sum_bias, sum_taps = carried
        at = pl.ds(pl.multiple_of(tile * ROWS, ROWS), ROWS)
        beyond = pl.ds(pl.multiple_of((tile + 1) * ROWS, ROWS), ROWS)
        since, until = segment_reach(
            info_ref, chunk * rows + tile * ROWS, slots, (ROWS, 128), total
        )
        here = lagged[at, :]
        grad = conv_grad[at, :]
        later = conv_grad[beyond, :]
        value = grad * channel_ref[TAP : TAP + 1, :]
        new_taps = [sum_taps[0] + grad * here]
        for lag in range(1, taps):
            ahead = jnp.where(
                place < ROWS - lag, pltpu.roll(grad, ROWS - lag, 0), pltpu.roll(later, ROWS - lag, 0)
            )
            value = value + jnp.where(widen(until > lag, lanes), ahead, 0.0) * (
                channel_ref[TAP + lag : TAP + lag + 1, :]
            )
            moved = jnp.where(
                place < lag, pltpu.roll(earlier, lag, 0), pltpu.roll(here, lag, 0)
            )
            new_taps.append(
                sum_taps[lag] + grad * jnp.where(widen(since >= lag, lanes), moved, 0.0)
            )
        projected[at, :lanes] = value
        return here, sum_bias + grad, tuple(new_taps)

    _, sum_bias, sum_taps = lax.fori_loop(
        0, tiles // group, unconvolve, (lag_edge_ref[0], empty, (empty,) * taps)
    )
    low = projected[...].astype(jnp.bfloat16)

    def project_back(projected_ref):
        channels = projected_ref.shape[2] // 2
        projected_ref[0, :, :channels] = low[:, :channels]
        projected_ref[0, :, channels:] = low[:, lanes : lanes + channels]

    pl.when(is_far == 0)(lambda: project_back(projected_near_ref))
    pl.when(is_far == 1)(lambda: project_back(projected_far_ref))
    for place_in, part in enumerate((*sum_taps, sum_bias, sum_a, sum_i, sum_rate)):
        sums[place_in] += part

    @pl.when(lap == laps - 1)
    def _():
        channel_grad_ref[...] = jnp.sum(sums[...], axis=1)


VMEM_LIMIT = 56 * 1024 * 1024


def run_forward(info, near, far, proj, gate, channels, taps, slots):
    chips, rows, depth = near.shape
    count = 2 * chips
    lanes = gate.shape[0]

    def at_chip(chunk, info_ref):
        return (place_of(chunk, info_ref[0], count)[1], 0, 0)

    def at_place(chunk, info_ref):
        is_far, chip = place_of(chunk, info_ref[0], count)
        return (is_far * chips + chip, 0, 0)

    def at_chunk(chunk, info_ref):
        return (chunk, 0, 0)

    def whole(chunk, info_ref):
        return (0, 0)

    def block(kind):
        return jax.ShapeDtypeStruct((count, rows, lanes), kind)

    wide = pl.BlockSpec((1, rows, depth), at_chip)
    narrow = pl.BlockSpec((1, rows, lanes), at_place)
    return pl.pallas_call(
        partial(mixer_forward, taps, slots),
        grid_spec=pltpu.PrefetchScalarGridSpec(
            num_scalar_prefetch=1,
            grid=(count,),
            in_specs=[
                wide,
                wide,
                pl.BlockSpec(proj.shape, whole),
                pl.BlockSpec(gate.shape, whole),
                pl.BlockSpec(channels.shape, whole),
            ],
            out_specs=[narrow] * 10 + [pl.BlockSpec((1, ROWS, lanes), at_chunk)],
            scratch_shapes=[
                pltpu.VMEM((depth, 2 * lanes), jnp.bfloat16),
                pltpu.VMEM((rows, 2 * lanes), jnp.float32),
                pltpu.VMEM((rows, lanes), jnp.float32),
                pltpu.VMEM((rows, 2 * lanes), jnp.float32),
                pltpu.VMEM((ROWS, lanes), jnp.float32),
                pltpu.VMEM((ROWS, lanes), jnp.float32),
            ],
        ),
        out_shape=[block(jnp.bfloat16)] * 3
        + [block(jnp.float32)] * 7
        + [jax.ShapeDtypeStruct((count, ROWS, lanes), jnp.float32)],
        compiler_params=pltpu.CompilerParams(
            dimension_semantics=("arbitrary",), vmem_limit_bytes=VMEM_LIMIT
        ),
        cost_estimate=pl.CostEstimate(flops=0, bytes_accessed=0, transcendentals=0),
        name="mixer_forward",
    )(info, near, far, proj, gate, channels)


def run_backward(info, near, far, out, gate, channels, saved, proj_columns, taps, slots):
    lagging, conv, *parts, lag_edge = saved
    chips, rows, depth = near.shape
    count = 2 * chips
    lanes = gate.shape[0]

    def at_chip(lap, info_ref):
        return (place_of(count - 1 - lap, info_ref[0], count)[1], 0, 0)

    def at_place(lap, info_ref):
        is_far, chip = place_of(count - 1 - lap, info_ref[0], count)
        return (is_far * chips + chip, 0, 0)

    def before(lap, info_ref):
        return (jnp.maximum(count - 2 - lap, 0), 0, 0)

    def whole(lap, info_ref):
        return (0, 0)

    wide = pl.BlockSpec((1, rows, depth), at_chip)
    narrow = pl.BlockSpec((1, rows, lanes), at_place)
    rim = pl.BlockSpec((1, ROWS, lanes), before)
    sums = taps + 4
    return pl.pallas_call(
        partial(mixer_backward, taps, slots),
        grid_spec=pltpu.PrefetchScalarGridSpec(
            num_scalar_prefetch=1,
            grid=(count,),
            in_specs=[
                wide,
                wide,
                pl.BlockSpec(out.shape, whole),
                pl.BlockSpec(gate.shape, whole),
                pl.BlockSpec(channels.shape, whole),
            ]
            + [narrow] * 9
            + [rim],
            out_specs=[
                pl.BlockSpec((1, rows, proj_columns), at_chip),
                pl.BlockSpec((1, rows, proj_columns), at_chip),
                pl.BlockSpec((lanes, 2 * lanes), whole),
                pl.BlockSpec((sums, lanes), whole),
            ],
            scratch_shapes=[
                pltpu.VMEM((rows, lanes), jnp.float32),
                pltpu.VMEM((rows, lanes), jnp.float32),
                pltpu.VMEM((rows, lanes), jnp.float32),
                pltpu.VMEM((rows, 2 * lanes), jnp.float32),
                pltpu.VMEM((rows, 2 * lanes), jnp.float32),
                pltpu.VMEM((rows + ROWS, lanes), jnp.float32),
                pltpu.VMEM((ROWS, lanes), jnp.float32),
                pltpu.VMEM((ROWS, lanes), jnp.float32),
                pltpu.VMEM((sums, ROWS, lanes), jnp.float32),
            ],
        ),
        out_shape=[
            jax.ShapeDtypeStruct((chips, rows, proj_columns), jnp.bfloat16),
            jax.ShapeDtypeStruct((chips, rows, proj_columns), jnp.bfloat16),
            jax.ShapeDtypeStruct((lanes, 2 * lanes), jnp.float32),
            jax.ShapeDtypeStruct((sums, lanes), jnp.float32),
        ],
        compiler_params=pltpu.CompilerParams(
            dimension_semantics=("arbitrary",), vmem_limit_bytes=VMEM_LIMIT
        ),
        cost_estimate=pl.CostEstimate(flops=0, bytes_accessed=0, transcendentals=0),
        name="mixer_backward",
    )(info, near, far, out, gate, channels, *parts, conv, lagging, lag_edge)


def proj_backward(part_ref, proj_ref, signal_ref, normed_ref):
    normed_ref[...] = lax.dot_general(
        part_ref[...], proj_ref[...], (((1,), (1,)), ((), ())), preferred_element_type=jnp.float32
    ).astype(jnp.bfloat16)


def run_proj_backward(part, proj, signal):
    rows, columns = part.shape
    steps = max(count for count in (3, 2, 1) if rows % (16 * count) == 0)
    return pl.pallas_call(
        proj_backward,
        grid=(steps,),
        in_specs=[
            pl.BlockSpec((rows // steps, columns), lambda step: (step, 0)),
            pl.BlockSpec(proj.shape, lambda step: (0, 0)),
            pl.BlockSpec(memory_space=pl.ANY),
        ],
        out_specs=pl.BlockSpec((rows // steps, proj.shape[0]), lambda step: (step, 0)),
        out_shape=jax.ShapeDtypeStruct((rows, proj.shape[0]), jnp.bfloat16),
        compiler_params=pltpu.CompilerParams(vmem_limit_bytes=VMEM_LIMIT),
        cost_estimate=pl.CostEstimate(
            flops=0, bytes_accessed=0, transcendentals=0
        ),
        name="proj_backward",
    )(part, proj, signal)


def deal_columns(moves, whole_ref, groups_ref):
    for group, inside, column, width in moves:
        groups_ref[group, :, inside : inside + width] = whole_ref[:, column : column + width]


def collect_columns(moves, groups_ref, weight_ref, whole_ref, lean_ref):
    for group, inside, column, width in moves:
        whole_ref[:, column : column + width] = groups_ref[
            group, :, inside : inside + width
        ].astype(jnp.float32)
    lean = jnp.zeros((weight_ref.shape[0], 128), jnp.float32)
    for column in range(0, weight_ref.shape[1], 128):
        span = slice(column, column + 128)
        lean = lean + whole_ref[:, span] * weight_ref[:, span].astype(jnp.float32)
    lean_ref[...] = jnp.sum(lean, axis=1, keepdims=True)


def hand_out(weight, moves):
    count = lax.axis_size("seq")
    rows, columns = weight.shape
    groups = pl.pallas_call(
        partial(deal_columns, moves),
        out_shape=jax.ShapeDtypeStruct((count, rows, columns // count), weight.dtype),
        compiler_params=pltpu.CompilerParams(vmem_limit_bytes=VMEM_LIMIT),
        name="deal_columns",
    )(weight)
    dealt = lax.all_to_all(groups, "seq", split_axis=0, concat_axis=0, tiled=True)
    return dealt.reshape(-1, columns // count)


def sum_planes(grad):
    return lax.psum_scatter(
        grad.astype(jnp.bfloat16), "bucket", scatter_dimension=0, tiled=True
    )


def spread_rows(summed):
    count = lax.axis_size("seq")
    blocks = summed.reshape(count, -1, summed.shape[1])
    return lax.all_to_all(blocks, "seq", split_axis=0, concat_axis=0, tiled=True)


def hand_back(blocks, weight, gain, moves):
    rows, columns = weight.shape
    whole, lean = pl.pallas_call(
        partial(collect_columns, moves),
        out_shape=[
            jax.ShapeDtypeStruct((rows, columns), jnp.float32),
            jax.ShapeDtypeStruct((rows, 1), jnp.float32),
        ],
        compiler_params=pltpu.CompilerParams(vmem_limit_bytes=VMEM_LIMIT),
        name="collect_columns",
    )(blocks, weight)
    return whole, lean[:, 0] / gain.astype(jnp.float32)


FOLD = 512


def row_spans(rows):
    parts = max(count for count in (4, 3, 2, 1) if rows % (16 * count) == 0)
    return [slice(part * rows // parts, (part + 1) * rows // parts) for part in range(parts)]


def feed_forward(near_ref, far_ref, wide_ref, feed_grad_ref, feed_ref, grad_ref, normed_ref):
    half = FOLD // 2

    def expand(part_ref):
        for span in row_spans(part_ref.shape[0]):
            product = jnp.dot(
                part_ref[span, :], wide_ref[...], preferred_element_type=jnp.float32
            )
            activated, slope = gelu_parts(product[:, :half])
            up = product[:, half:]
            feed_ref[span, :] = (activated * up).astype(jnp.bfloat16)
            feed_grad = feed_grad_ref[span, :]
            grad_ref[span, :half] = (feed_grad * up * slope).astype(jnp.bfloat16)
            grad_ref[span, half:] = (feed_grad * activated).astype(jnp.bfloat16)

        @pl.when(pl.program_id(1) == 0)
        def _():
            normed_ref[...] = part_ref[...]

    pl.when(pl.program_id(0) == 0)(lambda: expand(near_ref))
    pl.when(pl.program_id(0) == 1)(lambda: expand(far_ref))


def run_feed_forward(near, far, wide, feed_grad):
    rows, depth = near.shape
    tiles = wide.shape[1] // FOLD
    half = FOLD // 2

    def whole(part, tile):
        return (0, 0)

    return pl.pallas_call(
        feed_forward,
        grid=(2, tiles),
        in_specs=[
            pl.BlockSpec((rows, depth), whole),
            pl.BlockSpec((rows, depth), whole),
            pl.BlockSpec((depth, FOLD), lambda part, tile: (0, tile)),
            pl.BlockSpec((rows, half), lambda part, tile: (part, tile)),
        ],
        out_specs=[
            pl.BlockSpec((rows, half), lambda part, tile: (part, tile)),
            pl.BlockSpec((rows, FOLD), lambda part, tile: (part, tile)),
            pl.BlockSpec((rows, depth), lambda part, tile: (part, 0)),
        ],
        out_shape=[
            jax.ShapeDtypeStruct((2 * rows, tiles * half), jnp.bfloat16),
            jax.ShapeDtypeStruct((2 * rows, tiles * FOLD), jnp.bfloat16),
            jax.ShapeDtypeStruct((2 * rows, depth), jnp.bfloat16),
        ],
        compiler_params=pltpu.CompilerParams(vmem_limit_bytes=VMEM_LIMIT),
        cost_estimate=pl.CostEstimate(
            flops=4 * rows * depth * tiles * FOLD, bytes_accessed=0, transcendentals=0
        ),
        name="feed_forward",
    )(near, far, wide, feed_grad)


def feed_backward(upstream_ref, planes_ref, feed_grad_ref, narrow_ref):
    planes = planes_ref.shape[0]
    tile_rows = FOLD // 2 // planes
    tiles = planes_ref.shape[1] // tile_rows

    @pl.when(pl.program_id(0) == 0)
    def _():
        for tile in range(tiles):
            for plane in range(planes):
                target = (tile * planes + plane) * tile_rows
                narrow_ref[target : target + tile_rows, :] = planes_ref[
                    plane, tile * tile_rows : (tile + 1) * tile_rows, :
                ]

    feed_grad_ref[...] = lax.dot_general(
        upstream_ref[...],
        narrow_ref[...],
        (((1,), (1,)), ((), ())),
        preferred_element_type=jnp.float32,
    )


def run_feed_backward(upstream, narrow):
    rows, depth = upstream.shape
    planes, narrow_rows = narrow.shape[:2]
    width = planes * narrow_rows
    steps = max(count for count in range(1, 7) if rows % (16 * count) == 0)
    block = rows // steps

    def at_step(step):
        return (step, 0)

    return pl.pallas_call(
        feed_backward,
        grid=(steps,),
        in_specs=[
            pl.BlockSpec((block, depth), at_step),
            pl.BlockSpec((planes, narrow_rows, depth), lambda step: (0, 0, 0)),
        ],
        out_specs=[
            pl.BlockSpec((block, width), at_step),
            pl.BlockSpec((width, depth), lambda step: (0, 0)),
        ],
        out_shape=[
            jax.ShapeDtypeStruct((rows, width), jnp.float32),
            jax.ShapeDtypeStruct((width, depth), jnp.bfloat16),
        ],
        compiler_params=pltpu.CompilerParams(vmem_limit_bytes=VMEM_LIMIT),
        cost_estimate=pl.CostEstimate(
            flops=2 * rows * depth * width, bytes_accessed=0, transcendentals=0
        ),
        name="feed_backward",
    )(upstream, narrow)


def pad_lanes(values, lanes):
    return jnp.pad(values, [(0, 0)] * (values.ndim - 1) + [(0, lanes - values.shape[-1])])


def contract_halves(left_near, left_far, right_near, right_far, kind=jnp.bfloat16):
    parts = [
        contract_first(left.reshape(-1, left.shape[-1]), right.reshape(-1, right.shape[-1]))
        for left, right in ((left_near, right_near), (left_far, right_far))
    ]
    return (parts[0] + parts[1]).astype(kind)


def by_channels(
    tokens,
    lengths,
    norm_gain,
    in_proj,
    conv_weight,
    conv_bias,
    gate_weight,
    gate_bias,
    decay,
    out_proj,
    mlp_gain,
    gate_up,
    down_proj,
    cotangent,
):
    planes = lax.axis_size("bucket")
    count = lax.axis_size("seq")
    me = lax.axis_index("seq")
    odd = jnp.bitwise_and(me, 1)
    inputs = tokens[0].astype(jnp.float32)
    rows, depth = inputs.shape
    own_rows = in_proj.shape[0]
    width = in_proj.shape[1] // 2
    block_width = width // NB
    held = planes // 2
    channels = held * block_width
    lanes = -(-channels // 128) * 128
    chunk_rows = conv_weight.shape[0]
    hidden_width = gate_up.shape[1] // 2 // count
    hidden_rows = down_proj.shape[0]
    taps = conv_weight.shape[1]
    slots = lengths.shape[1]

    by_row = jnp.concatenate(
        [out_proj, gate_weight, conv_weight, conv_bias[:, None], gate_bias, decay[:, None]], axis=1
    )
    by_row_width = by_row.shape[1]
    gains = jnp.pad(
        jnp.stack([norm_gain, mlp_gain], axis=1), [(0, chunk_rows - own_rows), (0, 0)]
    )
    by_row = jnp.concatenate([by_row, gains], axis=1)
    by_row = pad_lanes(by_row, -(-(by_row_width + 2) // 128) * 128)
    by_row, in_proj = lax.optimization_barrier((by_row, in_proj))
    by_row = lax.all_gather(by_row, "bucket", axis=0, tiled=False)
    proj_moves = [
        (
            2 * pair + side,
            (half * held + index) * block_width,
            half * width + ((side * held + index) * (count // 2) + pair) * block_width,
            block_width,
        )
        for pair in range(count // 2)
        for side in range(2)
        for half in range(2)
        for index in range(held)
    ]
    tile_rows = FOLD // 2 // planes
    tiles = hidden_rows // tile_rows
    wide_moves = [
        (
            member,
            ((tile * 2 + half) * planes + plane) * tile_rows,
            ((half * planes + plane) * count + member) * hidden_rows + tile * tile_rows,
            tile_rows,
        )
        for member in range(count)
        for tile in range(tiles)
        for half in range(2)
        for plane in range(planes)
    ]
    tokens_near, by_row = gather_chips(tokens[0], by_row)
    tokens_far = swap_with(tokens_near, CORE)
    proj_dealt = hand_out(in_proj, proj_moves)
    gains = by_row[:, :own_rows, by_row_width : by_row_width + 2]
    gains = lax.all_gather(gains.transpose(2, 0, 1), "seq", axis=2).astype(jnp.float32)
    gain_one, gain_two = gains.reshape(2, 1, depth)
    gate_up_late, proj_dealt = lax.optimization_barrier((gate_up, proj_dealt))
    wide_dealt = hand_out(gate_up_late, wide_moves)
    proj = lax.all_gather(proj_dealt, "bucket", axis=0, tiled=True)

    ends = jnp.cumsum(lengths[0]).astype(jnp.int32)
    info = jnp.concatenate([me[None].astype(jnp.int32), ends])

    positions = me * rows + jnp.arange(rows, dtype=jnp.int32)
    keep = (positions < ends[-1]).astype(jnp.float32)[:, None]
    upstream = keep * cotangent[0].astype(jnp.float32)
    scale_one = lax.rsqrt(jnp.mean(inputs * inputs, axis=1, keepdims=True) + norm_eps)
    kept = lax.dynamic_slice_in_dim(by_row, odd * held, held, 0)
    given = lax.dynamic_slice_in_dim(by_row, (1 - odd) * held, held, 0)
    taken = swap_with(given, 1)
    pair = jnp.where(
        odd == 0, jnp.stack([kept, taken], axis=1), jnp.stack([taken, kept], axis=1)
    )
    by_channel = pair.reshape(channels, -1)
    out = jnp.pad(by_channel[:, :depth], [(0, lanes - channels), (0, 0)])
    gate_columns = 2 * block_width
    gate_rows = by_channel[:, depth : depth + gate_columns]
    gate_blocks = []
    for index in range(held):
        part = gate_rows[index * block_width : (index + 1) * block_width]
        at = index * block_width
        gate_blocks.append(
            jnp.concatenate(
                [
                    jnp.pad(side, [(0, 0), (at, lanes - at - block_width)])
                    for side in (part[:, :block_width], part[:, block_width:])
                ],
                axis=1,
            )
        )
    gate = jnp.pad(jnp.concatenate(gate_blocks, axis=0), [(0, lanes - channels), (0, 0)])
    small = by_channel[:, depth + gate_columns : by_row_width].astype(jnp.float32).T
    decay_channel = small[taps + 3]
    rate = jnp.pad(jax.nn.softplus(decay_channel), (0, lanes - channels), constant_values=0.01)
    channel = jnp.concatenate([pad_lanes(small[: taps + 3], lanes), rate[None]], axis=0)

    def normalize(low):
        values = low.astype(jnp.float32)
        scale = lax.rsqrt(jnp.mean(values * values, axis=2, keepdims=True) + norm_eps)
        return (values * scale * gain_one).astype(jnp.bfloat16)

    wide_dealt, down_proj, gain_one = lax.optimization_barrier((wide_dealt, down_proj, gain_one))
    normed_near, normed_far = normalize(tokens_near), normalize(tokens_far)
    upstream_low, normed_near, normed_far = lax.optimization_barrier(
        (upstream.astype(jnp.bfloat16), normed_near, normed_far)
    )
    upstream_parts = send_to_chips(upstream_low, upstream_low, upstream_low)
    narrow = lax.all_gather(down_proj, "bucket", axis=0)
    wide = lax.all_gather(wide_dealt, "bucket", axis=0, tiled=True)
    gated, *saved = run_forward(
        info, normed_near, normed_far, proj, gate, channel, taps, slots
    )
    gated, *upstream_parts = lax.optimization_barrier((gated, *upstream_parts))
    upstream_near = jnp.stack([upstream_low, *upstream_parts])
    upstream_far = swap_with(upstream_near, CORE)
    gated_near, upstream_near = lax.optimization_barrier((gated[: count // 2], upstream_near))
    mixed_far, mixed_near = (
        jnp.dot(part.reshape(-1, lanes), out, preferred_element_type=jnp.float32)
        .astype(jnp.bfloat16)
        .reshape(-1, rows, depth)
        for part in (gated[count // 2 :], gated_near)
    )
    mixed, narrow = reduce_plane(mixed_near, mixed_far, late=(narrow,))
    residual = inputs + mixed
    scale_two = lax.rsqrt(jnp.mean(residual * residual, axis=1, keepdims=True) + norm_eps)
    normed_two = (residual * scale_two * gain_two).astype(jnp.bfloat16)
    two_near = gather_chips(normed_two)
    two_far = swap_with(two_near, CORE)
    upstream_all = jnp.concatenate([upstream_near, upstream_far]).reshape(-1, depth)
    feed_grad, narrow = run_feed_backward(upstream_all, narrow)
    feed, expanded_grad, two_all = run_feed_forward(
        two_near.reshape(-1, depth), two_far.reshape(-1, depth), wide, feed_grad
    )
    half_rows = two_all.shape[0] // 2

    down_part = contract_first(feed, upstream_all).astype(jnp.bfloat16)
    down_part = (
        down_part.reshape(tiles, planes, tile_rows, depth)
        .transpose(1, 0, 2, 3)
        .reshape(hidden_width, depth)
    )
    down_grad = sum_planes(down_part).astype(jnp.float32)
    part_far = contract_last(expanded_grad[half_rows:], wide).astype(jnp.bfloat16)
    part_near = contract_last(expanded_grad[:half_rows], wide).astype(jnp.bfloat16)
    normed_two_grad, two_all, feed = reduce_plane(
        part_near.reshape(-1, rows, depth), part_far.reshape(-1, rows, depth), two_all, feed
    )
    def norm_back(values, scale, gain, grad):
        scaled = grad * gain
        lean = jnp.mean(scaled * values, axis=1, keepdims=True)
        return scale * scaled - scale * scale * scale * lean * values

    residual_grad = upstream + norm_back(residual, scale_two, gain_two, normed_two_grad)
    wide_part = contract_first(two_all, expanded_grad).astype(jnp.bfloat16)
    residual_grad, wide_part, down_part = lax.optimization_barrier(
        (residual_grad, wide_part, down_part)
    )
    wide_summed = sum_planes(wide_part)
    output_far, output_near = (
        jnp.dot(part, narrow, preferred_element_type=jnp.float32)
        .astype(jnp.bfloat16)
        .reshape(-1, rows, depth)
        for part in (feed[half_rows:], feed[:half_rows])
    )
    low_near, output_near, output_far, down_grad = gather_chips(
        residual_grad.astype(jnp.bfloat16), output_near, output_far, down_grad
    )
    output_other = swap_with(output_far, CORE)
    output_sums = [
        output_near[place].astype(jnp.float32) + output_other[place].astype(jnp.float32)
        for place in range(4)
    ]
    low_far = swap_with(low_near, CORE)
    low_far, *output_low = lax.optimization_barrier(
        (low_far, *(output_sums[place].astype(jnp.bfloat16) for place in (1, 2, 3)))
    )
    output_parts = send_to_chips(*output_low)
    proj_grad_near, proj_grad_far, gate_grad, channel_grad = run_backward(
        info, low_near, low_far, out, gate, channel, saved, 2 * channels, taps, slots
    )

    def through_proj(part):
        part = run_proj_backward(part.reshape(-1, 2 * channels), proj, signal)
        return part.reshape(-1, rows, depth)

    proj_part = contract_halves(normed_near, normed_far, proj_grad_near, proj_grad_far)
    proj_grad_far, proj_grad_near, proj_part, wide_summed = lax.optimization_barrier(
        (proj_grad_far, proj_grad_near, proj_part, wide_summed)
    )
    signal = swap_with(proj_part[:16, :128], CORE)
    part_far = through_proj(proj_grad_far)
    part_far, *output_parts = lax.optimization_barrier((part_far, *output_parts))
    mixed = residual + output_sums[0]
    for part in output_parts:
        mixed = mixed + part.astype(jnp.float32)
    mixed = (keep * mixed).astype(jnp.bfloat16)
    proj_summed = sum_planes(proj_part)
    part_near = through_proj(proj_grad_near)
    normed_grad, gated, mixed = reduce_plane(part_near, part_far, gated, mixed)

    out_grad = contract_halves(
        gated[: count // 2], gated[count // 2 :], low_near, low_far, jnp.float32
    )[:channels]
    gate_parts = []
    for index in range(held):
        at = index * block_width
        span = gate_grad[at : at + block_width]
        gate_parts.append(
            jnp.concatenate(
                [span[:, at : at + block_width], span[:, lanes + at : lanes + at + block_width]],
                axis=1,
            )
        )
    channel_grad = channel_grad[:, :channels]
    small_grad = jnp.concatenate(
        [
            channel_grad[: taps + 3],
            (channel_grad[taps + 3] * jax.nn.sigmoid(decay_channel))[None],
        ],
        axis=0,
    )
    by_row_grad = jnp.concatenate(
        [out_grad, jnp.concatenate(gate_parts, axis=0), small_grad.T], axis=1
    ).astype(jnp.bfloat16)
    by_row_grad = pad_lanes(by_row_grad, by_row.shape[2]).reshape(held, 2, chunk_rows, -1)
    kept = lax.dynamic_index_in_dim(by_row_grad, odd, 1, False)
    taken = swap_with(lax.dynamic_index_in_dim(by_row_grad, 1 - odd, 1, False), 1)
    by_row_grad = jnp.where(
        odd == 0, jnp.concatenate([kept, taken]), jnp.concatenate([taken, kept])
    ).reshape(planes * chunk_rows, -1)
    by_row_grad = sum_planes(by_row_grad)
    gate_up_grad, mlp_gain_grad = hand_back(spread_rows(wide_summed), gate_up, mlp_gain, wide_moves)
    token_grad = residual_grad + norm_back(inputs, scale_one, gain_one, normed_grad)
    token_grad, proj_blocks = lax.optimization_barrier((token_grad, spread_rows(proj_summed)))
    in_proj_grad, norm_gain_grad = hand_back(proj_blocks, in_proj, norm_gain, proj_moves)
    by_row_grad = by_row_grad.astype(jnp.float32)
    out_proj_grad, gate_weight_grad, *small_grads = pl.pallas_call(
        split_mixer_rows,
        out_shape=[
            jax.ShapeDtypeStruct((chunk_rows, columns), jnp.float32)
            for columns in (depth, gate_columns)
        ]
        + [jax.ShapeDtypeStruct((count_of, chunk_rows), jnp.float32) for count_of in (taps, 1, 2, 1)],
        name="split_mixer_rows",
    )(by_row_grad)
    conv_weight_grad, conv_bias_grad, gate_bias_grad, decay_grad = small_grads
    return (
        mixed[None],
        token_grad[None],
        norm_gain_grad,
        in_proj_grad,
        conv_weight_grad.T,
        conv_bias_grad[0],
        gate_weight_grad,
        gate_bias_grad.T,
        decay_grad[0],
        out_proj_grad,
        mlp_gain_grad,
        gate_up_grad,
        down_grad,
    )


def solution(mesh):
    planes, count = mesh.shape["bucket"], mesh.shape["seq"]
    whole_blocks = count == 8 and planes % 2 == 0 and planes * count == 2 * NB
    return jax.shard_map(
        by_channels if whole_blocks else on_device,
        mesh=mesh,
        in_specs=(
            P("bucket", "seq", None),
            P("bucket", None),
            P(("bucket", "seq")),
            P(("bucket", "seq"), None),
            P(("bucket", "seq"), None),
            P(("bucket", "seq")),
            P(("bucket", "seq"), None),
            P(("bucket", "seq"), None),
            P(("bucket", "seq")),
            P(("bucket", "seq"), None),
            P(("bucket", "seq")),
            P(("bucket", "seq"), None),
            P(("bucket", "seq"), None),
            P("bucket", "seq", None),
        ),
        out_specs=(
            P("bucket", "seq", None),
            P("bucket", "seq", None),
            P(("bucket", "seq")),
            P(("bucket", "seq"), None),
            P(("bucket", "seq"), None),
            P(("bucket", "seq")),
            P(("bucket", "seq"), None),
            P(("bucket", "seq"), None),
            P(("bucket", "seq")),
            P(("bucket", "seq"), None),
            P(("bucket", "seq")),
            P(("bucket", "seq"), None),
            P(("bucket", "seq"), None),
        ),
        check_vma=False,
    )
```
